32 devices in a mesh: ctx: 4 (over y, x), exp: 4 (over z), dp: 2 (over core).
Axes of the slice: x: 2, y: 2, z: 4, core: 2. Of those that a mesh axis runs over, the one named last changes fastest.
Arguments:
- queries: bfloat16 [8, 768, 2048], P(('dp', 'exp'), 'ctx'), parts along dimension 0, may hold values from -38 to 38
- keys: bfloat16 [8, 768, 256], P(('dp', 'exp'), 'ctx'), parts along dimension 0, may hold values from -4 to 4
- values: bfloat16 [8, 768, 256], P(('dp', 'exp'), 'ctx'), parts along dimension 0, may hold values from -6 to 6
- segments: int32 [8, 768], P(('dp', 'exp')), parts along dimension 0, may hold values from 0 to 7, never falling along the last dimension, each value on 1 to 384 neighbouring positions
- residual: bfloat16 [8, 768, 1024], P(('dp', 'exp'), 'ctx'), parts along dimension 0, may hold values from -3 to 3
- out_weight: bfloat16 [2048, 1024], P('ctx'), may hold values from -0.125 to 0.125
- gain: float32 [1024], replicated, may hold values from 0.1 to 1.9
- expert_ids: int32 [8, 768, 8], P(('dp', 'exp'), 'ctx'), parts along dimension 0, may hold values from 0 to 127, all different within a row; in each aligned block of 192 rows (0 to 191, 192 to 383, ..., all dimensions but the last counted through in order) at most 24 rows name the same one
- route_weights: float32 [8, 768, 8], P(('dp', 'exp'), 'ctx'), parts along dimension 0, may hold values from 0.05 to 0.5
- w_gate: bfloat16 [4, 1024, 384], P('exp'), may hold values from -0.1875 to 0.1875
- w_up: bfloat16 [4, 1024, 384], P('exp'), may hold values from -0.1875 to 0.1875
- w_down: bfloat16 [4, 384, 1024], P('exp'), may hold values from -0.3125 to 0.3125
Outputs:
- layer_out: bfloat16 [8, 768, 1024], P(('dp', 'exp'), 'ctx'), parts along dimension 0
The draws below stay inside these ranges and needn't reach their ends.
There are 2 independent parts, one for each index of `dp`. The reference program is written for one: setup_inputs(seed, part) draws one part's arguments, and reference() takes and returns one part's arrays. A program takes and returns all parts, laid end to end along the dimension named above; an argument that names none is the same for every part. Nothing has to cross between parts.
Inputs may be any that keep to these rules, and one draw needn't show every extreme that they name: `expert_ids`: in every aligned block of 192 positions of a sequence (one slab), no expert is named by more than 24 tokens, and in every draw some expert is named by exactly 24 tokens of some block; a token names 8 different experts. `segments`: document numbers never fall along a sequence.
All inputs are finite; a program needn't handle non-finite values.
Results may differ from the reference program's by a relative error of at most 0.006.
Values may be sent and summed in bfloat16 or wider, within the bound.
No kernel may reach another device: no remote copies, remote signals or barrier semaphores. Data moves between devices by JAX's collectives and lax.ppermute only.
A program may use at most 64 MiB of HBM per device.

```python
import math
import jax
import jax.numpy as jnp
import numpy as np
from jax import lax

D = 1024
HQ = 16
KVH = 2
HD = 128
FFE = 384
EXPERTS = 128
TOP = 8
DOCS = 8
TOK_DEV = 192
SEQ = 768
SEQS = 4
EXPERTS_FL = 4
CAP = 24
N_CTX = 4


def pair_fields(key):
    query_key = jax.random.fold_in(key, 101)
    key_key = jax.random.fold_in(key, 202)
    key_field = jnp.clip(jax.random.normal(key_key, (SEQS, SEQ, KVH, HD), jnp.float32), -4.0, 4.0)
    query_field = jnp.clip(jax.random.normal(query_key, (SEQS, SEQ, HQ * HD), jnp.float32), -4.0, 4.0)
    return (query_field, key_field.reshape(SEQS, SEQ, KVH * HD))


def draw_queries(key, part):
    return pair_fields(key)[0].astype(jnp.bfloat16)


def draw_keys(key, part):
    return pair_fields(key)[1].astype(jnp.bfloat16)


def block_levels(stream_key, extent, split, least, high):
    loudness = 1.0
    for dim, blocks in split:
        steps = jax.random.uniform(jax.random.fold_in(jax.random.fold_in(stream_key, 6), dim), (blocks,), jnp.float32, least / len(split), high / len(split))
        loudness = loudness * jnp.repeat(jnp.exp(steps), extent[dim] // blocks).reshape((-1,) + (1,) * (len(extent) - 1 - dim))
    return loudness


def length_profile(count, total, bound, skew):
    loads = [(1 << 20) // math.isqrt(grade ** skew) + 1 for grade in range(2, count + 1)]
    surplus, given = total - bound - (count - 1), [1] * (count - 1)
    while surplus > 0:
        movable = [i for i in range(count - 1) if given[i] < bound]
        pool, budget = sum([loads[i] for i in movable]), surplus
        for i in movable:
            more = min(bound - given[i], max(1, budget * loads[i] // pool), surplus)
            given[i] = given[i] + more
            surplus = surplus - more
    return np.array([bound] + given)


def ragged_sizes(stream_key, amount, total, limit, skew):
    if amount == 2:
        one = jax.random.randint(stream_key, (), max(1, total - limit), min(limit, total - 1) + 1)
        return jnp.stack([one, total - one])
    sizes = jnp.asarray(length_profile(amount, total, limit, skew), jnp.int32)
    twos = (amount - 1) // 2
    donor, sink = sizes[1:1 + 2 * twos:2], sizes[2:2 + 2 * twos:2]
    slack = jnp.minimum(donor - 1, limit - sink)
    passed = jax.random.randint(jax.random.fold_in(stream_key, 1), (twos,), 0, 1 << 20) % (slack + 1)
    sizes = sizes.at[1:1 + 2 * twos:2].set(donor - passed).at[2:2 + 2 * twos:2].set(sink + passed)
    return sizes[jax.random.permutation(jax.random.fold_in(stream_key, 2), amount)]


def deal_out(rng, own, number, rows, amount, top, reach, skew):
    order = jax.random.permutation(rng, amount)
    packed, usual = shares(amount, rows * top, reach, skew, True), shares(amount, rows * top, reach, skew, False)
    places = jnp.arange(amount)

    def named(tallies, rotation):
        used = int((tallies > 0).sum())
        fixed = max(1, used // 4)
        shifted = fixed + (places - fixed + rotation * (used - fixed)) % max(1, amount - fixed)
        return jnp.zeros((amount,), jnp.int32).at[order[jnp.where(places < fixed, places, shifted)]].set(jnp.asarray(tallies, jnp.int32))

    tallies = jnp.where(number % 4 == 0, named(packed, number // 4), named(usual, number - number // 4 - 1))
    mixed = jax.random.permutation(jax.random.fold_in(own, 3), amount)
    giver, taker = mixed[0:amount // 2 * 2:2], mixed[1:amount // 2 * 2:2]
    margin = jnp.minimum(tallies[giver] - 1, reach - tallies[taker]) // 2
    margin = jnp.where((giver == order[0]) | (taker == order[0]) | (tallies[taker] == 0), 0, jnp.maximum(margin, 0))
    shifted = jax.random.randint(jax.random.fold_in(own, 4), (amount // 2,), 0, 1 << 20) % (margin + 1)
    tallies = tallies.at[giver].add(-shifted).at[taker].add(shifted)
    items = jnp.searchsorted(jnp.cumsum(tallies), jnp.arange(rows * top), side="right").astype(jnp.int32)
    listing = items.reshape(top, rows).T
    listing = listing[jax.random.permutation(jax.random.fold_in(own, 1), rows)]
    rotation = jax.random.randint(jax.random.fold_in(own, 2), (rows, 1), 0, top)
    return jnp.take_along_axis(listing, (jnp.arange(top)[None, :] + rotation) % top, axis=1)


def shares(amount, total, reach, lean, full):
    weights = [(1 << 20) // math.isqrt(grade ** lean) + 1 for grade in range(1, amount + 1)]
    largest = reach if full else min(reach, max(-(-total // amount), total * weights[0] // sum(weights)))
    least = 1 if total - largest >= amount - 1 else 0
    holding, spare = [largest] + [least] * (amount - 1), total - largest - least * (amount - 1)
    while spare > 0:
        free = [i for i in range(1, amount) if holding[i] < largest] or [i for i in range(1, amount) if holding[i] < reach]
        whole, left = sum([weights[i] for i in free]), spare
        for i in free:
            addition = min(reach - holding[i], max(1, left * weights[i] // whole), spare)
            holding[i] = holding[i] + addition
            spare = spare - addition
    return np.array(holding)


def gaussian(own_key, extent, scale, limit, pieces=(), held_as=jnp.bfloat16):
    result = scale * jax.random.normal(own_key, extent, jnp.float32)
    if pieces:
        result = result * block_levels(own_key, extent, pieces, -0.22, 0.18)
    return jnp.clip(result, -limit, limit).astype(held_as)


def setup_inputs(seed: int = 0, part: int = 0) -> dict:
    key_list = jax.random.split(jax.random.key(seed), 13)
    part_keys = jax.random.split(jax.random.fold_in(key_list[12], part), 13)
    queries = draw_queries(jax.random.fold_in(jax.random.fold_in(key_list[12], part), 71), part)
    keys = draw_keys(jax.random.fold_in(jax.random.fold_in(key_list[12], part), 71), part)
    values = gaussian(part_keys[2], (SEQS, SEQ, KVH * HD), 1.0, 6.0, ((0, 4), (1, 4)))
    segments = jax.vmap(lambda own: jnp.searchsorted(jnp.cumsum(ragged_sizes(own, DOCS, SEQ, SEQ // 2, 2)), jnp.arange(SEQ), side="right"))(jax.random.split(part_keys[3], SEQS)).reshape((SEQS, SEQ)).astype(jnp.int32)
    residual = gaussian(part_keys[4], (SEQS, SEQ, D), 0.5, 3.0, ((0, 4), (1, 4)))
    out_weight = gaussian(key_list[5], (HQ * HD, D), (HQ * HD) ** -0.5, 0.125, ((0, 4),))
    gain = jnp.clip(1.0 + 0.18 * jax.random.normal(key_list[6], (D,), jnp.float32), 0.1, 1.9)
    expert_ids_keys = jax.random.split(jax.random.fold_in(part_keys[7], 1), SEQS * SEQ // TOK_DEV)
    expert_ids_turns = jax.random.permutation(jax.random.fold_in(part_keys[7], 3), SEQS * SEQ // TOK_DEV)
    expert_ids = jax.vmap(lambda own, number: deal_out(jax.random.fold_in(part_keys[7], 2), own, number, TOK_DEV, EXPERTS, TOP, CAP, 2))(expert_ids_keys, expert_ids_turns).reshape((SEQS, SEQ, TOP))
    route_weights = jnp.clip(jnp.exp(math.log(0.5) - 2.3025851 * jax.random.uniform(part_keys[8], (SEQS, SEQ, TOP), jnp.float32) ** block_levels(part_keys[8], (SEQS, SEQ, TOP), ((0, 4), (1, 4)), -0.2, 0.2)), 0.05, 0.5)
    w_gate = gaussian(key_list[9], (EXPERTS_FL, D, FFE), D ** -0.5, 0.1875, ((0, 4),))
    w_up = gaussian(key_list[10], (EXPERTS_FL, D, FFE), D ** -0.5, 0.1875, ((0, 4),))
    w_down = gaussian(key_list[11], (EXPERTS_FL, FFE, D), FFE ** -0.5, 0.3125, ((0, 4),))
    return {"queries": queries, "keys": keys, "values": values, "segments": segments, "residual": residual, "out_weight": out_weight, "gain": gain, "expert_ids": expert_ids, "route_weights": route_weights, "w_gate": w_gate, "w_up": w_up, "w_down": w_down}


def attend_sequence(operands):
    query_seq, key_seq, value_seq, seg_seq = operands
    groups = HQ // KVH
    block = math.gcd(SEQ, 256)
    scale_factor = 1.0 / math.sqrt(HD)
    key_f32 = key_seq.astype(jnp.float32).reshape(SEQ, KVH, HD)
    value_f32 = value_seq.astype(jnp.float32).reshape(SEQ, KVH, HD)
    key_pos = jnp.arange(SEQ, dtype=jnp.int32)

    def query_block(index):
        first_row = index * block
        query_f32 = lax.dynamic_slice_in_dim(query_seq, first_row, block, 0).astype(jnp.float32).reshape(block, KVH, groups, HD)
        query_pos = first_row + jnp.arange(block, dtype=jnp.int32)
        query_seg = lax.dynamic_slice_in_dim(seg_seq, first_row, block, 0)
        scores = jnp.einsum('qkgd,skd->qkgs', query_f32, key_f32) * scale_factor
        allowed = ((key_pos[None, :] <= query_pos[:, None]) & (seg_seq[None, :] == query_seg[:, None]))[:, None, None, :]
        row_max = lax.optimization_barrier(jnp.max(jnp.where(allowed, scores, -jnp.inf), axis=-1, keepdims=True))
        expo = jnp.where(allowed, jnp.exp(scores - row_max), 0.0)
        norm_sum = lax.optimization_barrier(jnp.sum(expo, axis=-1))
        probs = lax.optimization_barrier(expo.astype(jnp.bfloat16)).astype(jnp.float32)
        mixed = jnp.einsum('qkgs,skd->qkgd', probs, value_f32) / norm_sum[..., None]
        return mixed.reshape(block, HQ * HD).astype(jnp.bfloat16)
    return lax.map(query_block, jnp.arange(SEQ // block, dtype=jnp.int32)).reshape(SEQ, HQ * HD)

def reference(queries, keys, values, segments, residual, out_weight, gain, expert_ids, route_weights, w_gate, w_up, w_down):
    attended = lax.map(attend_sequence, (queries, keys, values, segments))
    total_tok = SEQS * SEQ
    projected = jnp.dot(attended.reshape(total_tok, HQ * HD), out_weight, preferred_element_type=jnp.float32)
    hidden_state = residual.reshape(total_tok, D).astype(jnp.float32) + projected
    normed = (hidden_state * lax.rsqrt(lax.optimization_barrier(jnp.mean(hidden_state * hidden_state, axis=-1, keepdims=True)) + 1e-06) * gain).astype(jnp.bfloat16)
    flat_ids = expert_ids.reshape(total_tok * TOP)
    flat_weights = jnp.concatenate([route_weights.reshape(total_tok * TOP), jnp.zeros((1,), jnp.float32)])
    normed_pad = jnp.concatenate([normed, jnp.zeros((1, D), jnp.bfloat16)], axis=0)
    most_rows = SEQS * N_CTX * CAP

    def one_expert(running, expert):
        index_list = jnp.nonzero(flat_ids == expert, size=most_rows, fill_value=total_tok * TOP)[0].astype(jnp.int32)
        token_index = index_list // TOP
        chosen_rows = normed_pad[token_index]
        gate_part = jnp.dot(chosen_rows, w_gate[expert], preferred_element_type=jnp.float32)
        up_part = jnp.dot(chosen_rows, w_up[expert], preferred_element_type=jnp.float32)
        expert_hidden = (jax.nn.silu(gate_part) * up_part).astype(jnp.bfloat16)
        expert_out = jnp.dot(expert_hidden, w_down[expert], preferred_element_type=jnp.float32).astype(jnp.bfloat16)
        running = running.at[token_index].add(flat_weights[index_list][:, None] * expert_out.astype(jnp.float32))
        return (running, None)
    moe_sum, _ = lax.scan(one_expert, jnp.zeros((total_tok + 1, D), jnp.float32), jnp.arange(EXPERTS_FL, dtype=jnp.int32))
    layer_out = (hidden_state + moe_sum[:total_tok]).astype(jnp.bfloat16)
    return layer_out.reshape(SEQS, SEQ, D)
```

```python
import functools
import math

import jax
import jax.numpy as jnp
from jax import lax
from jax.experimental import pallas as pl
from jax.experimental.pallas import tpu as pltpu
from jax.sharding import PartitionSpec as P

HQ = 16
KVH = 2
HD = 128
GROUPS = HQ // KVH
CAP = 24
NEG = -1e30
SCORE_SCALE = math.log2(math.e) / math.sqrt(HD)
F32 = jnp.float32
BF16 = jnp.bfloat16


def block_mask(segs_ref, me, back, rows):
    row = lax.broadcasted_iota(jnp.int32, (rows, rows), 0)
    col = lax.broadcasted_iota(jnp.int32, (rows, rows), 1)
    own_seg = segs_ref[pl.ds(me, 1), :]
    query_seg = jnp.sum(jnp.where(row == col, own_seg, 0), axis=1, keepdims=True)
    if back == 0:
        return (col <= row) & (own_seg == query_seg)
    key_seg = segs_ref[pl.ds(jnp.maximum(me - back, 0), 1), :]
    return (key_seg == query_seg) & (me >= back)


def head_scores(q_ref, k_ref, head, mask):
    kv = head // GROUPS
    scores = lax.dot_general(
        q_ref[:, head * HD : (head + 1) * HD],
        k_ref[:, kv * HD : (kv + 1) * HD],
        (((1,), (1,)), ((), ())),
        preferred_element_type=F32,
    )
    return jnp.where(mask, scores * SCORE_SCALE, NEG)


def own_kernel(
    q_ref, k_ref, v_ref, segs_ref, ids_ref, rw_ref, acc_ref, max_ref, sum_ref, place_ref, mix_ref
):
    rows = q_ref.shape[0]
    owners = lax.axis_size("exp")
    slots = mix_ref.shape[1]
    mask = block_mask(segs_ref, lax.axis_index("ctx"), 0, rows)
    for head in range(HQ):
        kv = head // GROUPS
        scores = head_scores(q_ref, k_ref, head, mask)
        row_max = jnp.max(scores, axis=1, keepdims=True)
        expo = jnp.exp2(scores - row_max)
        max_ref[:, head : head + 1] = row_max
        sum_ref[:, head : head + 1] = jnp.sum(expo, axis=1, keepdims=True)
        acc_ref[:, head * HD : (head + 1) * HD] = jnp.dot(
            expo.astype(BF16), v_ref[:, kv * HD : (kv + 1) * HD], preferred_element_type=F32
        )
    lane = lax.broadcasted_iota(jnp.int32, (rows, slots), 1)
    owner = lax.rem(lane // CAP + lax.axis_index("exp"), owners)
    hit = jnp.zeros((rows, slots), jnp.bool_)
    weight = jnp.zeros((rows, slots), F32)
    for choice in range(ids_ref.shape[1]):
        same = ids_ref[:, choice : choice + 1] == owner
        hit = hit | same
        weight = jnp.where(same, rw_ref[:, choice : choice + 1], weight)
    row = lax.broadcasted_iota(jnp.int32, (rows, rows), 0)
    col = lax.broadcasted_iota(jnp.int32, (rows, rows), 1)
    before = (col < row).astype(F32).astype(BF16)
    rank = jnp.dot(before, hit.astype(F32).astype(BF16), preferred_element_type=F32)
    placed = hit & (rank == lax.rem(lane, CAP).astype(F32))
    place_ref[...] = placed.astype(F32).astype(BF16)
    mix_ref[...] = jnp.where(placed, weight, 0.0)


def rest_kernel(back_count, q_ref, segs_ref, acc_ref, max_ref, sum_ref, *refs):
    key_refs, value_refs = refs[:back_count], refs[back_count : 2 * back_count]
    out_ref = refs[2 * back_count]
    rows = q_ref.shape[0]
    me = lax.axis_index("ctx")
    masks = [block_mask(segs_ref, me, back + 1, rows) for back in range(back_count)]
    for head in range(HQ):
        kv = head // GROUPS
        old_max = max_ref[:, head : head + 1]
        scores = [head_scores(q_ref, key_refs[b], head, masks[b]) for b in range(back_count)]
        new_max = old_max
        for part in scores:
            new_max = jnp.maximum(new_max, jnp.max(part, axis=1, keepdims=True))
        fix = jnp.exp2(old_max - new_max)
        total = sum_ref[:, head : head + 1] * fix
        accum = acc_ref[:, head * HD : (head + 1) * HD] * fix
        for b, part in enumerate(scores):
            expo = jnp.exp2(part - new_max)
            total = total + jnp.sum(expo, axis=1, keepdims=True)
            accum = accum + jnp.dot(
                expo.astype(BF16),
                value_refs[b][:, kv * HD : (kv + 1) * HD],
                preferred_element_type=F32,
            )
        out_ref[:, head * HD : (head + 1) * HD] = (accum / total).astype(BF16)


def project_kernel(pieces, n_ctx, att_ref, res_ref, gain_ref, place_ref, own_w_ref, *refs):
    piece_refs = refs[: len(pieces)]
    owners = lax.axis_size("exp")
    hidden_ref = refs[len(pieces)]
    send_refs = refs[len(pieces) + 1 : len(pieces) + 1 + owners]
    w_buf, sems = refs[len(pieces) + 1 + owners :]
    me, core = lax.axis_index("ctx"), lax.axis_index("dp")
    share = own_w_ref.shape[0]
    copies = {}
    start = pl.multiple_of(me * share, share)
    copies[0] = [pltpu.make_async_copy(own_w_ref, w_buf.at[pl.ds(start, share)], sems.at[0])]
    copies[0][0].start()
    for number, (flip, other, offset) in enumerate(pieces):
        ref = piece_refs[number]
        size = ref.shape[0]
        cores = lax.axis_size("dp")
        lead = lax.rem(core + other, cores) * (share // cores)
        start = pl.multiple_of((me ^ flip) * share + lead + offset, size)
        copy = pltpu.make_async_copy(ref, w_buf.at[pl.ds(start, size)], sems.at[number + 1])
        copy.start()
        copies.setdefault(flip, []).append(copy)
    hidden = res_ref[...].astype(F32)
    for flip in range(n_ctx):
        for copy in copies[flip]:
            copy.wait()
        start = pl.multiple_of((me ^ flip) * share, share)
        hidden = hidden + jnp.dot(
            att_ref[:, pl.ds(start, share)],
            w_buf[pl.ds(start, share), :],
            preferred_element_type=F32,
        )
    hidden_ref[...] = hidden
    mean = jnp.mean(hidden * hidden, axis=1, keepdims=True)
    normed = (hidden * lax.rsqrt(mean + 1e-06) * gain_ref[...]).astype(BF16)
    rows = lax.dot_general(
        place_ref[...], normed, (((0,), (0,)), ((), ())), preferred_element_type=F32
    )
    for step in range(owners):
        send_refs[step][...] = rows[step * CAP : (step + 1) * CAP, :].astype(BF16)


def stack(refs):
    return jnp.concatenate([ref[...].astype(F32) for ref in refs], axis=0).astype(BF16)


def expert_kernel(owners, *refs):
    row_refs = refs[:owners]
    gate_ref, up_ref, down_ref = refs[owners : owners + 3]
    out_refs = refs[owners + 3 :]
    rows = stack(row_refs)
    gate = jnp.dot(rows, gate_ref[...], preferred_element_type=F32)
    up = jnp.dot(rows, up_ref[...], preferred_element_type=F32)
    hidden = (gate / (1.0 + jnp.exp(-gate)) * up).astype(BF16)
    out = jnp.dot(hidden, down_ref[...], preferred_element_type=F32)
    for step in range(owners):
        out_refs[step][...] = out[step * CAP : (step + 1) * CAP, :].astype(BF16)


def combine_kernel(owners, hidden_ref, mix_ref, *refs):
    row_refs, out_ref = refs[:owners], refs[owners]
    rows = stack(row_refs)
    mix = mix_ref[...]
    high = mix.astype(BF16)
    low = (mix - high.astype(F32)).astype(BF16)
    total = hidden_ref[...]
    total = total + jnp.dot(high, rows, preferred_element_type=F32)
    total = total + jnp.dot(low, rows, preferred_element_type=F32)
    out_ref[...] = total.astype(BF16)


def call(kernel, outs, args, specs=None, scratch=(), limit=24, flops=1_000_000):
    vmem = pl.BlockSpec(memory_space=pltpu.VMEM)
    nbytes = sum(math.prod(a.shape) * a.dtype.itemsize for a in list(args) + list(outs))
    return pl.pallas_call(
        kernel,
        out_shape=outs,
        in_specs=specs or [vmem] * len(args),
        out_specs=[vmem] * len(outs),
        scratch_shapes=list(scratch),
        compiler_params=pltpu.CompilerParams(vmem_limit_bytes=limit << 20),
        cost_estimate=pl.CostEstimate(flops=flops, bytes_accessed=nbytes, transcendentals=0),
    )(*args)


def gather_weight(weight):
    n_ctx, cores = lax.axis_size("ctx"), lax.axis_size("dp")
    core = lax.axis_index("dp")
    share = weight.shape[0]
    half = share // cores // 2
    bits = [1 << b for b in range(n_ctx.bit_length() - 1)]
    found = {}
    first = core * (share // cores)
    for part, order in enumerate((bits, bits[::-1])):
        held = {0: lax.dynamic_slice_in_dim(weight, first + part * half, half, 0)}
        for bit in order:
            pairs = [(i, i ^ bit) for i in range(n_ctx)]
            for flip, piece in list(held.items()):
                held[flip ^ bit] = lax.ppermute(piece, "ctx", pairs)
        for flip, piece in held.items():
            if flip:
                found[flip, 0, part * half] = piece
    for (flip, _, offset), piece in list(found.items()):
        for other in range(1, cores):
            pairs = [((i + other) % cores, i) for i in range(cores)]
            found[flip, other, offset] = lax.ppermute(piece, "dp", pairs)
    return found


def per_device(
    queries,
    keys,
    values,
    segments,
    residual,
    out_weight,
    gain,
    expert_ids,
    route_weights,
    w_gate,
    w_up,
    w_down,
):
    tok_rows = queries.shape[1]
    width = residual.shape[2]
    n_ctx, owners = lax.axis_size("ctx"), lax.axis_size("exp")
    slots = owners * CAP
    longest = segments.shape[1] // 2
    back_count = min(n_ctx - 1, -(-(longest - 1) // tok_rows))

    key_blocks, value_blocks = [], []
    for back in range(1, back_count + 1):
        pairs = [(i, i + back) for i in range(n_ctx - back)]
        key_blocks.append(lax.ppermute(keys[0], "ctx", pairs))
        value_blocks.append(lax.ppermute(values[0], "ctx", pairs))
    pieces = gather_weight(out_weight)

    shape = jax.ShapeDtypeStruct
    segs = segments[0].reshape(n_ctx, tok_rows)
    accum, row_max, row_sum, place, mix = call(
        own_kernel,
        [
            shape((tok_rows, HQ * HD), F32),
            shape((tok_rows, HQ), F32),
            shape((tok_rows, HQ), F32),
            shape((tok_rows, slots), BF16),
            shape((tok_rows, slots), F32),
        ],
        [queries[0], keys[0], values[0], segs, expert_ids[0], route_weights[0]],
        flops=4 * tok_rows * tok_rows * HQ * HD,
    )
    (attended,) = call(
        functools.partial(rest_kernel, back_count),
        [shape((tok_rows, HQ * HD), BF16)],
        [queries[0], segs, accum, row_max, row_sum, *key_blocks, *value_blocks],
        flops=4 * back_count * tok_rows * tok_rows * HQ * HD,
    )
    vmem, anywhere = pl.BlockSpec(memory_space=pltpu.VMEM), pl.BlockSpec(memory_space=pl.ANY)
    hidden, *sends = call(
        functools.partial(project_kernel, list(pieces), n_ctx),
        [shape((tok_rows, width), F32)] + [shape((CAP, width), BF16)] * owners,
        [attended, residual[0], gain[None, :], place, out_weight, *pieces.values()],
        specs=[vmem] * 4 + [anywhere] * (1 + len(pieces)),
        scratch=[
            pltpu.VMEM((n_ctx * out_weight.shape[0], width), BF16),
            pltpu.SemaphoreType.DMA((len(pieces) + 1,)),
        ],
        flops=2 * tok_rows * HQ * HD * width,
    )
    rows = [sends[0]]
    for step in range(1, owners):
        pairs = [(i, (i + step) % owners) for i in range(owners)]
        rows.append(lax.ppermute(sends[step], "exp", pairs))
    done = call(
        functools.partial(expert_kernel, owners),
        [shape((CAP, width), BF16)] * owners,
        [*rows, w_gate[0], w_up[0], w_down[0]],
        flops=6 * slots * width * w_gate.shape[2],
    )
    back = [done[0]]
    for step in range(1, owners):
        pairs = [((i + step) % owners, i) for i in range(owners)]
        back.append(lax.ppermute(done[step], "exp", pairs))
    (out,) = call(
        functools.partial(combine_kernel, owners),
        [shape((tok_rows, width), BF16)],
        [hidden, mix, *back],
        flops=4 * tok_rows * slots * width,
    )
    return out[None]


def solution(mesh):
    return jax.shard_map(
        per_device,
        mesh=mesh,
        in_specs=(
            P(("dp", "exp"), "ctx", None),
            P(("dp", "exp"), "ctx", None),
            P(("dp", "exp"), "ctx", None),
            P(("dp", "exp"), None),
            P(("dp", "exp"), "ctx", None),
            P("ctx", None),
            P(),
            P(("dp", "exp"), "ctx", None),
            P(("dp", "exp"), "ctx", None),
            P("exp", None, None),
            P("exp", None, None),
            P("exp", None, None),
        ),
        out_specs=P(("dp", "exp"), "ctx", None),
        check_vma=False,
    )
```

```python
import functools
import math

import jax
import jax.numpy as jnp
from jax import lax
from jax.experimental import pallas as pl
from jax.experimental.pallas import tpu as pltpu
from jax.sharding import PartitionSpec as P

HQ = 16
KVH = 2
HD = 128
GROUPS = HQ // KVH
CAP = 24
NEG = -1e30
SCORE_SCALE = math.log2(math.e) / math.sqrt(HD)
F32 = jnp.float32
BF16 = jnp.bfloat16


def slab_segments(segs_ref, index, count, rows):
    found = segs_ref[:, 0:rows]
    for slab in range(1, count):
        found = jnp.where(index == slab, segs_ref[:, slab * rows : (slab + 1) * rows], found)
    return found


def score_bias(segs_ref, backs, count, rows):
    me = lax.axis_index("ctx")
    row = lax.broadcasted_iota(jnp.int32, (rows, rows), 0)
    col = lax.broadcasted_iota(jnp.int32, (rows, rows), 1)
    own_seg = slab_segments(segs_ref, me, count, rows)
    query_seg = jnp.sum(jnp.where(row == col, own_seg, 0), axis=1, keepdims=True)
    parts = []
    for back in backs:
        if back == 0:
            allowed = (col <= row) & (own_seg == query_seg)
        else:
            key_seg = slab_segments(segs_ref, jnp.maximum(me - back, 0), count, rows)
            allowed = (key_seg == query_seg) & (me >= back)
        parts.append(jnp.where(allowed, 0.0, NEG))
    return parts


def head_scores(q_ref, keys, head, bias):
    scores = lax.dot_general(
        q_ref[:, head * HD : (head + 1) * HD],
        keys,
        (((1,), (1,)), ((), ())),
        preferred_element_type=F32,
    )
    return scores * SCORE_SCALE + bias


def pack_kernel(k_ref, v_ref, kv_ref, sems):
    width = k_ref.shape[1]
    copies = [
        pltpu.make_async_copy(k_ref, kv_ref.at[:, pl.ds(0, width)], sems.at[0]),
        pltpu.make_async_copy(v_ref, kv_ref.at[:, pl.ds(width, width)], sems.at[1]),
    ]
    for copy in copies:
        copy.start()
    for copy in copies:
        copy.wait()


def gate_kernel(piece_ref, mark_ref, out_ref):
    del piece_ref, mark_ref, out_ref


def after(piece, mark):
    spec = pl.BlockSpec(memory_space=pl.ANY)
    return pl.pallas_call(
        gate_kernel,
        out_shape=jax.ShapeDtypeStruct(piece.shape, piece.dtype),
        in_specs=[spec, spec],
        out_specs=spec,
        input_output_aliases={0: 0},
    )(piece, mark)


def own_kernel(
    n_ctx, q_ref, kv_ref, segs_ref, ids_ref, rw_ref, res_ref, acc_ref, max_ref, sum_ref, place_ref, mix_ref, rows_ref
):
    rows = q_ref.shape[0]
    slots = mix_ref.shape[0]
    (bias,) = score_bias(segs_ref, (0,), n_ctx, rows)
    ones = jnp.ones((rows, HD), BF16)
    for kv in range(KVH):
        keys = kv_ref[:, kv * HD : (kv + 1) * HD]
        values = jnp.concatenate([kv_ref[:, (KVH + kv) * HD : (KVH + kv + 1) * HD], ones], axis=1)
        for head in range(kv * GROUPS, (kv + 1) * GROUPS):
            scores = head_scores(q_ref, keys, head, bias)
            row_max = jnp.max(scores, axis=1, keepdims=True)
            expo = jnp.exp2(scores - row_max).astype(BF16)
            mixed = jnp.dot(expo, values, preferred_element_type=F32)
            max_ref[:, head : head + 1] = row_max
            sum_ref[:, head : head + 1] = mixed[:, HD : HD + 1]
            acc_ref[:, head * HD : (head + 1) * HD] = mixed[:, :HD]
    slot = lax.broadcasted_iota(jnp.int32, (slots, rows), 0)
    owner = lax.rem(slot // CAP + lax.axis_index("exp"), slots // CAP)
    hit = jnp.zeros((slots, rows), jnp.bool_)
    weight = jnp.zeros((slots, rows), F32)
    for choice in range(ids_ref.shape[0]):
        same = ids_ref[choice : choice + 1, :] == owner
        hit = hit | same
        weight = jnp.where(same, rw_ref[choice : choice + 1, :], weight)
    row = lax.broadcasted_iota(jnp.int32, (rows, rows), 0)
    col = lax.broadcasted_iota(jnp.int32, (rows, rows), 1)
    before = (row < col).astype(F32).astype(BF16)
    rank = jnp.dot(hit.astype(F32).astype(BF16), before, preferred_element_type=F32)
    placed = hit & (rank == lax.rem(slot, CAP).astype(F32))
    place = placed.astype(F32).astype(BF16)
    place_ref[...] = place
    mix_ref[...] = jnp.where(placed, weight, 0.0)
    rows_ref[...] = jnp.dot(place, res_ref[...], preferred_element_type=F32)


def rest_kernel(n_ctx, back_count, q_ref, segs_ref, acc_ref, max_ref, sum_ref, place_ref, rows_ref, *refs):
    kv_refs = refs[:back_count]
    out_ref = refs[back_count]
    send_refs = refs[back_count + 1 :]
    rows = q_ref.shape[0]
    biases = score_bias(segs_ref, range(1, back_count + 1), n_ctx, rows)
    bias = jnp.concatenate(biases, axis=1)
    ones = jnp.ones((rows * back_count, HD), BF16)
    for kv in range(KVH):
        keys = jnp.concatenate([ref[:, kv * HD : (kv + 1) * HD] for ref in kv_refs], axis=0)
        values = jnp.concatenate(
            [ref[:, (KVH + kv) * HD : (KVH + kv + 1) * HD] for ref in kv_refs], axis=0
        )
        values = jnp.concatenate([values, ones], axis=1)
        for head in range(kv * GROUPS, (kv + 1) * GROUPS):
            old_max = max_ref[:, head : head + 1]
            scores = head_scores(q_ref, keys, head, bias)
            new_max = jnp.maximum(old_max, jnp.max(scores, axis=1, keepdims=True))
            expo = jnp.exp2(scores - new_max).astype(BF16)
            mixed = jnp.dot(expo, values, preferred_element_type=F32)
            fix = jnp.exp2(old_max - new_max)
            total = sum_ref[:, head : head + 1] * fix + mixed[:, HD : HD + 1]
            accum = acc_ref[:, head * HD : (head + 1) * HD] * fix + mixed[:, :HD]
            out_ref[:, head * HD : (head + 1) * HD] = (accum / total).astype(BF16)
    routed = jnp.dot(place_ref[...], out_ref[...], preferred_element_type=F32)
    wide = routed.shape[1]
    for step, ref in enumerate(send_refs):
        ref[:, :wide] = routed[step * CAP : (step + 1) * CAP, :].astype(BF16)
        ref[:, wide:] = rows_ref[step * CAP : (step + 1) * CAP, :].astype(BF16)


def stack(parts):
    return jnp.concatenate([part.astype(F32) for part in parts], axis=0).astype(BF16)


def project(total, att, starts, piece_refs):
    for start, ref in zip(starts, piece_refs):
        size = ref.shape[0]
        lead = pl.multiple_of(start(lax.axis_index("ctx"), lax.axis_index("dp")), size)
        total = total + jnp.dot(att(lead, size), ref[...], preferred_element_type=F32)
    return total


def expert_kernel(owners, starts, *refs):
    row_refs = refs[:owners]
    gain_ref, gate_ref, up_ref, down_ref = refs[owners : owners + 4]
    piece_refs = refs[owners + 4 : owners + 4 + len(starts)]
    out_refs = refs[owners + 4 + len(starts) : -1]
    att_ref = refs[-1]
    wide = att_ref.shape[1]
    att_ref[...] = stack([ref[:, :wide] for ref in row_refs])
    hidden = jnp.concatenate([ref[:, wide:].astype(F32) for ref in row_refs], axis=0)
    hidden = project(hidden, lambda lead, size: att_ref[:, pl.ds(lead, size)], starts, piece_refs)
    mean = jnp.mean(hidden * hidden, axis=1, keepdims=True)
    normed = (hidden * lax.rsqrt(mean + 1e-06) * gain_ref[...]).astype(BF16)
    gate = jnp.dot(normed, gate_ref[...], preferred_element_type=F32)
    up = jnp.dot(normed, up_ref[...], preferred_element_type=F32)
    act = (gate / (1.0 + jnp.exp(-gate)) * up).astype(BF16)
    out = jnp.dot(act, down_ref[...], preferred_element_type=F32)
    for step in range(owners):
        out_refs[step][...] = out[step * CAP : (step + 1) * CAP, :].astype(BF16)


def project_kernel(starts, att_ref, res_ref, *refs):
    hidden_ref = refs[-1]
    hidden_ref[...] = project(
        res_ref[...].astype(F32),
        lambda lead, size: att_ref[:, pl.ds(lead, size)],
        starts,
        refs[:-1],
    )


def combine_kernel(owners, hidden_ref, mix_ref, *refs):
    row_refs, out_ref = refs[:owners], refs[owners]
    rows = stack([ref[...] for ref in row_refs])
    mix = mix_ref[...]
    high = mix.astype(BF16)
    low = (mix - high.astype(F32)).astype(BF16)
    total = hidden_ref[...]
    for part in (high, low):
        total = total + lax.dot_general(
            part, rows, (((0,), (0,)), ((), ())), preferred_element_type=F32
        )
    out_ref[...] = total.astype(BF16)


def call(kernel, outs, args, micros, space=pltpu.VMEM, scratch=(), limit=24):
    spec = pl.BlockSpec(memory_space=space)
    nbytes = sum(math.prod(a.shape) * a.dtype.itemsize for a in list(args) + list(outs))
    return pl.pallas_call(
        kernel,
        out_shape=outs,
        in_specs=[spec] * len(args),
        out_specs=[spec] * len(outs),
        scratch_shapes=list(scratch),
        compiler_params=pltpu.CompilerParams(vmem_limit_bytes=limit << 20),
        cost_estimate=pl.CostEstimate(
            flops=int(micros * 1.15e9), bytes_accessed=nbytes, transcendentals=0
        ),
    )(*args)


def gather_weight(weight, mark):
    n_ctx, cores = lax.axis_size("ctx"), lax.axis_size("dp")
    share = weight.shape[0]
    if (n_ctx, cores) != (4, 2):
        whole = lax.all_gather(weight, "ctx", axis=0, tiled=True)
        return [whole], [lambda me, core: 0]
    both = ("ctx", "dp")
    devices = [(me, core) for me in range(n_ctx) for core in range(cores)]
    near = lax.ppermute(
        weight, both, [(me * 2 + core, (me ^ (1 + core)) * 2 + core) for me, core in devices]
    )
    near = after(near, mark)
    far = lax.ppermute(
        near, both, [(me * 2 + core, (me ^ (2 - core)) * 2 + core) for me, core in devices]
    )
    swapped = lax.ppermute(near, "dp", [(0, 1), (1, 0)])
    starts = [
        lambda me, core: me * share,
        lambda me, core: (me ^ (1 + core)) * share,
        lambda me, core: (me ^ (2 - core)) * share,
        lambda me, core: (me ^ 3) * share,
    ]
    return [weight, near, swapped, far], starts


def per_device(
    queries,
    keys,
    values,
    segments,
    residual,
    out_weight,
    gain,
    expert_ids,
    route_weights,
    w_gate,
    w_up,
    w_down,
):
    tok_rows = queries.shape[1]
    width = residual.shape[2]
    att_width = queries.shape[2]
    n_ctx, owners = lax.axis_size("ctx"), lax.axis_size("exp")
    slots = owners * CAP
    longest = segments.shape[1] // 2
    back_count = min(n_ctx - 1, -(-(longest - 1) // tok_rows))
    shape = jax.ShapeDtypeStruct

    (own_kv,) = call(
        pack_kernel,
        [shape((tok_rows, 2 * KVH * HD), BF16)],
        [keys[0], values[0]],
        micros=1,
        space=pl.ANY,
        limit=60,
        scratch=[pltpu.SemaphoreType.DMA((2,))],
    )
    kv_blocks = []
    for back in range(1, back_count + 1):
        pairs = [(i, (i + back) % n_ctx) for i in range(n_ctx)]
        kv_blocks.append(lax.ppermute(own_kv, "ctx", pairs))
    accum, row_max, row_sum, place, mix, rows = call(
        functools.partial(own_kernel, n_ctx),
        [
            shape((tok_rows, att_width), F32),
            shape((tok_rows, HQ), F32),
            shape((tok_rows, HQ), F32),
            shape((slots, tok_rows), BF16),
            shape((slots, tok_rows), F32),
            shape((slots, width), F32),
        ],
        [queries[0], own_kv, segments, expert_ids[0].T, route_weights[0].T, residual[0]],
        micros=3,
    )
    attended, *sends = call(
        functools.partial(rest_kernel, n_ctx, back_count),
        [shape((tok_rows, att_width), BF16)] + [shape((CAP, att_width + width), BF16)] * owners,
        [queries[0], segments, accum, row_max, row_sum, place, rows, *kv_blocks],
        micros=5,
    )
    pieces, starts = gather_weight(out_weight, attended)
    rows = [sends[0]]
    for step in range(1, owners):
        pairs = [(i, (i + step) % owners) for i in range(owners)]
        rows.append(lax.ppermute(sends[step], "exp", pairs))
    done = call(
        functools.partial(expert_kernel, owners, starts),
        [shape((CAP, width), BF16)] * owners,
        [*rows, gain[None, :], w_gate[0], w_up[0], w_down[0], *pieces],
        micros=2,
        scratch=[pltpu.VMEM((slots, att_width), BF16)],
    )
    back = [done[0]]
    for step in range(1, owners):
        pairs = [((i + step) % owners, i) for i in range(owners)]
        back.append(lax.ppermute(done[step], "exp", pairs))
    (hidden,) = call(
        functools.partial(project_kernel, starts),
        [shape((tok_rows, width), F32)],
        [attended, residual[0], *pieces],
        micros=2,
    )
    (out,) = call(
        functools.partial(combine_kernel, owners),
        [shape((tok_rows, width), BF16)],
        [hidden, mix, *back],
        micros=1,
    )
    return out[None]


def solution(mesh):
    return jax.shard_map(
        per_device,
        mesh=mesh,
        in_specs=(
            P(("dp", "exp"), "ctx", None),
            P(("dp", "exp"), "ctx", None),
            P(("dp", "exp"), "ctx", None),
            P(("dp", "exp"), None),
            P(("dp", "exp"), "ctx", None),
            P("ctx", None),
            P(),
            P(("dp", "exp"), "ctx", None),
            P(("dp", "exp"), "ctx", None),
            P("exp", None, None),
            P("exp", None, None),
            P("exp", None, None),
        ),
        out_specs=P(("dp", "exp"), "ctx", None),
        check_vma=False,
    )
```

```python
import functools
import math

import jax
import jax.numpy as jnp
from jax import lax
from jax.experimental import pallas as pl
from jax.experimental.pallas import tpu as pltpu
from jax.sharding import PartitionSpec as P

HQ = 16
KVH = 2
HD = 128
GROUPS = HQ // KVH
CAP = 24
NEG = -1e30
SCORE_SCALE = math.log2(math.e) / math.sqrt(HD)
F32 = jnp.float32
BF16 = jnp.bfloat16


def slab_segments(segs_ref, index, count, rows):
    found = segs_ref[:, 0:rows]
    for slab in range(1, count):
        found = jnp.where(index == slab, segs_ref[:, slab * rows : (slab + 1) * rows], found)
    return found


def score_bias(segs_ref, backs, count, rows):
    me = lax.axis_index("ctx")
    row = lax.broadcasted_iota(jnp.int32, (rows, rows), 0)
    col = lax.broadcasted_iota(jnp.int32, (rows, rows), 1)
    own_seg = slab_segments(segs_ref, me, count, rows)
    query_seg = jnp.sum(jnp.where(row == col, own_seg, 0), axis=1, keepdims=True)
    parts = []
    for back in backs:
        if back == 0:
            allowed = (col <= row) & (own_seg == query_seg)
        else:
            key_seg = slab_segments(segs_ref, jnp.maximum(me - back, 0), count, rows)
            allowed = (key_seg == query_seg) & (me >= back)
        parts.append(jnp.where(allowed, 0.0, NEG))
    return parts


def group_scores(q_ref, keys, kv, bias):
    heads = range(kv * GROUPS, (kv + 1) * GROUPS)
    stacked = jnp.concatenate([q_ref[:, h * HD : (h + 1) * HD] for h in heads], axis=0)
    scores = lax.dot_general(
        stacked, keys, (((1,), (1,)), ((), ())), preferred_element_type=F32
    )
    return scores.reshape(GROUPS, *bias.shape) * SCORE_SCALE + bias


def weigh(expo, values):
    rows = expo.shape[0] * expo.shape[1]
    mixed = jnp.dot(
        expo.astype(BF16).reshape(rows, expo.shape[2]), values, preferred_element_type=F32
    ).reshape(*expo.shape[:2], 2 * HD)
    return mixed[:, :, :HD], mixed[:, :, HD : HD + 1]


def gate_kernel(*refs):
    del refs


def after(piece, *marks):
    spec = pl.BlockSpec(memory_space=pl.ANY)
    return pl.pallas_call(
        gate_kernel,
        out_shape=jax.ShapeDtypeStruct(piece.shape, piece.dtype),
        in_specs=[spec] * (1 + len(marks)),
        out_specs=spec,
        input_output_aliases={0: 0},
        compiler_params=pltpu.CompilerParams(vmem_limit_bytes=1 << 20),
    )(piece, *marks)


def send_rows(place, values, send_refs):
    routed = jnp.dot(place, values, preferred_element_type=F32)
    for step, ref in enumerate(send_refs):
        ref[...] = routed[step * CAP : (step + 1) * CAP, :].astype(BF16)


def own_kernel(
    n_ctx,
    q_ref,
    kv_ref,
    segs_ref,
    ids_ref,
    rw_ref,
    res_ref,
    acc_ref,
    max_ref,
    sum_ref,
    place_ref,
    mix_ref,
    *send_refs,
):
    rows = q_ref.shape[0]
    slots = mix_ref.shape[0]
    (bias,) = score_bias(segs_ref, (0,), n_ctx, rows)
    ones = jnp.ones((rows, HD), BF16)
    for kv in range(KVH):
        keys = kv_ref[:, kv * HD : (kv + 1) * HD]
        values = jnp.concatenate([kv_ref[:, (KVH + kv) * HD : (KVH + kv + 1) * HD], ones], axis=1)
        scores = group_scores(q_ref, keys, kv, bias)
        row_max = jnp.max(scores, axis=2, keepdims=True)
        accum, row_sum = weigh(jnp.exp2(scores - row_max), values)
        acc_ref[kv] = accum
        max_ref[kv] = row_max
        sum_ref[kv] = row_sum
    slot = lax.broadcasted_iota(jnp.int32, (slots, rows), 0)
    owner = lax.rem(slot // CAP + lax.axis_index("exp"), slots // CAP)
    hit = jnp.zeros((slots, rows), jnp.bool_)
    weight = jnp.zeros((slots, rows), F32)
    for choice in range(ids_ref.shape[0]):
        same = ids_ref[choice : choice + 1, :] == owner
        hit = hit | same
        weight = jnp.where(same, rw_ref[choice : choice + 1, :], weight)
    row = lax.broadcasted_iota(jnp.int32, (rows, rows), 0)
    col = lax.broadcasted_iota(jnp.int32, (rows, rows), 1)
    before = (row < col).astype(F32).astype(BF16)
    rank = jnp.dot(hit.astype(F32).astype(BF16), before, preferred_element_type=F32)
    placed = hit & (rank == lax.rem(slot, CAP).astype(F32))
    place = placed.astype(F32).astype(BF16)
    place_ref[...] = place
    mix_ref[...] = jnp.where(placed, weight, 0.0)
    send_rows(place, res_ref[...], send_refs)


def rest_kernel(
    n_ctx, back_count, q_ref, segs_ref, acc_ref, max_ref, sum_ref, place_ref, *refs
):
    kv_refs = refs[:back_count]
    out_ref, *send_refs = refs[-1 - lax.axis_size("exp") :]
    rows = q_ref.shape[0]
    biases = score_bias(segs_ref, range(1, back_count + 1), n_ctx, rows)
    bias = jnp.concatenate(biases, axis=1)
    ones = jnp.ones((rows * back_count, HD), BF16)
    for kv in range(KVH):
        keys = jnp.concatenate([ref[:, kv * HD : (kv + 1) * HD] for ref in kv_refs], axis=0)
        values = jnp.concatenate(
            [ref[:, (KVH + kv) * HD : (KVH + kv + 1) * HD] for ref in kv_refs], axis=0
        )
        values = jnp.concatenate([values, ones], axis=1)
        scores = group_scores(q_ref, keys, kv, bias)
        old_max = max_ref[kv]
        new_max = jnp.maximum(old_max, jnp.max(scores, axis=2, keepdims=True))
        accum, row_sum = weigh(jnp.exp2(scores - new_max), values)
        fix = jnp.exp2(old_max - new_max)
        total = sum_ref[kv] * fix + row_sum
        attended = ((acc_ref[kv] * fix + accum) / total).astype(BF16)
        for group in range(GROUPS):
            head = kv * GROUPS + group
            out_ref[:, head * HD : (head + 1) * HD] = attended[group]
    send_rows(place_ref[...], out_ref[...], send_refs)


def stack(parts):
    return jnp.concatenate([part.astype(F32) for part in parts], axis=0).astype(BF16)


def project(total, att, starts, piece_refs):
    for start, ref in zip(starts, piece_refs):
        size = ref.shape[0]
        lead = pl.multiple_of(start(lax.axis_index("ctx"), lax.axis_index("dp")), size)
        total = total + jnp.dot(att(lead, size), ref[...], preferred_element_type=F32)
    return total


def expert_kernel(owners, starts, gain_ref, gate_ref, up_ref, down_ref, *refs):
    att_refs, res_refs, refs = refs[:owners], refs[owners : 2 * owners], refs[2 * owners :]
    piece_refs, out_refs, att_ref = refs[: len(starts)], refs[len(starts) : -1], refs[-1]
    att_ref[...] = stack([ref[...] for ref in att_refs])
    hidden = jnp.concatenate([ref[...].astype(F32) for ref in res_refs], axis=0)
    hidden = project(hidden, lambda lead, size: att_ref[:, pl.ds(lead, size)], starts, piece_refs)
    mean = jnp.mean(hidden * hidden, axis=1, keepdims=True)
    normed = (hidden * lax.rsqrt(mean + 1e-06) * gain_ref[...]).astype(BF16)
    gate = jnp.dot(normed, gate_ref[...], preferred_element_type=F32)
    up = jnp.dot(normed, up_ref[...], preferred_element_type=F32)
    act = (gate / (1.0 + jnp.exp(-gate)) * up).astype(BF16)
    out = jnp.dot(act, down_ref[...], preferred_element_type=F32)
    for step in range(owners):
        out_refs[step][...] = out[step * CAP : (step + 1) * CAP, :].astype(BF16)


def project_kernel(starts, att_ref, res_ref, *refs):
    hidden_ref = refs[-1]
    hidden_ref[...] = project(
        res_ref[...].astype(F32),
        lambda lead, size: att_ref[:, pl.ds(lead, size)],
        starts,
        refs[:-1],
    )


def combine_kernel(owners, hidden_ref, mix_ref, *refs):
    row_refs, out_ref = refs[:owners], refs[owners]
    rows = stack([ref[...] for ref in row_refs])
    mix = mix_ref[...]
    high = mix.astype(BF16)
    low = (mix - high.astype(F32)).astype(BF16)
    total = hidden_ref[...]
    for part in (high, low):
        total = total + lax.dot_general(
            part, rows, (((0,), (0,)), ((), ())), preferred_element_type=F32
        )
    out_ref[...] = total.astype(BF16)


def call(kernel, outs, args, micros, space=pltpu.VMEM, scratch=(), limit=24):
    spec = pl.BlockSpec(memory_space=space)
    nbytes = sum(math.prod(a.shape) * a.dtype.itemsize for a in list(args) + list(outs))
    return pl.pallas_call(
        kernel,
        out_shape=outs,
        in_specs=[spec] * len(args),
        out_specs=[spec] * len(outs),
        scratch_shapes=list(scratch),
        compiler_params=pltpu.CompilerParams(vmem_limit_bytes=limit << 20),
        cost_estimate=pl.CostEstimate(
            flops=int(micros * 1.15e9), bytes_accessed=nbytes, transcendentals=0
        ),
    )(*args)


def exchange(blocks, sign):
    count = len(blocks)
    pairs = [[(i, (i + sign * s) % count) for i in range(count)] for s in range(count)]
    return [blocks[0]] + [lax.ppermute(blocks[s], "exp", pairs[s]) for s in range(1, count)]


def gather_weight(weight, *marks):
    n_ctx, cores = lax.axis_size("ctx"), lax.axis_size("dp")
    share = weight.shape[0]
    if (n_ctx, cores) != (4, 2):
        whole = lax.all_gather(weight, "ctx", axis=0, tiled=True)
        return [whole], [lambda me, core: 0]
    both = ("ctx", "dp")
    devices = [(me, core) for me in range(n_ctx) for core in range(cores)]
    near = lax.ppermute(
        weight, both, [(me * 2 + core, (me ^ (1 + core)) * 2 + core) for me, core in devices]
    )
    near = after(near, *marks)
    far = lax.ppermute(
        near, both, [(me * 2 + core, (me ^ (2 - core)) * 2 + core) for me, core in devices]
    )
    swapped = lax.ppermute(near, "dp", [(0, 1), (1, 0)])
    starts = [
        lambda me, core: me * share,
        lambda me, core: (me ^ (1 + core)) * share,
        lambda me, core: (me ^ (2 - core)) * share,
        lambda me, core: (me ^ 3) * share,
    ]
    return [weight, near, swapped, far], starts


def per_device(
    queries,
    keys,
    values,
    segments,
    residual,
    out_weight,
    gain,
    expert_ids,
    route_weights,
    w_gate,
    w_up,
    w_down,
):
    tok_rows = queries.shape[1]
    width = residual.shape[2]
    att_width = queries.shape[2]
    n_ctx, owners = lax.axis_size("ctx"), lax.axis_size("exp")
    slots = owners * CAP
    longest = segments.shape[1] // 2
    back_count = min(n_ctx - 1, -(-(longest - 1) // tok_rows))
    shape = jax.ShapeDtypeStruct

    own_kv = jnp.concatenate([keys[0], values[0]], axis=1)
    kv_blocks = []
    for back in range(1, back_count + 1):
        pairs = [(i, (i + back) % n_ctx) for i in range(n_ctx)]
        kv_blocks.append(lax.ppermute(own_kv, "ctx", pairs))
    accum, row_max, row_sum, place, mix, *res_rows = call(
        functools.partial(own_kernel, n_ctx),
        [
            shape((KVH, GROUPS, tok_rows, HD), F32),
            shape((KVH, GROUPS, tok_rows, 1), F32),
            shape((KVH, GROUPS, tok_rows, 1), F32),
            shape((slots, tok_rows), BF16),
            shape((slots, tok_rows), F32),
        ]
        + [shape((CAP, width), BF16)] * owners,
        [queries[0], own_kv, segments, expert_ids[0].T, route_weights[0].T, residual[0]],
        micros=3,
    )
    res_rows = exchange(res_rows, 1)
    attended, *att_rows = call(
        functools.partial(rest_kernel, n_ctx, back_count),
        [shape((tok_rows, att_width), BF16)] + [shape((CAP, att_width), BF16)] * owners,
        [queries[0], segments, accum, row_max, row_sum, place, *kv_blocks],
        micros=5,
    )
    pieces, starts = gather_weight(out_weight, *kv_blocks, *res_rows[1:])
    done = call(
        functools.partial(expert_kernel, owners, starts),
        [shape((CAP, width), BF16)] * owners,
        [gain[None, :], w_gate[0], w_up[0], w_down[0]]
        + [*exchange(att_rows, 1), *res_rows, *pieces],
        micros=2,
        scratch=[pltpu.VMEM((slots, att_width), BF16)],
    )
    back = exchange(done, -1)
    (hidden,) = call(
        functools.partial(project_kernel, starts),
        [shape((tok_rows, width), F32)],
        [attended, residual[0], *pieces],
        micros=2,
    )
    (out,) = call(
        functools.partial(combine_kernel, owners),
        [shape((tok_rows, width), BF16)],
        [hidden, mix, *back],
        micros=1,
    )
    return out[None]


def solution(mesh):
    return jax.shard_map(
        per_device,
        mesh=mesh,
        in_specs=(
            P(("dp", "exp"), "ctx", None),
            P(("dp", "exp"), "ctx", None),
            P(("dp", "exp"), "ctx", None),
            P(("dp", "exp"), None),
            P(("dp", "exp"), "ctx", None),
            P("ctx", None),
            P(),
            P(("dp", "exp"), "ctx", None),
            P(("dp", "exp"), "ctx", None),
            P("exp", None, None),
            P("exp", None, None),
            P("exp", None, None),
        ),
        out_specs=P(("dp", "exp"), "ctx", None),
        check_vma=False,
    )
```

```python
import functools
import math

import jax
import jax.numpy as jnp
from jax import lax
from jax.experimental import pallas as pl
from jax.experimental.pallas import tpu as pltpu
from jax.sharding import PartitionSpec as P

HQ = 16
KVH = 2
HD = 128
GROUPS = HQ // KVH
CAP = 24
NEG = -1e30
SCORE_SCALE = math.log2(math.e) / math.sqrt(HD)
F32 = jnp.float32
BF16 = jnp.bfloat16


def slab_segments(segs_ref, index, count, rows):
    found = segs_ref[:, 0:rows]
    for slab in range(1, count):
        found = jnp.where(index == slab, segs_ref[:, slab * rows : (slab + 1) * rows], found)
    return found


def score_bias(segs_ref, backs, count, rows):
    me = lax.axis_index("ctx")
    row = lax.broadcasted_iota(jnp.int32, (rows, rows), 0)
    col = lax.broadcasted_iota(jnp.int32, (rows, rows), 1)
    own_seg = slab_segments(segs_ref, me, count, rows)
    query_seg = jnp.sum(jnp.where(row == col, own_seg, 0), axis=1, keepdims=True)
    parts = []
    for back in backs:
        if back == 0:
            allowed = (col <= row) & (own_seg == query_seg)
        else:
            key_seg = slab_segments(segs_ref, jnp.maximum(me - back, 0), count, rows)
            allowed = (key_seg == query_seg) & (me >= back)
        parts.append(jnp.where(allowed, 0.0, NEG))
    return parts


def group_scores(stacked, keys, bias):
    scores = lax.dot_general(
        stacked, keys, (((1,), (1,)), ((), ())), preferred_element_type=F32
    )
    return scores.reshape(GROUPS, *bias.shape) * SCORE_SCALE + bias


def weigh(expo, values):
    rows = expo.shape[0] * expo.shape[1]
    mixed = jnp.dot(
        expo.astype(BF16).reshape(rows, expo.shape[2]), values, preferred_element_type=F32
    ).reshape(*expo.shape[:2], 2 * HD)
    return mixed[:, :, :HD], mixed[:, :, HD : HD + 1]


def gate_kernel(*refs):
    del refs


def after(piece, *marks):
    spec = pl.BlockSpec(memory_space=pl.ANY)
    return pl.pallas_call(
        gate_kernel,
        out_shape=jax.ShapeDtypeStruct(piece.shape, piece.dtype),
        in_specs=[spec] * (1 + len(marks)),
        out_specs=spec,
        input_output_aliases={0: 0},
        compiler_params=pltpu.CompilerParams(vmem_limit_bytes=1 << 20),
    )(piece, *marks)


def own_kernel(
    n_ctx,
    q_ref,
    kv_ref,
    segs_ref,
    ids_ref,
    rw_ref,
    res_ref,
    acc_ref,
    max_ref,
    sum_ref,
    place_ref,
    mix_ref,
    queries_ref,
    rows_ref,
):
    rows = q_ref.shape[0]
    slots = mix_ref.shape[0]
    (bias,) = score_bias(segs_ref, (0,), n_ctx, rows)
    ones = jnp.ones((rows, HD), BF16)
    for kv in range(KVH):
        keys = kv_ref[:, kv * HD : (kv + 1) * HD]
        values = jnp.concatenate([kv_ref[:, (KVH + kv) * HD : (KVH + kv + 1) * HD], ones], axis=1)
        heads = range(kv * GROUPS, (kv + 1) * GROUPS)
        stacked = jnp.concatenate([q_ref[:, h * HD : (h + 1) * HD] for h in heads], axis=0)
        queries_ref[kv] = stacked
        scores = group_scores(stacked, keys, bias)
        row_max = jnp.max(scores, axis=2, keepdims=True)
        accum, row_sum = weigh(jnp.exp2(scores - row_max), values)
        acc_ref[kv] = accum
        max_ref[kv] = row_max
        sum_ref[kv] = row_sum
    slot = lax.broadcasted_iota(jnp.int32, (slots, rows), 0)
    owner = lax.rem(slot // CAP + lax.axis_index("exp"), slots // CAP)
    hit = jnp.zeros((slots, rows), jnp.bool_)
    weight = jnp.zeros((slots, rows), F32)
    for choice in range(ids_ref.shape[0]):
        same = ids_ref[choice : choice + 1, :] == owner
        hit = hit | same
        weight = jnp.where(same, rw_ref[choice : choice + 1, :], weight)
    row = lax.broadcasted_iota(jnp.int32, (rows, rows), 0)
    col = lax.broadcasted_iota(jnp.int32, (rows, rows), 1)
    before = (row < col).astype(F32).astype(BF16)
    rank = jnp.dot(hit.astype(F32).astype(BF16), before, preferred_element_type=F32)
    placed = hit & (rank == lax.rem(slot, CAP).astype(F32))
    place = placed.astype(F32).astype(BF16)
    place_ref[...] = place
    mix_ref[...] = jnp.where(placed, weight, 0.0)
    rows_ref[...] = jnp.dot(place, res_ref[...], preferred_element_type=F32)


def rest_kernel(
    n_ctx,
    back_count,
    segs_ref,
    acc_ref,
    max_ref,
    sum_ref,
    place_ref,
    queries_ref,
    rows_ref,
    *refs,
):
    kv_refs = refs[:back_count]
    out_ref, *send_refs = refs[-1 - lax.axis_size("exp") :]
    rows = queries_ref.shape[1] // GROUPS
    biases = score_bias(segs_ref, range(1, back_count + 1), n_ctx, rows)
    bias = jnp.concatenate(biases, axis=1)
    ones = jnp.ones((rows * back_count, HD), BF16)
    for kv in range(KVH):
        keys = jnp.concatenate([ref[:, kv * HD : (kv + 1) * HD] for ref in kv_refs], axis=0)
        values = jnp.concatenate(
            [ref[:, (KVH + kv) * HD : (KVH + kv + 1) * HD] for ref in kv_refs], axis=0
        )
        values = jnp.concatenate([values, ones], axis=1)
        scores = group_scores(queries_ref[kv], keys, bias)
        old_max = max_ref[kv]
        new_max = jnp.maximum(old_max, jnp.max(scores, axis=2, keepdims=True))
        accum, row_sum = weigh(jnp.exp2(scores - new_max), values)
        fix = jnp.exp2(old_max - new_max)
        total = sum_ref[kv] * fix + row_sum
        attended = ((acc_ref[kv] * fix + accum) / total).astype(BF16)
        for group in range(GROUPS):
            head = kv * GROUPS + group
            out_ref[:, head * HD : (head + 1) * HD] = attended[group]
    routed = jnp.dot(place_ref[...], out_ref[...], preferred_element_type=F32)
    wide = routed.shape[1]
    for step, ref in enumerate(send_refs):
        ref[:, :wide] = routed[step * CAP : (step + 1) * CAP, :].astype(BF16)
        ref[:, wide:] = rows_ref[step * CAP : (step + 1) * CAP, :].astype(BF16)


def stack(parts):
    return jnp.concatenate([part.astype(F32) for part in parts], axis=0).astype(BF16)


def project(total, att, starts, piece_refs):
    for start, ref in zip(starts, piece_refs):
        size = ref.shape[0]
        lead = pl.multiple_of(start(lax.axis_index("ctx"), lax.axis_index("dp")), size)
        total = total + jnp.dot(att(lead, size), ref[...], preferred_element_type=F32)
    return total


def expert_kernel(owners, starts, gain_ref, gate_ref, up_ref, down_ref, *refs):
    row_refs, refs = refs[:owners], refs[owners:]
    piece_refs, out_refs, att_ref = refs[: len(starts)], refs[len(starts) : -1], refs[-1]
    wide = att_ref.shape[1]
    att_ref[...] = stack([ref[:, :wide] for ref in row_refs])
    hidden = jnp.concatenate([ref[:, wide:].astype(F32) for ref in row_refs], axis=0)
    hidden = project(hidden, lambda lead, size: att_ref[:, pl.ds(lead, size)], starts, piece_refs)
    mean = jnp.mean(hidden * hidden, axis=1, keepdims=True)
    normed = (hidden * lax.rsqrt(mean + 1e-06) * gain_ref[...]).astype(BF16)
    gate = jnp.dot(normed, gate_ref[...], preferred_element_type=F32)
    up = jnp.dot(normed, up_ref[...], preferred_element_type=F32)
    act = (gate / (1.0 + jnp.exp(-gate)) * up).astype(BF16)
    out = jnp.dot(act, down_ref[...], preferred_element_type=F32)
    for step in range(owners):
        out_refs[step][...] = out[step * CAP : (step + 1) * CAP, :].astype(BF16)


def project_kernel(starts, att_ref, res_ref, *refs):
    hidden_ref = refs[-1]
    hidden_ref[...] = project(
        res_ref[...].astype(F32),
        lambda lead, size: att_ref[:, pl.ds(lead, size)],
        starts,
        refs[:-1],
    )


def combine_kernel(owners, hidden_ref, mix_ref, *refs):
    row_refs, out_ref = refs[:owners], refs[owners]
    rows = stack([ref[...] for ref in row_refs])
    mix = mix_ref[...]
    high = mix.astype(BF16)
    low = (mix - high.astype(F32)).astype(BF16)
    total = hidden_ref[...]
    for part in (high, low):
        total = total + lax.dot_general(
            part, rows, (((0,), (0,)), ((), ())), preferred_element_type=F32
        )
    out_ref[...] = total.astype(BF16)


def call(kernel, outs, args, micros, scratch=(), limit=24):
    spec = pl.BlockSpec(memory_space=pltpu.VMEM)
    nbytes = sum(math.prod(a.shape) * a.dtype.itemsize for a in list(args) + list(outs))
    return pl.pallas_call(
        kernel,
        out_shape=outs,
        in_specs=[spec] * len(args),
        out_specs=[spec] * len(outs),
        scratch_shapes=list(scratch),
        compiler_params=pltpu.CompilerParams(vmem_limit_bytes=limit << 20),
        cost_estimate=pl.CostEstimate(
            flops=int(micros * 1.15e9), bytes_accessed=nbytes, transcendentals=0
        ),
    )(*args)


def exchange(blocks, sign):
    count = len(blocks)
    pairs = [[(i, (i + sign * s) % count) for i in range(count)] for s in range(count)]
    return [blocks[0]] + [lax.ppermute(blocks[s], "exp", pairs[s]) for s in range(1, count)]


def gather_weight(weight, *marks):
    n_ctx, cores = lax.axis_size("ctx"), lax.axis_size("dp")
    share = weight.shape[0]
    if (n_ctx, cores) != (4, 2):
        whole = lax.all_gather(weight, "ctx", axis=0, tiled=True)
        return [whole], [lambda me, core: 0]
    both = ("ctx", "dp")
    devices = [(me, core) for me in range(n_ctx) for core in range(cores)]
    near = lax.ppermute(
        weight, both, [(me * 2 + core, (me ^ (1 + core)) * 2 + core) for me, core in devices]
    )
    near = after(near, *marks)
    far = lax.ppermute(
        near, both, [(me * 2 + core, (me ^ (2 - core)) * 2 + core) for me, core in devices]
    )
    swapped = lax.ppermute(near, "dp", [(0, 1), (1, 0)])
    starts = [
        lambda me, core: me * share,
        lambda me, core: (me ^ (1 + core)) * share,
        lambda me, core: (me ^ (2 - core)) * share,
        lambda me, core: (me ^ 3) * share,
    ]
    return [weight, near, swapped, far], starts


def per_device(
    queries,
    keys,
    values,
    segments,
    residual,
    out_weight,
    gain,
    expert_ids,
    route_weights,
    w_gate,
    w_up,
    w_down,
):
    tok_rows = queries.shape[1]
    width = residual.shape[2]
    att_width = queries.shape[2]
    n_ctx, owners = lax.axis_size("ctx"), lax.axis_size("exp")
    slots = owners * CAP
    longest = segments.shape[1] // 2
    back_count = min(n_ctx - 1, -(-(longest - 1) // tok_rows))
    shape = jax.ShapeDtypeStruct

    own_kv = jnp.concatenate([keys[0], values[0]], axis=1)
    kv_blocks = []
    for back in range(1, back_count + 1):
        pairs = [(i, (i + back) % n_ctx) for i in range(n_ctx)]
        kv_blocks.append(lax.ppermute(own_kv, "ctx", pairs))
    accum, row_max, row_sum, place, mix, stacked, res_rows = call(
        functools.partial(own_kernel, n_ctx),
        [
            shape((KVH, GROUPS, tok_rows, HD), F32),
            shape((KVH, GROUPS, tok_rows, 1), F32),
            shape((KVH, GROUPS, tok_rows, 1), F32),
            shape((slots, tok_rows), BF16),
            shape((slots, tok_rows), F32),
            shape((KVH, GROUPS * tok_rows, HD), BF16),
            shape((slots, width), F32),
        ],
        [queries[0], own_kv, segments, expert_ids[0].T, route_weights[0].T, residual[0]],
        micros=3,
    )
    attended, *routed = call(
        functools.partial(rest_kernel, n_ctx, back_count),
        [shape((tok_rows, att_width), BF16)]
        + [shape((CAP, att_width + width), BF16)] * owners,
        [segments, accum, row_max, row_sum, place, stacked, res_rows, *kv_blocks],
        micros=5,
    )
    pieces, starts = gather_weight(out_weight, place, *kv_blocks)
    done = call(
        functools.partial(expert_kernel, owners, starts),
        [shape((CAP, width), BF16)] * owners,
        [gain[None, :], w_gate[0], w_up[0], w_down[0]]
        + [*exchange(routed, 1), *pieces],
        micros=2,
        scratch=[pltpu.VMEM((slots, att_width), BF16)],
    )
    back = exchange(done, -1)
    (hidden,) = call(
        functools.partial(project_kernel, starts),
        [shape((tok_rows, width), F32)],
        [attended, residual[0], *pieces],
        micros=2,
    )
    (out,) = call(
        functools.partial(combine_kernel, owners),
        [shape((tok_rows, width), BF16)],
        [hidden, mix, *back],
        micros=1,
    )
    return out[None]


def solution(mesh):
    return jax.shard_map(
        per_device,
        mesh=mesh,
        in_specs=(
            P(("dp", "exp"), "ctx", None),
            P(("dp", "exp"), "ctx", None),
            P(("dp", "exp"), "ctx", None),
            P(("dp", "exp"), None),
            P(("dp", "exp"), "ctx", None),
            P("ctx", None),
            P(),
            P(("dp", "exp"), "ctx", None),
            P(("dp", "exp"), "ctx", None),
            P("exp", None, None),
            P("exp", None, None),
            P("exp", None, None),
        ),
        out_specs=P(("dp", "exp"), "ctx", None),
        check_vma=False,
    )
```

```python
import functools
import math

import jax
import jax.numpy as jnp
from jax import lax
from jax.experimental import pallas as pl
from jax.experimental.pallas import tpu as pltpu
from jax.sharding import PartitionSpec as P

HQ = 16
KVH = 2
HD = 128
GROUPS = HQ // KVH
CAP = 24
NEG = -1e30
SCORE_SCALE = math.log2(math.e) / math.sqrt(HD)
F32 = jnp.float32
BF16 = jnp.bfloat16


def slab_segments(segs_ref, index, count, rows):
    found = segs_ref[:, 0:rows]
    for slab in range(1, count):
        found = jnp.where(index == slab, segs_ref[:, slab * rows : (slab + 1) * rows], found)
    return found


def score_bias(segs_ref, backs, count, rows):
    me = lax.axis_index("ctx")
    row = lax.broadcasted_iota(jnp.int32, (rows, rows), 0)
    col = lax.broadcasted_iota(jnp.int32, (rows, rows), 1)
    own_seg = slab_segments(segs_ref, me, count, rows)
    query_seg = jnp.sum(jnp.where(row == col, own_seg, 0), axis=1, keepdims=True)
    parts = []
    for back in backs:
        if back == 0:
            allowed = (col <= row) & (own_seg == query_seg)
        else:
            key_seg = slab_segments(segs_ref, jnp.maximum(me - back, 0), count, rows)
            allowed = (key_seg == query_seg) & (me >= back)
        parts.append(jnp.where(allowed, 0.0, NEG))
    return parts


def group_scores(stacked, keys, bias):
    scores = lax.dot_general(
        stacked, keys, (((1,), (1,)), ((), ())), preferred_element_type=F32
    )
    return scores.reshape(GROUPS, *bias.shape) * SCORE_SCALE + bias


def weigh(expo, values):
    rows = expo.shape[0] * expo.shape[1]
    mixed = jnp.dot(
        expo.astype(BF16).reshape(rows, expo.shape[2]), values, preferred_element_type=F32
    ).reshape(*expo.shape[:2], 2 * HD)
    return mixed[:, :, :HD], mixed[:, :, HD : HD + 1]


def gate_kernel(*refs):
    del refs


def after(piece, *marks):
    spec = pl.BlockSpec(memory_space=pl.ANY)
    return pl.pallas_call(
        gate_kernel,
        out_shape=jax.ShapeDtypeStruct(piece.shape, piece.dtype),
        in_specs=[spec] * (1 + len(marks)),
        out_specs=spec,
        input_output_aliases={0: 0},
        compiler_params=pltpu.CompilerParams(vmem_limit_bytes=1 << 20),
    )(piece, *marks)


def join_kernel(first_ref, second_ref, mark_ref, whole_ref, sems):
    del mark_ref
    half = first_ref.shape[0]
    core = lax.rem(lax.axis_index("dp"), 2)
    copies = []
    for index, (lead, ref) in enumerate([(core, first_ref), (1 - core, second_ref)]):
        target = whole_ref.at[pl.ds(pl.multiple_of(lead * half, half), half)]
        copies.append(pltpu.make_async_copy(ref, target, sems.at[index]))
        copies[-1].start()
    for copy in copies:
        copy.wait()


def own_kernel(
    n_ctx,
    q_ref,
    kv_ref,
    segs_ref,
    w_ref,
    acc_ref,
    max_ref,
    sum_ref,
    queries_ref,
    first_ref,
    second_ref,
    sems,
):
    half = first_ref.shape[0]
    core = lax.rem(lax.axis_index("dp"), 2)
    copies = []
    for index, (lead, ref) in enumerate([(core, first_ref), (1 - core, second_ref)]):
        source = w_ref.at[pl.ds(pl.multiple_of(lead * half, half), half)]
        copies.append(pltpu.make_async_copy(source, ref, sems.at[index]))
        copies[-1].start()
    rows = q_ref.shape[0]
    (bias,) = score_bias(segs_ref, (0,), n_ctx, rows)
    ones = jnp.ones((rows, HD), BF16)
    for kv in range(KVH):
        keys = kv_ref[:, kv * HD : (kv + 1) * HD]
        values = jnp.concatenate([kv_ref[:, (KVH + kv) * HD : (KVH + kv + 1) * HD], ones], axis=1)
        heads = range(kv * GROUPS, (kv + 1) * GROUPS)
        stacked = jnp.concatenate([q_ref[:, h * HD : (h + 1) * HD] for h in heads], axis=0)
        queries_ref[kv] = stacked
        scores = group_scores(stacked, keys, bias)
        row_max = jnp.max(scores, axis=2, keepdims=True)
        accum, row_sum = weigh(jnp.exp2(scores - row_max), values)
        acc_ref[kv] = accum
        max_ref[kv] = row_max
        sum_ref[kv] = row_sum
    for copy in copies:
        copy.wait()


def route_kernel(ids_ref, rw_ref, res_ref, place_ref, mix_ref, rows_ref):
    slots, rows = mix_ref.shape
    slot = lax.broadcasted_iota(jnp.int32, (slots, rows), 0)
    owner = lax.rem(slot // CAP + lax.axis_index("exp"), slots // CAP)
    hit = jnp.zeros((slots, rows), jnp.bool_)
    weight = jnp.zeros((slots, rows), F32)
    for choice in range(ids_ref.shape[0]):
        same = ids_ref[choice : choice + 1, :] == owner
        hit = hit | same
        weight = jnp.where(same, rw_ref[choice : choice + 1, :], weight)
    row = lax.broadcasted_iota(jnp.int32, (rows, rows), 0)
    col = lax.broadcasted_iota(jnp.int32, (rows, rows), 1)
    before = (row < col).astype(F32).astype(BF16)
    rank = jnp.dot(hit.astype(F32).astype(BF16), before, preferred_element_type=F32)
    placed = hit & (rank == lax.rem(slot, CAP).astype(F32))
    place = placed.astype(F32).astype(BF16)
    place_ref[...] = place
    mix_ref[...] = jnp.where(placed, weight, 0.0)
    rows_ref[...] = jnp.dot(place, res_ref[...], preferred_element_type=F32)


def rest_kernel(
    n_ctx,
    back_count,
    segs_ref,
    acc_ref,
    max_ref,
    sum_ref,
    place_ref,
    queries_ref,
    rows_ref,
    *refs,
):
    kv_refs = refs[:back_count]
    out_ref, *send_refs = refs[-1 - lax.axis_size("exp") :]
    rows = queries_ref.shape[1] // GROUPS
    biases = score_bias(segs_ref, range(1, back_count + 1), n_ctx, rows)
    bias = jnp.concatenate(biases, axis=1)
    ones = jnp.ones((rows * back_count, HD), BF16)
    for kv in range(KVH):
        keys = jnp.concatenate([ref[:, kv * HD : (kv + 1) * HD] for ref in kv_refs], axis=0)
        values = jnp.concatenate(
            [ref[:, (KVH + kv) * HD : (KVH + kv + 1) * HD] for ref in kv_refs], axis=0
        )
        values = jnp.concatenate([values, ones], axis=1)
        scores = group_scores(queries_ref[kv], keys, bias)
        old_max = max_ref[kv]
        new_max = jnp.maximum(old_max, jnp.max(scores, axis=2, keepdims=True))
        accum, row_sum = weigh(jnp.exp2(scores - new_max), values)
        fix = jnp.exp2(old_max - new_max)
        total = sum_ref[kv] * fix + row_sum
        attended = ((acc_ref[kv] * fix + accum) / total).astype(BF16)
        for group in range(GROUPS):
            head = kv * GROUPS + group
            out_ref[:, head * HD : (head + 1) * HD] = attended[group]
    routed = jnp.dot(place_ref[...], out_ref[...], preferred_element_type=F32)
    wide = routed.shape[1]
    for step, ref in enumerate(send_refs):
        ref[:, :wide] = routed[step * CAP : (step + 1) * CAP, :].astype(BF16)
        ref[:, wide:] = rows_ref[step * CAP : (step + 1) * CAP, :].astype(BF16)


def stack(parts):
    return jnp.concatenate([part.astype(F32) for part in parts], axis=0).astype(BF16)


def project(total, att, starts, piece_refs):
    for start, ref in zip(starts, piece_refs):
        size = ref.shape[0]
        lead = pl.multiple_of(start(lax.axis_index("ctx"), lax.axis_index("dp"), size), size)
        total = total + jnp.dot(att(lead, size), ref[...], preferred_element_type=F32)
    return total


def arrive_kernel(owners, starts, *refs):
    row_refs, piece_refs, (att_ref, hidden_ref) = refs[:owners], refs[owners:-2], refs[-2:]
    wide = att_ref.shape[1]
    att_ref[...] = stack([ref[:, :wide] for ref in row_refs])
    hidden = jnp.concatenate([ref[:, wide:].astype(F32) for ref in row_refs], axis=0)
    hidden_ref[...] = project(
        hidden, lambda lead, size: att_ref[:, pl.ds(lead, size)], starts, piece_refs
    )


def expert_kernel(starts, gain_ref, gate_ref, up_ref, down_ref, att_ref, part_ref, *refs):
    piece_refs, out_refs = refs[: len(starts)], refs[len(starts) :]
    hidden = project(
        part_ref[...], lambda lead, size: att_ref[:, pl.ds(lead, size)], starts, piece_refs
    )
    mean = jnp.mean(hidden * hidden, axis=1, keepdims=True)
    normed = (hidden * lax.rsqrt(mean + 1e-06) * gain_ref[...]).astype(BF16)
    gate = jnp.dot(normed, gate_ref[...], preferred_element_type=F32)
    up = jnp.dot(normed, up_ref[...], preferred_element_type=F32)
    act = (gate / (1.0 + jnp.exp(-gate)) * up).astype(BF16)
    out = jnp.dot(act, down_ref[...], preferred_element_type=F32)
    for step, ref in enumerate(out_refs):
        ref[...] = out[step * CAP : (step + 1) * CAP, :].astype(BF16)


def project_kernel(starts, att_ref, res_ref, *refs):
    hidden_ref = refs[-1]
    hidden_ref[...] = project(
        res_ref[...].astype(F32),
        lambda lead, size: att_ref[:, pl.ds(lead, size)],
        starts,
        refs[:-1],
    )


def combine_kernel(owners, hidden_ref, mix_ref, *refs):
    row_refs, out_ref = refs[:owners], refs[owners]
    rows = stack([ref[...] for ref in row_refs])
    mix = mix_ref[...]
    high = mix.astype(BF16)
    low = (mix - high.astype(F32)).astype(BF16)
    total = hidden_ref[...]
    for part in (high, low):
        total = total + lax.dot_general(
            part, rows, (((0,), (0,)), ((), ())), preferred_element_type=F32
        )
    out_ref[...] = total.astype(BF16)


def call(kernel, outs, args, micros, scratch=(), limit=24, free_in=0, free_out=0):
    vmem, free = pl.BlockSpec(memory_space=pltpu.VMEM), pl.BlockSpec(memory_space=pl.ANY)
    nbytes = sum(math.prod(a.shape) * a.dtype.itemsize for a in list(args) + list(outs))
    return pl.pallas_call(
        kernel,
        out_shape=outs,
        in_specs=[vmem] * (len(args) - free_in) + [free] * free_in,
        out_specs=[vmem] * (len(outs) - free_out) + [free] * free_out,
        scratch_shapes=list(scratch),
        compiler_params=pltpu.CompilerParams(vmem_limit_bytes=limit << 20),
        cost_estimate=pl.CostEstimate(
            flops=int(micros * 1.15e9), bytes_accessed=nbytes, transcendentals=0
        ),
    )(*args)


def exchange(blocks, sign):
    count = len(blocks)
    pairs = [[(i, (i + sign * s) % count) for i in range(count)] for s in range(count)]
    return [blocks[0]] + [lax.ppermute(blocks[s], "exp", pairs[s]) for s in range(1, count)]


def gather_weight(weight, first, second, arrived, attended):
    n_ctx, cores = lax.axis_size("ctx"), lax.axis_size("dp")
    share = weight.shape[0]
    if (n_ctx, cores) != (4, 2):
        whole = lax.all_gather(weight, "ctx", axis=0, tiled=True)
        return [whole], [lambda me, core, size: 0]
    both = ("ctx", "dp")
    devices = [(me, core) for me in range(n_ctx) for core in range(cores)]
    aside = [(me * 2 + core, (me ^ (1 + core)) * 2 + core) for me, core in devices]
    across = [(me * 2 + core, (me ^ (2 - core)) * 2 + core) for me, core in devices]
    near_first = lax.ppermute(after(first, *arrived), both, aside)
    near_second = lax.ppermute(after(second, *arrived), both, aside)
    near_first = after(near_first, attended)
    far = lax.ppermute(near_first, both, across)
    (near,) = call(
        join_kernel,
        [jax.ShapeDtypeStruct(weight.shape, BF16)],
        [near_first, near_second, attended],
        micros=1,
        free_in=3,
        free_out=1,
        limit=1,
        scratch=[pltpu.SemaphoreType.DMA((2,))],
    )
    swap = [(0, 1), (1, 0)]
    pieces = [weight, near, far, lax.ppermute(near, "dp", swap), lax.ppermute(far, "dp", swap)]
    starts = [
        lambda me, core, size: me * share,
        lambda me, core, size: (me ^ (1 + core)) * share,
        lambda me, core, size: (me ^ 3) * share + core * size,
        lambda me, core, size: (me ^ (2 - core)) * share,
        lambda me, core, size: (me ^ 3) * share + (1 - core) * size,
    ]
    return pieces, starts


def per_device(
    queries,
    keys,
    values,
    segments,
    residual,
    out_weight,
    gain,
    expert_ids,
    route_weights,
    w_gate,
    w_up,
    w_down,
):
    tok_rows = queries.shape[1]
    width = residual.shape[2]
    att_width = queries.shape[2]
    n_ctx, owners = lax.axis_size("ctx"), lax.axis_size("exp")
    slots = owners * CAP
    longest = segments.shape[1] // 2
    back_count = min(n_ctx - 1, -(-(longest - 1) // tok_rows))
    shape = jax.ShapeDtypeStruct

    own_kv = jnp.concatenate([keys[0], values[0]], axis=1)
    kv_blocks = []
    for back in range(1, back_count + 1):
        pairs = [(i, (i + back) % n_ctx) for i in range(n_ctx)]
        kv_blocks.append(lax.ppermute(own_kv, "ctx", pairs))
    half = shape((out_weight.shape[0] // 2, width), BF16)
    accum, row_max, row_sum, stacked, first, second = call(
        functools.partial(own_kernel, n_ctx),
        [
            shape((KVH, GROUPS, tok_rows, HD), F32),
            shape((KVH, GROUPS, tok_rows, 1), F32),
            shape((KVH, GROUPS, tok_rows, 1), F32),
            shape((KVH, GROUPS * tok_rows, HD), BF16),
            half,
            half,
        ],
        [queries[0], own_kv, segments, out_weight],
        micros=3,
        free_in=1,
        free_out=2,
        scratch=[pltpu.SemaphoreType.DMA((2,))],
    )
    place, mix, res_rows = call(
        route_kernel,
        [
            shape((slots, tok_rows), BF16),
            shape((slots, tok_rows), F32),
            shape((slots, width), F32),
        ],
        [expert_ids[0].T, route_weights[0].T, residual[0]],
        micros=1,
    )
    attended, *routed = call(
        functools.partial(rest_kernel, n_ctx, back_count),
        [shape((tok_rows, att_width), BF16)]
        + [shape((CAP, att_width + width), BF16)] * owners,
        [segments, accum, row_max, row_sum, place, stacked, res_rows, *kv_blocks],
        micros=5,
    )
    pieces, starts = gather_weight(out_weight, first, second, kv_blocks, attended)
    early = min(2, len(pieces))
    arrived, part = call(
        functools.partial(arrive_kernel, owners, starts[:early]),
        [shape((slots, att_width), BF16), shape((slots, width), F32)],
        [*exchange(routed, 1), *pieces[:early]],
        micros=10,
    )
    done = call(
        functools.partial(expert_kernel, starts[early:]),
        [shape((CAP, width), BF16)] * owners,
        [gain[None, :], w_gate[0], w_up[0], w_down[0], arrived, part, *pieces[early:]],
        micros=2,
    )
    back = exchange(done, -1)
    (hidden,) = call(
        functools.partial(project_kernel, starts),
        [shape((tok_rows, width), F32)],
        [attended, residual[0], *pieces],
        micros=2,
    )
    (out,) = call(
        functools.partial(combine_kernel, owners),
        [shape((tok_rows, width), BF16)],
        [hidden, mix, *back],
        micros=1,
    )
    return out[None]


def solution(mesh):
    return jax.shard_map(
        per_device,
        mesh=mesh,
        in_specs=(
            P(("dp", "exp"), "ctx", None),
            P(("dp", "exp"), "ctx", None),
            P(("dp", "exp"), "ctx", None),
            P(("dp", "exp"), None),
            P(("dp", "exp"), "ctx", None),
            P("ctx", None),
            P(),
            P(("dp", "exp"), "ctx", None),
            P(("dp", "exp"), "ctx", None),
            P("exp", None, None),
            P("exp", None, None),
            P("exp", None, None),
        ),
        out_specs=P(("dp", "exp"), "ctx", None),
        check_vma=False,
    )
```

```python
import functools
import math

import jax
import jax.numpy as jnp
from jax import lax
from jax.experimental import pallas as pl
from jax.experimental.pallas import tpu as pltpu
from jax.sharding import PartitionSpec as P

HQ = 16
KVH = 2
HD = 128
GROUPS = HQ // KVH
CAP = 24
NEG = -1e30
SCORE_SCALE = math.log2(math.e) / math.sqrt(HD)
F32 = jnp.float32
BF16 = jnp.bfloat16


def slab_segments(segs_ref, index, count, rows):
    found = segs_ref[:, 0:rows]
    for slab in range(1, count):
        found = jnp.where(index == slab, segs_ref[:, slab * rows : (slab + 1) * rows], found)
    return found


def score_bias(segs_ref, backs, count, rows):
    me = lax.axis_index("ctx")
    row = lax.broadcasted_iota(jnp.int32, (rows, rows), 0)
    col = lax.broadcasted_iota(jnp.int32, (rows, rows), 1)
    own_seg = slab_segments(segs_ref, me, count, rows)
    query_seg = jnp.sum(jnp.where(row == col, own_seg, 0), axis=1, keepdims=True)
    parts = []
    for back in backs:
        if back == 0:
            allowed = (col <= row) & (own_seg == query_seg)
        else:
            key_seg = slab_segments(segs_ref, jnp.maximum(me - back, 0), count, rows)
            allowed = (key_seg == query_seg) & (me >= back)
        parts.append(jnp.where(allowed, 0.0, NEG))
    return parts


def group_scores(stacked, keys, bias):
    scores = lax.dot_general(
        stacked, keys, (((1,), (1,)), ((), ())), preferred_element_type=F32
    )
    return scores.reshape(GROUPS, *bias.shape) * SCORE_SCALE + bias


def weigh(expo, values):
    rows = expo.shape[0] * expo.shape[1]
    mixed = jnp.dot(
        expo.astype(BF16).reshape(rows, expo.shape[2]), values, preferred_element_type=F32
    ).reshape(*expo.shape[:2], 2 * HD)
    return mixed[:, :, :HD], mixed[:, :, HD : HD + 1]


def gate_kernel(*refs):
    del refs


def after(piece, *marks):
    spec = pl.BlockSpec(memory_space=pl.ANY)
    return pl.pallas_call(
        gate_kernel,
        out_shape=jax.ShapeDtypeStruct(piece.shape, piece.dtype),
        in_specs=[spec] * (1 + len(marks)),
        out_specs=spec,
        input_output_aliases={0: 0},
        compiler_params=pltpu.CompilerParams(vmem_limit_bytes=1 << 20),
    )(piece, *marks)


def join_kernel(first_ref, second_ref, mark_ref, whole_ref, sems):
    del mark_ref
    half = first_ref.shape[0]
    core = lax.rem(lax.axis_index("dp"), 2)
    copies = []
    for index, (lead, ref) in enumerate([(core, first_ref), (1 - core, second_ref)]):
        target = whole_ref.at[pl.ds(pl.multiple_of(lead * half, half), half)]
        copies.append(pltpu.make_async_copy(ref, target, sems.at[index]))
        copies[-1].start()
    for copy in copies:
        copy.wait()


def own_kernel(
    n_ctx,
    q_ref,
    kv_ref,
    segs_ref,
    w_ref,
    acc_ref,
    max_ref,
    sum_ref,
    queries_ref,
    first_ref,
    second_ref,
    sems,
):
    half = first_ref.shape[0]
    core = lax.rem(lax.axis_index("dp"), 2)
    copies = []
    for index, (lead, ref) in enumerate([(core, first_ref), (1 - core, second_ref)]):
        source = w_ref.at[pl.ds(pl.multiple_of(lead * half, half), half)]
        copies.append(pltpu.make_async_copy(source, ref, sems.at[index]))
        copies[-1].start()
    rows = q_ref.shape[0]
    (bias,) = score_bias(segs_ref, (0,), n_ctx, rows)
    ones = jnp.ones((rows, HD), BF16)
    for kv in range(KVH):
        keys = kv_ref[:, kv * HD : (kv + 1) * HD]
        values = jnp.concatenate([kv_ref[:, (KVH + kv) * HD : (KVH + kv + 1) * HD], ones], axis=1)
        heads = range(kv * GROUPS, (kv + 1) * GROUPS)
        stacked = jnp.concatenate([q_ref[:, h * HD : (h + 1) * HD] for h in heads], axis=0)
        queries_ref[kv] = stacked
        scores = group_scores(stacked, keys, bias)
        row_max = jnp.max(scores, axis=2, keepdims=True)
        accum, row_sum = weigh(jnp.exp2(scores - row_max), values)
        acc_ref[kv] = accum
        max_ref[kv] = row_max
        sum_ref[kv] = row_sum
    for copy in copies:
        copy.wait()


def route_kernel(ids_ref, rw_ref, res_ref, place_ref, mix_ref, rows_ref):
    slots, rows = mix_ref.shape
    slot = lax.broadcasted_iota(jnp.int32, (slots, rows), 0)
    owner = lax.rem(slot // CAP + lax.axis_index("exp"), slots // CAP)
    hit = jnp.zeros((slots, rows), jnp.bool_)
    weight = jnp.zeros((slots, rows), F32)
    for choice in range(ids_ref.shape[0]):
        same = ids_ref[choice : choice + 1, :] == owner
        hit = hit | same
        weight = jnp.where(same, rw_ref[choice : choice + 1, :], weight)
    row = lax.broadcasted_iota(jnp.int32, (rows, rows), 0)
    col = lax.broadcasted_iota(jnp.int32, (rows, rows), 1)
    before = (row < col).astype(F32).astype(BF16)
    rank = jnp.dot(hit.astype(F32).astype(BF16), before, preferred_element_type=F32)
    placed = hit & (rank == lax.rem(slot, CAP).astype(F32))
    place = placed.astype(F32).astype(BF16)
    place_ref[...] = place
    mix_ref[...] = jnp.where(placed, weight, 0.0)
    rows_ref[...] = jnp.dot(place, res_ref[...], preferred_element_type=F32)


def rest_kernel(
    n_ctx,
    back_count,
    segs_ref,
    acc_ref,
    max_ref,
    sum_ref,
    place_ref,
    queries_ref,
    rows_ref,
    w_ref,
    *refs,
):
    kv_refs = refs[:back_count]
    out_ref, *send_refs = refs[back_count:-1]
    routed_ref = refs[-1]
    rows = queries_ref.shape[1] // GROUPS
    biases = score_bias(segs_ref, range(1, back_count + 1), n_ctx, rows)
    bias = jnp.concatenate(biases, axis=1)
    ones = jnp.ones((rows * back_count, HD), BF16)
    for kv in range(KVH):
        keys = jnp.concatenate([ref[:, kv * HD : (kv + 1) * HD] for ref in kv_refs], axis=0)
        values = jnp.concatenate(
            [ref[:, (KVH + kv) * HD : (KVH + kv + 1) * HD] for ref in kv_refs], axis=0
        )
        values = jnp.concatenate([values, ones], axis=1)
        scores = group_scores(queries_ref[kv], keys, bias)
        old_max = max_ref[kv]
        new_max = jnp.maximum(old_max, jnp.max(scores, axis=2, keepdims=True))
        accum, row_sum = weigh(jnp.exp2(scores - new_max), values)
        fix = jnp.exp2(old_max - new_max)
        total = sum_ref[kv] * fix + row_sum
        attended = ((acc_ref[kv] * fix + accum) / total).astype(BF16)
        for group in range(GROUPS):
            head = kv * GROUPS + group
            out_ref[:, head * HD : (head + 1) * HD] = attended[group]
    routed_ref[...] = jnp.dot(place_ref[...], out_ref[...], preferred_element_type=F32)
    me, share = lax.axis_index("ctx"), w_ref.shape[0]

    def quarter(flip):
        return routed_ref[:, pl.ds(pl.multiple_of((me ^ flip) * share, share), share)]

    part = rows_ref[...] + jnp.dot(
        quarter(0).astype(BF16), w_ref[...], preferred_element_type=F32
    )
    blocks = [quarter(flip) for flip in range(1, n_ctx)] + [part]
    for step, ref in enumerate(send_refs):
        for place, block in enumerate(blocks):
            ref[:, place * share : place * share + block.shape[1]] = block[
                step * CAP : (step + 1) * CAP, :
            ].astype(BF16)


def stack(parts):
    return jnp.concatenate([part.astype(F32) for part in parts], axis=0).astype(BF16)


def project(total, att_ref, entries, piece_refs, moved):
    me, core = lax.axis_index("ctx"), lax.axis_index("dp")
    share = att_ref.shape[1] // (lax.axis_size("ctx") - moved)
    for piece, size, flip, offset, row in entries:
        quarter = flip(core) - 1 if moved else me ^ flip(core)
        lead = pl.multiple_of(quarter * share + offset(core), size)
        rows = pl.ds(pl.multiple_of(row(me), size), size)
        total = total + jnp.dot(
            att_ref[:, pl.ds(lead, size)], piece_refs[piece][rows, :], preferred_element_type=F32
        )
    return total


def arrive_kernel(owners, entries, *refs):
    row_refs, piece_refs, (att_ref, hidden_ref) = refs[:owners], refs[owners:-2], refs[-2:]
    wide = att_ref.shape[1]
    att_ref[...] = stack([ref[:, :wide] for ref in row_refs])
    hidden = jnp.concatenate([ref[:, wide:].astype(F32) for ref in row_refs], axis=0)
    hidden_ref[...] = project(hidden, att_ref, entries, piece_refs, True)


def expert_kernel(entries, count, gain_ref, gate_ref, up_ref, down_ref, att_ref, part_ref, *refs):
    piece_refs, out_refs = refs[:count], refs[count:]
    hidden = project(part_ref[...], att_ref, entries, piece_refs, True)
    mean = jnp.mean(hidden * hidden, axis=1, keepdims=True)
    normed = (hidden * lax.rsqrt(mean + 1e-06) * gain_ref[...]).astype(BF16)
    gate = jnp.dot(normed, gate_ref[...], preferred_element_type=F32)
    up = jnp.dot(normed, up_ref[...], preferred_element_type=F32)
    act = (gate / (1.0 + jnp.exp(-gate)) * up).astype(BF16)
    out = jnp.dot(act, down_ref[...], preferred_element_type=F32)
    for step, ref in enumerate(out_refs):
        ref[...] = out[step * CAP : (step + 1) * CAP, :].astype(BF16)


def project_kernel(entries, att_ref, res_ref, *refs):
    hidden = res_ref[...].astype(F32)
    refs[-1][...] = project(hidden, att_ref, entries, refs[:-1], False)


def combine_kernel(owners, hidden_ref, mix_ref, *refs):
    row_refs, out_ref = refs[:owners], refs[owners]
    rows = stack([ref[...] for ref in row_refs])
    mix = mix_ref[...]
    high = mix.astype(BF16)
    low = (mix - high.astype(F32)).astype(BF16)
    total = hidden_ref[...]
    for part in (high, low):
        total = total + lax.dot_general(
            part, rows, (((0,), (0,)), ((), ())), preferred_element_type=F32
        )
    out_ref[...] = total.astype(BF16)


def call(kernel, outs, args, micros, scratch=(), limit=24, free_in=0, free_out=0):
    vmem, free = pl.BlockSpec(memory_space=pltpu.VMEM), pl.BlockSpec(memory_space=pl.ANY)
    nbytes = sum(math.prod(a.shape) * a.dtype.itemsize for a in list(args) + list(outs))
    return pl.pallas_call(
        kernel,
        out_shape=outs,
        in_specs=[vmem] * (len(args) - free_in) + [free] * free_in,
        out_specs=[vmem] * (len(outs) - free_out) + [free] * free_out,
        scratch_shapes=list(scratch),
        compiler_params=pltpu.CompilerParams(vmem_limit_bytes=limit << 20),
        cost_estimate=pl.CostEstimate(
            flops=int(micros * 1.15e9), bytes_accessed=nbytes, transcendentals=0
        ),
    )(*args)


def exchange(blocks, sign):
    count = len(blocks)
    pairs = [[(i, (i + sign * s) % count) for i in range(count)] for s in range(count)]
    return [blocks[0]] + [lax.ppermute(blocks[s], "exp", pairs[s]) for s in range(1, count)]


def gather_weight(weight, first, second, arrived, attended):
    n_ctx, cores = lax.axis_size("ctx"), lax.axis_size("dp")
    share = weight.shape[0]
    if (n_ctx, cores) != (4, 2):
        whole = lax.all_gather(weight, "ctx", axis=0, tiled=True)
        entries = [
            (0, share, lambda core, f=f: f, lambda core: 0, lambda me, f=f: (me ^ f) * share)
            for f in range(n_ctx)
        ]
        return [whole], entries
    both = ("ctx", "dp")
    devices = [(me, core) for me in range(n_ctx) for core in range(cores)]
    aside = [(me * 2 + core, (me ^ (1 + core)) * 2 + core) for me, core in devices]
    across = [(me * 2 + core, (me ^ (2 - core)) * 2 + core) for me, core in devices]
    near_first = lax.ppermute(after(first, arrived[-1]), both, aside)
    near_second = lax.ppermute(after(second, *arrived), both, aside)
    near_first = after(near_first, attended)
    far = lax.ppermute(near_first, both, across)
    (near,) = call(
        join_kernel,
        [jax.ShapeDtypeStruct(weight.shape, BF16)],
        [near_first, near_second, attended],
        micros=1,
        free_in=3,
        free_out=1,
        limit=1,
        scratch=[pltpu.SemaphoreType.DMA((2,))],
    )
    swap = [(0, 1), (1, 0)]
    pieces = [weight, near, far, lax.ppermute(near, "dp", swap), lax.ppermute(far, "dp", swap)]
    half = share // 2
    first_row = lambda me: 0
    entries = [
        (0, share, lambda core: 0, lambda core: 0, first_row),
        (1, share, lambda core: 1 + core, lambda core: 0, first_row),
        (2, half, lambda core: 3, lambda core: core * half, first_row),
        (3, share, lambda core: 2 - core, lambda core: 0, first_row),
        (4, half, lambda core: 3, lambda core: (1 - core) * half, first_row),
    ]
    return pieces, entries


def per_device(
    queries,
    keys,
    values,
    segments,
    residual,
    out_weight,
    gain,
    expert_ids,
    route_weights,
    w_gate,
    w_up,
    w_down,
):
    tok_rows = queries.shape[1]
    width = residual.shape[2]
    att_width = queries.shape[2]
    n_ctx, owners = lax.axis_size("ctx"), lax.axis_size("exp")
    slots = owners * CAP
    moved_width = att_width - out_weight.shape[0]
    longest = segments.shape[1] // 2
    back_count = min(n_ctx - 1, -(-(longest - 1) // tok_rows))
    shape = jax.ShapeDtypeStruct

    own_kv = jnp.concatenate([keys[0], values[0]], axis=1)
    kv_blocks = []
    for back in range(1, back_count + 1):
        pairs = [(i, (i + back) % n_ctx) for i in range(n_ctx)]
        kv_blocks.append(lax.ppermute(own_kv, "ctx", pairs))
    half = shape((out_weight.shape[0] // 2, width), BF16)
    accum, row_max, row_sum, stacked, first, second = call(
        functools.partial(own_kernel, n_ctx),
        [
            shape((KVH, GROUPS, tok_rows, HD), F32),
            shape((KVH, GROUPS, tok_rows, 1), F32),
            shape((KVH, GROUPS, tok_rows, 1), F32),
            shape((KVH, GROUPS * tok_rows, HD), BF16),
            half,
            half,
        ],
        [queries[0], own_kv, segments, out_weight],
        micros=3,
        free_in=1,
        free_out=2,
        scratch=[pltpu.SemaphoreType.DMA((2,))],
    )
    place, mix, res_rows = call(
        route_kernel,
        [
            shape((slots, tok_rows), BF16),
            shape((slots, tok_rows), F32),
            shape((slots, width), F32),
        ],
        [expert_ids[0].T, route_weights[0].T, residual[0]],
        micros=1,
    )
    attended, *routed = call(
        functools.partial(rest_kernel, n_ctx, back_count),
        [shape((tok_rows, att_width), BF16)]
        + [shape((CAP, moved_width + width), BF16)] * owners,
        [segments, accum, row_max, row_sum, place, stacked, res_rows, out_weight, *kv_blocks],
        micros=5,
        scratch=[pltpu.VMEM((slots, att_width), F32)],
    )
    pieces, entries = gather_weight(out_weight, first, second, kv_blocks, attended)
    early = pieces[1:2]
    late = pieces[2:] or pieces
    now = [(0, *entry[1:]) for entry in entries[1:] if early and entry[0] == 1]
    skipped = len(pieces) - len(late)
    then = [(entry[0] - skipped, *entry[1:]) for entry in entries[1:] if entry[0] >= skipped]
    arrived, part = call(
        functools.partial(arrive_kernel, owners, now),
        [shape((slots, moved_width), BF16), shape((slots, width), F32)],
        [*exchange(routed, 1), *early],
        micros=10,
    )
    done = call(
        functools.partial(expert_kernel, then, len(late)),
        [shape((CAP, width), BF16)] * owners,
        [gain[None, :], w_gate[0], w_up[0], w_down[0], arrived, part, *late],
        micros=2,
    )
    back = exchange(done, -1)
    (hidden,) = call(
        functools.partial(project_kernel, entries),
        [shape((tok_rows, width), F32)],
        [attended, residual[0], *pieces],
        micros=2,
    )
    (out,) = call(
        functools.partial(combine_kernel, owners),
        [shape((tok_rows, width), BF16)],
        [hidden, mix, *back],
        micros=1,
    )
    return out[None]


def solution(mesh):
    return jax.shard_map(
        per_device,
        mesh=mesh,
        in_specs=(
            P(("dp", "exp"), "ctx", None),
            P(("dp", "exp"), "ctx", None),
            P(("dp", "exp"), "ctx", None),
            P(("dp", "exp"), None),
            P(("dp", "exp"), "ctx", None),
            P("ctx", None),
            P(),
            P(("dp", "exp"), "ctx", None),
            P(("dp", "exp"), "ctx", None),
            P("exp", None, None),
            P("exp", None, None),
            P("exp", None, None),
        ),
        out_specs=P(("dp", "exp"), "ctx", None),
        check_vma=False,
    )
```

```python
import functools
import math

import jax
import jax.numpy as jnp
from jax import lax
from jax.experimental import pallas as pl
from jax.experimental.pallas import tpu as pltpu
from jax.sharding import PartitionSpec as P

HQ = 16
KVH = 2
HD = 128
GROUPS = HQ // KVH
CAP = 24
NEG = -1e30
SCORE_SCALE = math.log2(math.e) / math.sqrt(HD)
F32 = jnp.float32
BF16 = jnp.bfloat16


def slab_segments(segs_ref, index, count, rows):
    found = segs_ref[:, 0:rows]
    for slab in range(1, count):
        found = jnp.where(index == slab, segs_ref[:, slab * rows : (slab + 1) * rows], found)
    return found


def score_bias(segs_ref, backs, count, rows):
    me = lax.axis_index("ctx")
    row = lax.broadcasted_iota(jnp.int32, (rows, rows), 0)
    col = lax.broadcasted_iota(jnp.int32, (rows, rows), 1)
    own_seg = slab_segments(segs_ref, me, count, rows)
    query_seg = jnp.sum(jnp.where(row == col, own_seg, 0), axis=1, keepdims=True)
    parts = []
    for back in backs:
        if back == 0:
            allowed = (col <= row) & (own_seg == query_seg)
        else:
            key_seg = slab_segments(segs_ref, jnp.maximum(me - back, 0), count, rows)
            allowed = (key_seg == query_seg) & (me >= back)
        parts.append(jnp.where(allowed, 0.0, NEG))
    return parts


def group_scores(stacked, keys, bias):
    scores = lax.dot_general(
        stacked, keys, (((1,), (1,)), ((), ())), preferred_element_type=F32
    )
    return scores.reshape(GROUPS, *bias.shape) * SCORE_SCALE + bias


def weigh(expo, values):
    rows = expo.shape[0] * expo.shape[1]
    mixed = jnp.dot(
        expo.astype(BF16).reshape(rows, expo.shape[2]), values, preferred_element_type=F32
    ).reshape(*expo.shape[:2], 2 * HD)
    return mixed[:, :, :HD], mixed[:, :, HD : HD + 1]


def gate_kernel(*refs):
    del refs


def after(piece, *marks):
    spec = pl.BlockSpec(memory_space=pl.ANY)
    return pl.pallas_call(
        gate_kernel,
        out_shape=jax.ShapeDtypeStruct(piece.shape, piece.dtype),
        in_specs=[spec] * (1 + len(marks)),
        out_specs=spec,
        input_output_aliases={0: 0},
        compiler_params=pltpu.CompilerParams(vmem_limit_bytes=1 << 20),
    )(piece, *marks)


def join_kernel(first_ref, second_ref, mark_ref, whole_ref, sems):
    del mark_ref
    half = first_ref.shape[0]
    core = lax.rem(lax.axis_index("dp"), 2)
    copies = []
    for index, (lead, ref) in enumerate([(core, first_ref), (1 - core, second_ref)]):
        target = whole_ref.at[pl.ds(pl.multiple_of(lead * half, half), half)]
        copies.append(pltpu.make_async_copy(ref, target, sems.at[index]))
        copies[-1].start()
    for copy in copies:
        copy.wait()


def own_kernel(
    n_ctx,
    q_ref,
    kv_ref,
    segs_ref,
    w_ref,
    acc_ref,
    max_ref,
    sum_ref,
    queries_ref,
    first_ref,
    second_ref,
    sems,
):
    half = first_ref.shape[0]
    core = lax.rem(lax.axis_index("dp"), 2)
    copies = []
    for index, (lead, ref) in enumerate([(core, first_ref), (1 - core, second_ref)]):
        source = w_ref.at[pl.ds(pl.multiple_of(lead * half, half), half)]
        copies.append(pltpu.make_async_copy(source, ref, sems.at[index]))
        copies[-1].start()
    rows = q_ref.shape[0]
    (bias,) = score_bias(segs_ref, (0,), n_ctx, rows)
    ones = jnp.ones((rows, HD), BF16)
    for kv in range(KVH):
        keys = kv_ref[:, kv * HD : (kv + 1) * HD]
        values = jnp.concatenate([kv_ref[:, (KVH + kv) * HD : (KVH + kv + 1) * HD], ones], axis=1)
        heads = range(kv * GROUPS, (kv + 1) * GROUPS)
        stacked = jnp.concatenate([q_ref[:, h * HD : (h + 1) * HD] for h in heads], axis=0)
        queries_ref[kv] = stacked
        scores = group_scores(stacked, keys, bias)
        row_max = jnp.max(scores, axis=2, keepdims=True)
        accum, row_sum = weigh(jnp.exp2(scores - row_max), values)
        acc_ref[kv] = accum
        max_ref[kv] = row_max
        sum_ref[kv] = row_sum
    for copy in copies:
        copy.wait()


def route_kernel(ids_ref, rw_ref, res_ref, place_ref, mix_ref, rows_ref):
    slots, rows = mix_ref.shape
    slot = lax.broadcasted_iota(jnp.int32, (slots, rows), 0)
    owner = lax.rem(slot // CAP + lax.axis_index("exp"), slots // CAP)
    hit = jnp.zeros((slots, rows), jnp.bool_)
    weight = jnp.zeros((slots, rows), F32)
    for choice in range(ids_ref.shape[0]):
        same = ids_ref[choice : choice + 1, :] == owner
        hit = hit | same
        weight = jnp.where(same, rw_ref[choice : choice + 1, :], weight)
    row = lax.broadcasted_iota(jnp.int32, (rows, rows), 0)
    col = lax.broadcasted_iota(jnp.int32, (rows, rows), 1)
    before = (row < col).astype(F32).astype(BF16)
    rank = jnp.dot(hit.astype(F32).astype(BF16), before, preferred_element_type=F32)
    placed = hit & (rank == lax.rem(slot, CAP).astype(F32))
    place = placed.astype(F32).astype(BF16)
    place_ref[...] = place
    mix_ref[...] = jnp.where(placed, weight, 0.0)
    rows_ref[...] = jnp.dot(place, res_ref[...], preferred_element_type=F32)


def rest_kernel(
    n_ctx,
    back_count,
    segs_ref,
    acc_ref,
    max_ref,
    sum_ref,
    place_ref,
    queries_ref,
    rows_ref,
    w_ref,
    *refs,
):
    kv_refs = refs[:back_count]
    out_ref, *send_refs = refs[back_count:-1]
    routed_ref = refs[-1]
    rows = queries_ref.shape[1] // GROUPS
    biases = score_bias(segs_ref, range(1, back_count + 1), n_ctx, rows)
    bias = jnp.concatenate(biases, axis=1)
    ones = jnp.ones((rows * back_count, HD), BF16)
    for kv in range(KVH):
        keys = jnp.concatenate([ref[:, kv * HD : (kv + 1) * HD] for ref in kv_refs], axis=0)
        values = jnp.concatenate(
            [ref[:, (KVH + kv) * HD : (KVH + kv + 1) * HD] for ref in kv_refs], axis=0
        )
        values = jnp.concatenate([values, ones], axis=1)
        scores = group_scores(queries_ref[kv], keys, bias)
        old_max = max_ref[kv]
        new_max = jnp.maximum(old_max, jnp.max(scores, axis=2, keepdims=True))
        accum, row_sum = weigh(jnp.exp2(scores - new_max), values)
        fix = jnp.exp2(old_max - new_max)
        total = sum_ref[kv] * fix + row_sum
        attended = ((acc_ref[kv] * fix + accum) / total).astype(BF16)
        for group in range(GROUPS):
            head = kv * GROUPS + group
            out_ref[:, head * HD : (head + 1) * HD] = attended[group]
    routed_ref[...] = jnp.dot(place_ref[...], out_ref[...], preferred_element_type=F32)
    me, share = lax.axis_index("ctx"), w_ref.shape[0]

    def quarter(flip):
        return routed_ref[:, pl.ds(pl.multiple_of((me ^ flip) * share, share), share)]

    part = rows_ref[...] + jnp.dot(
        quarter(0).astype(BF16), w_ref[...], preferred_element_type=F32
    )
    blocks = [quarter(flip) for flip in range(1, n_ctx)] + [part]
    for step, ref in enumerate(send_refs):
        for place, block in enumerate(blocks):
            ref[:, place * share : place * share + block.shape[1]] = block[
                step * CAP : (step + 1) * CAP, :
            ].astype(BF16)


def stack(parts):
    return jnp.concatenate([part.astype(F32) for part in parts], axis=0).astype(BF16)


def project(total, att_ref, entries, piece_refs, moved):
    me, core = lax.axis_index("ctx"), lax.axis_index("dp")
    share = att_ref.shape[1] // (lax.axis_size("ctx") - moved)
    for piece, size, flip, offset, row in entries:
        quarter = flip(core) - 1 if moved else me ^ flip(core)
        lead = pl.multiple_of(quarter * share + offset(core), size)
        rows = pl.ds(pl.multiple_of(row(me), size), size)
        total = total + jnp.dot(
            att_ref[:, pl.ds(lead, size)], piece_refs[piece][rows, :], preferred_element_type=F32
        )
    return total


def arrive_kernel(owners, entries, *refs):
    row_refs, piece_refs, (att_ref, hidden_ref) = refs[:owners], refs[owners:-2], refs[-2:]
    wide = att_ref.shape[1]
    att_ref[...] = stack([ref[:, :wide] for ref in row_refs])
    hidden = jnp.concatenate([ref[:, wide:].astype(F32) for ref in row_refs], axis=0)
    hidden_ref[...] = project(hidden, att_ref, entries, piece_refs, True)


def expert_kernel(entries, count, gain_ref, gate_ref, up_ref, down_ref, att_ref, part_ref, *refs):
    piece_refs, out_refs = refs[:count], refs[count:]
    hidden = project(part_ref[...], att_ref, entries, piece_refs, True)
    mean = jnp.mean(hidden * hidden, axis=1, keepdims=True)
    normed = (hidden * lax.rsqrt(mean + 1e-06) * gain_ref[...]).astype(BF16)
    gate = jnp.dot(normed, gate_ref[...], preferred_element_type=F32)
    up = jnp.dot(normed, up_ref[...], preferred_element_type=F32)
    act = (gate / (1.0 + jnp.exp(-gate)) * up).astype(BF16)
    out = jnp.dot(act, down_ref[...], preferred_element_type=F32)
    for step, ref in enumerate(out_refs):
        ref[...] = out[step * CAP : (step + 1) * CAP, :].astype(BF16)


def project_kernel(entries, att_ref, res_ref, *refs):
    hidden = res_ref[...].astype(F32)
    refs[-1][...] = project(hidden, att_ref, entries, refs[:-1], False)


def combine_kernel(owners, hidden_ref, mix_ref, *refs):
    row_refs, out_ref = refs[:owners], refs[owners]
    rows = stack([ref[...] for ref in row_refs])
    mix = mix_ref[...]
    high = mix.astype(BF16)
    low = (mix - high.astype(F32)).astype(BF16)
    total = hidden_ref[...]
    for part in (high, low):
        total = total + lax.dot_general(
            part, rows, (((0,), (0,)), ((), ())), preferred_element_type=F32
        )
    out_ref[...] = total.astype(BF16)


def call(kernel, outs, args, micros, scratch=(), limit=24, free_in=0, free_out=0):
    vmem, free = pl.BlockSpec(memory_space=pltpu.VMEM), pl.BlockSpec(memory_space=pl.ANY)
    nbytes = sum(math.prod(a.shape) * a.dtype.itemsize for a in list(args) + list(outs))
    return pl.pallas_call(
        kernel,
        out_shape=outs,
        in_specs=[vmem] * (len(args) - free_in) + [free] * free_in,
        out_specs=[vmem] * (len(outs) - free_out) + [free] * free_out,
        scratch_shapes=list(scratch),
        compiler_params=pltpu.CompilerParams(vmem_limit_bytes=limit << 20),
        cost_estimate=pl.CostEstimate(
            flops=int(micros * 1.15e9), bytes_accessed=nbytes, transcendentals=0
        ),
    )(*args)


def exchange(blocks, sign):
    count = len(blocks)
    pairs = [[(i, (i + sign * s) % count) for i in range(count)] for s in range(count)]
    return [blocks[0]] + [lax.ppermute(blocks[s], "exp", pairs[s]) for s in range(1, count)]


def gather_weight(weight, first, second, arrived, attended):
    n_ctx, cores = lax.axis_size("ctx"), lax.axis_size("dp")
    share = weight.shape[0]
    if (n_ctx, cores) != (4, 2):
        whole = lax.all_gather(weight, "ctx", axis=0, tiled=True)
        entries = [
            (0, share, lambda core, f=f: f, lambda core: 0, lambda me, f=f: (me ^ f) * share)
            for f in range(n_ctx)
        ]
        return [whole], entries
    both = ("ctx", "dp")
    devices = [(me, core) for me in range(n_ctx) for core in range(cores)]
    aside = [(me * 2 + core, (me ^ (1 + core)) * 2 + core) for me, core in devices]
    across = [(me * 2 + core, (me ^ (2 - core)) * 2 + core) for me, core in devices]
    near_first = lax.ppermute(first, both, aside)
    near_second = lax.ppermute(after(second, *arrived), both, aside)
    near_first = after(near_first, attended)
    far = lax.ppermute(near_first, both, across)
    (near,) = call(
        join_kernel,
        [jax.ShapeDtypeStruct(weight.shape, BF16)],
        [near_first, near_second, attended],
        micros=1,
        free_in=3,
        free_out=1,
        limit=1,
        scratch=[pltpu.SemaphoreType.DMA((2,))],
    )
    swap = [(0, 1), (1, 0)]
    pieces = [weight, near, far, lax.ppermute(near, "dp", swap), lax.ppermute(far, "dp", swap)]
    half = share // 2
    first_row = lambda me: 0
    entries = [
        (0, share, lambda core: 0, lambda core: 0, first_row),
        (1, share, lambda core: 1 + core, lambda core: 0, first_row),
        (2, half, lambda core: 3, lambda core: core * half, first_row),
        (3, share, lambda core: 2 - core, lambda core: 0, first_row),
        (4, half, lambda core: 3, lambda core: (1 - core) * half, first_row),
    ]
    return pieces, entries


def per_device(
    queries,
    keys,
    values,
    segments,
    residual,
    out_weight,
    gain,
    expert_ids,
    route_weights,
    w_gate,
    w_up,
    w_down,
):
    tok_rows = queries.shape[1]
    width = residual.shape[2]
    att_width = queries.shape[2]
    n_ctx, owners = lax.axis_size("ctx"), lax.axis_size("exp")
    slots = owners * CAP
    moved_width = att_width - out_weight.shape[0]
    longest = segments.shape[1] // 2
    back_count = min(n_ctx - 1, -(-(longest - 1) // tok_rows))
    shape = jax.ShapeDtypeStruct

    own_kv = jnp.concatenate([keys[0], values[0]], axis=1)
    kv_blocks = []
    for back in range(1, back_count + 1):
        pairs = [(i, (i + back) % n_ctx) for i in range(n_ctx)]
        kv_blocks.append(lax.ppermute(own_kv, "ctx", pairs))
    half = shape((out_weight.shape[0] // 2, width), BF16)
    accum, row_max, row_sum, stacked, first, second = call(
        functools.partial(own_kernel, n_ctx),
        [
            shape((KVH, GROUPS, tok_rows, HD), F32),
            shape((KVH, GROUPS, tok_rows, 1), F32),
            shape((KVH, GROUPS, tok_rows, 1), F32),
            shape((KVH, GROUPS * tok_rows, HD), BF16),
            half,
            half,
        ],
        [queries[0], own_kv, segments, out_weight],
        micros=3,
        free_in=1,
        free_out=2,
        scratch=[pltpu.SemaphoreType.DMA((2,))],
    )
    place, mix, res_rows = call(
        route_kernel,
        [
            shape((slots, tok_rows), BF16),
            shape((slots, tok_rows), F32),
            shape((slots, width), F32),
        ],
        [expert_ids[0].T, route_weights[0].T, residual[0]],
        micros=1,
    )
    attended, *routed = call(
        functools.partial(rest_kernel, n_ctx, back_count),
        [shape((tok_rows, att_width), BF16)]
        + [shape((CAP, moved_width + width), BF16)] * owners,
        [segments, accum, row_max, row_sum, place, stacked, res_rows, out_weight, *kv_blocks],
        micros=5,
        scratch=[pltpu.VMEM((slots, att_width), F32)],
    )
    pieces, entries = gather_weight(out_weight, first, second, kv_blocks, attended)
    early = pieces[1:2]
    late = pieces[2:] or pieces
    now = [(0, *entry[1:]) for entry in entries[1:] if early and entry[0] == 1]
    skipped = len(pieces) - len(late)
    then = [(entry[0] - skipped, *entry[1:]) for entry in entries[1:] if entry[0] >= skipped]
    arrived, part = call(
        functools.partial(arrive_kernel, owners, now),
        [shape((slots, moved_width), BF16), shape((slots, width), F32)],
        [*exchange(routed, 1), *early],
        micros=10,
    )
    done = call(
        functools.partial(expert_kernel, then, len(late)),
        [shape((CAP, width), BF16)] * owners,
        [gain[None, :], w_gate[0], w_up[0], w_down[0], arrived, part, *late],
        micros=2,
    )
    back = exchange(done, -1)
    (hidden,) = call(
        functools.partial(project_kernel, entries),
        [shape((tok_rows, width), F32)],
        [attended, residual[0], *pieces],
        micros=2,
    )
    (out,) = call(
        functools.partial(combine_kernel, owners),
        [shape((tok_rows, width), BF16)],
        [hidden, mix, *back],
        micros=1,
    )
    return out[None]


def solution(mesh):
    return jax.shard_map(
        per_device,
        mesh=mesh,
        in_specs=(
            P(("dp", "exp"), "ctx", None),
            P(("dp", "exp"), "ctx", None),
            P(("dp", "exp"), "ctx", None),
            P(("dp", "exp"), None),
            P(("dp", "exp"), "ctx", None),
            P("ctx", None),
            P(),
            P(("dp", "exp"), "ctx", None),
            P(("dp", "exp"), "ctx", None),
            P("exp", None, None),
            P("exp", None, None),
            P("exp", None, None),
        ),
        out_specs=P(("dp", "exp"), "ctx", None),
        check_vma=False,
    )
```

```python
import functools
import math

import jax
import jax.numpy as jnp
from jax import lax
from jax.experimental import pallas as pl
from jax.experimental.pallas import tpu as pltpu
from jax.sharding import PartitionSpec as P

HQ = 16
KVH = 2
HD = 128
GROUPS = HQ // KVH
CAP = 24
NEG = -1e30
SCORE_SCALE = math.log2(math.e) / math.sqrt(HD)
F32 = jnp.float32
BF16 = jnp.bfloat16


def slab_segments(segs_ref, index, count, rows):
    found = segs_ref[:, 0:rows]
    for slab in range(1, count):
        found = jnp.where(index == slab, segs_ref[:, slab * rows : (slab + 1) * rows], found)
    return found


def score_bias(segs_ref, backs, count, rows):
    me = lax.axis_index("ctx")
    row = lax.broadcasted_iota(jnp.int32, (rows, rows), 0)
    col = lax.broadcasted_iota(jnp.int32, (rows, rows), 1)
    own_seg = slab_segments(segs_ref, me, count, rows)
    query_seg = jnp.sum(jnp.where(row == col, own_seg, 0), axis=1, keepdims=True)
    parts = []
    for back in backs:
        if back == 0:
            allowed = (col <= row) & (own_seg == query_seg)
        else:
            key_seg = slab_segments(segs_ref, jnp.maximum(me - back, 0), count, rows)
            allowed = (key_seg == query_seg) & (me >= back)
        parts.append(jnp.where(allowed, 0.0, NEG))
    return parts


def group_scores(stacked, keys, bias):
    scores = lax.dot_general(
        stacked, keys, (((1,), (1,)), ((), ())), preferred_element_type=F32
    )
    return scores.reshape(GROUPS, *bias.shape) * SCORE_SCALE + bias


def weigh(expo, values):
    rows = expo.shape[0] * expo.shape[1]
    mixed = jnp.dot(
        expo.astype(BF16).reshape(rows, expo.shape[2]), values, preferred_element_type=F32
    ).reshape(*expo.shape[:2], 2 * HD)
    return mixed[:, :, :HD], mixed[:, :, HD : HD + 1]


def mark_kernel(*refs):
    refs[-1][...] = jnp.zeros_like(refs[-1])


def gate_kernel(*refs):
    del refs


def after(piece, *marks):
    spec = pl.BlockSpec(memory_space=pl.ANY)
    return pl.pallas_call(
        gate_kernel,
        out_shape=jax.ShapeDtypeStruct(piece.shape, piece.dtype),
        in_specs=[spec] * (1 + len(marks)),
        out_specs=spec,
        input_output_aliases={0: 0},
        compiler_params=pltpu.CompilerParams(vmem_limit_bytes=1 << 20),
    )(piece, *marks)


def join_kernel(first_ref, second_ref, mark_ref, whole_ref, sems):
    del mark_ref
    half = first_ref.shape[0]
    core = lax.rem(lax.axis_index("dp"), 2)
    copies = []
    for index, (lead, ref) in enumerate([(core, first_ref), (1 - core, second_ref)]):
        target = whole_ref.at[pl.ds(pl.multiple_of(lead * half, half), half)]
        copies.append(pltpu.make_async_copy(ref, target, sems.at[index]))
        copies[-1].start()
    for copy in copies:
        copy.wait()


def own_kernel(
    n_ctx,
    q_ref,
    kv_ref,
    segs_ref,
    mark_ref,
    w_ref,
    acc_ref,
    max_ref,
    sum_ref,
    queries_ref,
    first_ref,
    second_ref,
    sems,
):
    del mark_ref
    half = first_ref.shape[0]
    core = lax.rem(lax.axis_index("dp"), 2)
    copies = []
    for index, (lead, ref) in enumerate([(core, first_ref), (1 - core, second_ref)]):
        source = w_ref.at[pl.ds(pl.multiple_of(lead * half, half), half)]
        copies.append(pltpu.make_async_copy(source, ref, sems.at[index]))
        copies[-1].start()
    rows = q_ref.shape[0]
    (bias,) = score_bias(segs_ref, (0,), n_ctx, rows)
    ones = jnp.ones((rows, HD), BF16)
    for kv in range(KVH):
        keys = kv_ref[:, kv * HD : (kv + 1) * HD]
        values = jnp.concatenate([kv_ref[:, (KVH + kv) * HD : (KVH + kv + 1) * HD], ones], axis=1)
        heads = range(kv * GROUPS, (kv + 1) * GROUPS)
        stacked = jnp.concatenate([q_ref[:, h * HD : (h + 1) * HD] for h in heads], axis=0)
        queries_ref[kv] = stacked
        scores = group_scores(stacked, keys, bias)
        row_max = jnp.max(scores, axis=2, keepdims=True)
        accum, row_sum = weigh(jnp.exp2(scores - row_max), values)
        acc_ref[kv] = accum
        max_ref[kv] = row_max
        sum_ref[kv] = row_sum
    for copy in copies:
        copy.wait()


def route_kernel(ids_ref, rw_ref, res_ref, place_ref, mix_ref, rows_ref):
    slots, rows = mix_ref.shape
    slot = lax.broadcasted_iota(jnp.int32, (slots, rows), 0)
    owner = (slot // CAP) ^ lax.axis_index("exp")
    hit = jnp.zeros((slots, rows), jnp.bool_)
    weight = jnp.zeros((slots, rows), F32)
    for choice in range(ids_ref.shape[0]):
        same = ids_ref[choice : choice + 1, :] == owner
        hit = hit | same
        weight = jnp.where(same, rw_ref[choice : choice + 1, :], weight)
    row = lax.broadcasted_iota(jnp.int32, (rows, rows), 0)
    col = lax.broadcasted_iota(jnp.int32, (rows, rows), 1)
    before = (row < col).astype(F32).astype(BF16)
    rank = jnp.dot(hit.astype(F32).astype(BF16), before, preferred_element_type=F32)
    placed = hit & (rank == lax.rem(slot, CAP).astype(F32))
    place = placed.astype(F32).astype(BF16)
    place_ref[...] = place
    mix_ref[...] = jnp.where(placed, weight, 0.0)
    rows_ref[...] = jnp.dot(place, res_ref[...], preferred_element_type=F32)


def attend_blocks(n_ctx, backs, segs_ref, state_refs, queries_ref, kv_refs, write):
    acc_ref, max_ref, sum_ref = state_refs
    rows = queries_ref.shape[1] // GROUPS
    bias = jnp.concatenate(score_bias(segs_ref, backs, n_ctx, rows), axis=1)
    ones = jnp.ones((rows * len(backs), HD), BF16)
    for kv in range(KVH):
        keys = jnp.concatenate([ref[:, kv * HD : (kv + 1) * HD] for ref in kv_refs], axis=0)
        values = jnp.concatenate(
            [ref[:, (KVH + kv) * HD : (KVH + kv + 1) * HD] for ref in kv_refs], axis=0
        )
        values = jnp.concatenate([values, ones], axis=1)
        scores = group_scores(queries_ref[kv], keys, bias)
        old_max = max_ref[kv]
        new_max = jnp.maximum(old_max, jnp.max(scores, axis=2, keepdims=True))
        accum, row_sum = weigh(jnp.exp2(scores - new_max), values)
        fix = jnp.exp2(old_max - new_max)
        write(kv, acc_ref[kv] * fix + accum, new_max, sum_ref[kv] * fix + row_sum)


def far_kernel(n_ctx, backs, segs_ref, acc_ref, max_ref, sum_ref, queries_ref, *refs):
    kv_refs, (acc_out, max_out, sum_out) = refs[:-3], refs[-3:]

    def write(kv, accum, row_max, row_sum):
        acc_out[kv] = accum
        max_out[kv] = row_max
        sum_out[kv] = row_sum

    state = (acc_ref, max_ref, sum_ref)
    attend_blocks(n_ctx, backs, segs_ref, state, queries_ref, kv_refs, write)


def near_kernel(
    n_ctx,
    segs_ref,
    acc_ref,
    max_ref,
    sum_ref,
    queries_ref,
    place_ref,
    rows_ref,
    w_ref,
    kv_ref,
    *refs,
):
    out_ref, *send_refs = refs[: 1 + lax.axis_size("exp")]
    routed_ref = refs[-1]

    def write(kv, accum, row_max, row_sum):
        attended = (accum / row_sum).astype(BF16)
        for group in range(GROUPS):
            head = kv * GROUPS + group
            out_ref[:, head * HD : (head + 1) * HD] = attended[group]

    state = (acc_ref, max_ref, sum_ref)
    attend_blocks(n_ctx, (1,), segs_ref, state, queries_ref, (kv_ref,), write)
    routed_ref[...] = jnp.dot(place_ref[...], out_ref[...], preferred_element_type=F32)
    me, share = lax.axis_index("ctx"), w_ref.shape[0]

    def quarter(flip):
        return routed_ref[:, pl.ds(pl.multiple_of((me ^ flip) * share, share), share)]

    part = rows_ref[...] + jnp.dot(
        quarter(0).astype(BF16), w_ref[...], preferred_element_type=F32
    )
    blocks = [quarter(flip) for flip in range(1, n_ctx)] + [part]
    for step, ref in enumerate(send_refs):
        for place, block in enumerate(blocks):
            ref[:, place * share : place * share + block.shape[1]] = block[
                step * CAP : (step + 1) * CAP, :
            ].astype(BF16)


def stack(parts):
    return jnp.concatenate([part.astype(F32) for part in parts], axis=0).astype(BF16)


def project(total, att_ref, entries, piece_refs, moved):
    me, core = lax.axis_index("ctx"), lax.axis_index("dp")
    share = att_ref.shape[1] // (lax.axis_size("ctx") - moved)
    for piece, size, flip, offset, row in entries:
        quarter = flip(core) - 1 if moved else me ^ flip(core)
        lead = pl.multiple_of(quarter * share + offset(core), size)
        rows = pl.ds(pl.multiple_of(row(me), size), size)
        total = total + jnp.dot(
            att_ref[:, pl.ds(lead, size)], piece_refs[piece][rows, :], preferred_element_type=F32
        )
    return total


def arrive_kernel(owners, entries, *refs):
    row_refs, piece_refs, (att_ref, hidden_ref) = refs[:owners], refs[owners:-2], refs[-2:]
    row_refs = row_refs[:1] + row_refs[:0:-1]
    wide = att_ref.shape[1]
    att_ref[...] = stack([ref[:, :wide] for ref in row_refs])
    hidden = jnp.concatenate([ref[:, wide:].astype(F32) for ref in row_refs], axis=0)
    hidden_ref[...] = project(hidden, att_ref, entries, piece_refs, True)


def expert_kernel(entries, count, gain_ref, gate_ref, up_ref, down_ref, att_ref, part_ref, *refs):
    piece_refs, out_refs = refs[:count], refs[count:]
    hidden = project(part_ref[...], att_ref, entries, piece_refs, True)
    mean = jnp.mean(hidden * hidden, axis=1, keepdims=True)
    normed = (hidden * lax.rsqrt(mean + 1e-06) * gain_ref[...]).astype(BF16)
    gate = jnp.dot(normed, gate_ref[...], preferred_element_type=F32)
    up = jnp.dot(normed, up_ref[...], preferred_element_type=F32)
    act = (gate / (1.0 + jnp.exp(-gate)) * up).astype(BF16)
    out = jnp.dot(act, down_ref[...], preferred_element_type=F32)
    for step, ref in enumerate(out_refs):
        ref[...] = out[step * CAP : (step + 1) * CAP, :].astype(BF16)


def project_kernel(entries, att_ref, res_ref, *refs):
    hidden = res_ref[...].astype(F32)
    refs[-1][...] = project(hidden, att_ref, entries, refs[:-1], False)


def combine_kernel(owners, hidden_ref, mix_ref, *refs):
    row_refs, out_ref = refs[:1] + refs[owners - 1 : 0 : -1], refs[owners]
    rows = stack([ref[...] for ref in row_refs])
    mix = mix_ref[...]
    high = mix.astype(BF16)
    low = (mix - high.astype(F32)).astype(BF16)
    total = hidden_ref[...]
    for part in (high, low):
        total = total + lax.dot_general(
            part, rows, (((0,), (0,)), ((), ())), preferred_element_type=F32
        )
    out_ref[...] = total.astype(BF16)


def call(kernel, outs, args, micros, scratch=(), limit=24, free_in=0, free_out=0):
    vmem, free = pl.BlockSpec(memory_space=pltpu.VMEM), pl.BlockSpec(memory_space=pl.ANY)
    nbytes = sum(math.prod(a.shape) * a.dtype.itemsize for a in list(args) + list(outs))
    return pl.pallas_call(
        kernel,
        out_shape=outs,
        in_specs=[vmem] * (len(args) - free_in) + [free] * free_in,
        out_specs=[vmem] * (len(outs) - free_out) + [free] * free_out,
        scratch_shapes=list(scratch),
        compiler_params=pltpu.CompilerParams(vmem_limit_bytes=limit << 20),
        cost_estimate=pl.CostEstimate(
            flops=int(micros * 1.15e9), bytes_accessed=nbytes, transcendentals=0
        ),
    )(*args)


def exchange(blocks):
    count = len(blocks)
    return [blocks[0]] + [
        lax.ppermute(blocks[s], "exp", [(i, i ^ s) for i in range(count)])
        for s in range(count - 1, 0, -1)
    ]


def gather_weight(weight, first, second, started, attended):
    n_ctx, cores = lax.axis_size("ctx"), lax.axis_size("dp")
    share = weight.shape[0]
    if (n_ctx, cores) != (4, 2):
        whole = lax.all_gather(weight, "ctx", axis=0, tiled=True)
        entries = [
            (0, share, lambda core, f=f: f, lambda core: 0, lambda me, f=f: (me ^ f) * share)
            for f in range(n_ctx)
        ]
        return [whole], entries
    both = ("ctx", "dp")
    devices = [(me, core) for me in range(n_ctx) for core in range(cores)]
    aside = [(me * 2 + core, (me ^ (1 + core)) * 2 + core) for me, core in devices]
    across = [(me * 2 + core, (me ^ (2 - core)) * 2 + core) for me, core in devices]
    near_first = lax.ppermute(first, both, aside)
    near_second = lax.ppermute(after(second, started), both, aside)
    near_first = after(near_first, attended)
    far = lax.ppermute(near_first, both, across)
    (near,) = call(
        join_kernel,
        [jax.ShapeDtypeStruct(weight.shape, BF16)],
        [near_first, near_second, attended],
        micros=1,
        free_in=3,
        free_out=1,
        limit=1,
        scratch=[pltpu.SemaphoreType.DMA((2,))],
    )
    swap = [(0, 1), (1, 0)]
    pieces = [weight, near, far, lax.ppermute(near, "dp", swap), lax.ppermute(far, "dp", swap)]
    half = share // 2
    first_row = lambda me: 0
    entries = [
        (0, share, lambda core: 0, lambda core: 0, first_row),
        (1, share, lambda core: 1 + core, lambda core: 0, first_row),
        (2, half, lambda core: 3, lambda core: core * half, first_row),
        (3, share, lambda core: 2 - core, lambda core: 0, first_row),
        (4, half, lambda core: 3, lambda core: (1 - core) * half, first_row),
    ]
    return pieces, entries


def per_device(
    queries,
    keys,
    values,
    segments,
    residual,
    out_weight,
    gain,
    expert_ids,
    route_weights,
    w_gate,
    w_up,
    w_down,
):
    tok_rows = queries.shape[1]
    width = residual.shape[2]
    att_width = queries.shape[2]
    n_ctx, owners = lax.axis_size("ctx"), lax.axis_size("exp")
    slots = owners * CAP
    moved_width = att_width - out_weight.shape[0]
    longest = segments.shape[1] // 2
    back_count = min(n_ctx - 1, -(-(longest - 1) // tok_rows))
    shape = jax.ShapeDtypeStruct

    own_kv = jnp.concatenate([keys[0], values[0]], axis=1)
    kv_blocks = []
    for back in range(1, back_count + 1):
        pairs = [(i, (i + back) % n_ctx) for i in range(n_ctx)]
        kv_blocks.append(lax.ppermute(own_kv, "ctx", pairs))
    (mark,) = call(mark_kernel, [shape((8, 128), F32)], [own_kv], micros=5, free_in=1, limit=1)
    half = shape((out_weight.shape[0] // 2, width), BF16)
    accum, row_max, row_sum, stacked, first, second = call(
        functools.partial(own_kernel, n_ctx),
        [
            shape((KVH, GROUPS, tok_rows, HD), F32),
            shape((KVH, GROUPS, tok_rows, 1), F32),
            shape((KVH, GROUPS, tok_rows, 1), F32),
            shape((KVH, GROUPS * tok_rows, HD), BF16),
            half,
            half,
        ],
        [queries[0], own_kv, segments, mark, out_weight],
        micros=3,
        free_in=1,
        free_out=2,
        scratch=[pltpu.SemaphoreType.DMA((2,))],
    )
    place, mix, res_rows = call(
        route_kernel,
        [
            shape((slots, tok_rows), BF16),
            shape((slots, tok_rows), F32),
            shape((slots, width), F32),
        ],
        [expert_ids[0].T, route_weights[0].T, residual[0]],
        micros=1,
    )
    state = [accum, row_max, row_sum]
    if back_count > 1:
        state = call(
            functools.partial(far_kernel, n_ctx, range(2, back_count + 1)),
            [shape(part.shape, F32) for part in state],
            [segments, *state, stacked, *kv_blocks[1:]],
            micros=3,
        )
    attended, *routed = call(
        functools.partial(near_kernel, n_ctx),
        [shape((tok_rows, att_width), BF16)]
        + [shape((CAP, moved_width + width), BF16)] * owners,
        [segments, *state, stacked, place, res_rows, out_weight, kv_blocks[0]],
        micros=3,
        scratch=[pltpu.VMEM((slots, att_width), F32)],
    )
    pieces, entries = gather_weight(out_weight, first, second, state[0], attended)
    early = pieces[1:2]
    late = pieces[2:] or pieces
    now = [(0, *entry[1:]) for entry in entries[1:] if early and entry[0] == 1]
    skipped = len(pieces) - len(late)
    then = [(entry[0] - skipped, *entry[1:]) for entry in entries[1:] if entry[0] >= skipped]
    arrived, part = call(
        functools.partial(arrive_kernel, owners, now),
        [shape((slots, moved_width), BF16), shape((slots, width), F32)],
        [*exchange(routed), *early],
        micros=10,
    )
    done = call(
        functools.partial(expert_kernel, then, len(late)),
        [shape((CAP, width), BF16)] * owners,
        [gain[None, :], w_gate[0], w_up[0], w_down[0], arrived, part, *late],
        micros=2,
    )
    back = exchange(done)
    (hidden,) = call(
        functools.partial(project_kernel, entries),
        [shape((tok_rows, width), F32)],
        [attended, residual[0], *pieces],
        micros=2,
    )
    (out,) = call(
        functools.partial(combine_kernel, owners),
        [shape((tok_rows, width), BF16)],
        [hidden, mix, *back],
        micros=1,
    )
    return out[None]


def solution(mesh):
    return jax.shard_map(
        per_device,
        mesh=mesh,
        in_specs=(
            P(("dp", "exp"), "ctx", None),
            P(("dp", "exp"), "ctx", None),
            P(("dp", "exp"), "ctx", None),
            P(("dp", "exp"), None),
            P(("dp", "exp"), "ctx", None),
            P("ctx", None),
            P(),
            P(("dp", "exp"), "ctx", None),
            P(("dp", "exp"), "ctx", None),
            P("exp", None, None),
            P("exp", None, None),
            P("exp", None, None),
        ),
        out_specs=P(("dp", "exp"), "ctx", None),
        check_vma=False,
    )
```

```python
import functools
import math

import jax
import jax.numpy as jnp
from jax import lax
from jax.experimental import pallas as pl
from jax.experimental.pallas import tpu as pltpu
from jax.sharding import PartitionSpec as P

HQ = 16
KVH = 2
HD = 128
GROUPS = HQ // KVH
CAP = 24
NEG = -1e30
SCORE_SCALE = math.log2(math.e) / math.sqrt(HD)
F32 = jnp.float32
BF16 = jnp.bfloat16


def slab_segments(segs_ref, index, count, rows):
    found = segs_ref[:, 0:rows]
    for slab in range(1, count):
        found = jnp.where(index == slab, segs_ref[:, slab * rows : (slab + 1) * rows], found)
    return found


def score_bias(segs_ref, backs, count, rows):
    me = lax.axis_index("ctx")
    row = lax.broadcasted_iota(jnp.int32, (rows, rows), 0)
    col = lax.broadcasted_iota(jnp.int32, (rows, rows), 1)
    own_seg = slab_segments(segs_ref, me, count, rows)
    query_seg = jnp.sum(jnp.where(row == col, own_seg, 0), axis=1, keepdims=True)
    parts = []
    for back in backs:
        if back == 0:
            allowed = (col <= row) & (own_seg == query_seg)
        else:
            key_seg = slab_segments(segs_ref, jnp.maximum(me - back, 0), count, rows)
            allowed = (key_seg == query_seg) & (me >= back)
        parts.append(jnp.where(allowed, 0.0, NEG))
    return parts


def group_scores(stacked, keys, bias):
    scores = lax.dot_general(
        stacked, keys, (((1,), (1,)), ((), ())), preferred_element_type=F32
    )
    return scores.reshape(GROUPS, *bias.shape) * SCORE_SCALE + bias


def weigh(expo, values):
    rows = expo.shape[0] * expo.shape[1]
    mixed = jnp.dot(
        expo.astype(BF16).reshape(rows, expo.shape[2]), values, preferred_element_type=F32
    ).reshape(*expo.shape[:2], 2 * HD)
    return mixed[:, :, :HD], mixed[:, :, HD:]


def mark_kernel(*refs):
    refs[-1][...] = jnp.zeros_like(refs[-1])


def gate_kernel(*refs):
    del refs


def after(piece, *marks):
    spec = pl.BlockSpec(memory_space=pl.ANY)
    return pl.pallas_call(
        gate_kernel,
        out_shape=jax.ShapeDtypeStruct(piece.shape, piece.dtype),
        in_specs=[spec] * (1 + len(marks)),
        out_specs=spec,
        input_output_aliases={0: 0},
        compiler_params=pltpu.CompilerParams(vmem_limit_bytes=1 << 20),
    )(piece, *marks)


def join_kernel(first_ref, second_ref, mark_ref, whole_ref, sems):
    del mark_ref
    half = first_ref.shape[0]
    core = lax.rem(lax.axis_index("dp"), 2)
    copies = []
    for index, (lead, ref) in enumerate([(core, first_ref), (1 - core, second_ref)]):
        target = whole_ref.at[pl.ds(pl.multiple_of(lead * half, half), half)]
        copies.append(pltpu.make_async_copy(ref, target, sems.at[index]))
        copies[-1].start()
    for copy in copies:
        copy.wait()


def own_kernel(
    n_ctx,
    q_ref,
    kv_ref,
    segs_ref,
    mark_ref,
    w_ref,
    acc_ref,
    max_ref,
    sum_ref,
    queries_ref,
    first_ref,
    second_ref,
    sems,
):
    del mark_ref
    half = first_ref.shape[0]
    core = lax.rem(lax.axis_index("dp"), 2)
    copies = []
    for index, (lead, ref) in enumerate([(core, first_ref), (1 - core, second_ref)]):
        source = w_ref.at[pl.ds(pl.multiple_of(lead * half, half), half)]
        copies.append(pltpu.make_async_copy(source, ref, sems.at[index]))
        copies[-1].start()
    rows = q_ref.shape[0]
    (bias,) = score_bias(segs_ref, (0,), n_ctx, rows)
    ones = jnp.ones((rows, HD), BF16)
    for kv in range(KVH):
        keys = kv_ref[:, kv * HD : (kv + 1) * HD]
        values = jnp.concatenate([kv_ref[:, (KVH + kv) * HD : (KVH + kv + 1) * HD], ones], axis=1)
        heads = range(kv * GROUPS, (kv + 1) * GROUPS)
        stacked = jnp.concatenate([q_ref[:, h * HD : (h + 1) * HD] for h in heads], axis=0)
        queries_ref[kv] = stacked
        scores = group_scores(stacked, keys, bias)
        row_max = jnp.max(scores, axis=2, keepdims=True)
        accum, row_sum = weigh(jnp.exp2(scores - row_max), values)
        acc_ref[kv] = accum
        max_ref[kv] = jnp.broadcast_to(row_max, max_ref.shape[1:])
        sum_ref[kv] = row_sum
    for copy in copies:
        copy.wait()


def route_kernel(ids_ref, rw_ref, res_ref, place_ref, mix_ref, rows_ref):
    slots, rows = mix_ref.shape
    slot = lax.broadcasted_iota(jnp.int32, (slots, rows), 0)
    owner = (slot // CAP) ^ lax.axis_index("exp")
    hit = jnp.zeros((slots, rows), jnp.bool_)
    weight = jnp.zeros((slots, rows), F32)
    for choice in range(ids_ref.shape[0]):
        same = ids_ref[choice : choice + 1, :] == owner
        hit = hit | same
        weight = jnp.where(same, rw_ref[choice : choice + 1, :], weight)
    row = lax.broadcasted_iota(jnp.int32, (rows, rows), 0)
    col = lax.broadcasted_iota(jnp.int32, (rows, rows), 1)
    before = (row < col).astype(F32).astype(BF16)
    rank = jnp.dot(hit.astype(F32).astype(BF16), before, preferred_element_type=F32)
    placed = hit & (rank == lax.rem(slot, CAP).astype(F32))
    place = placed.astype(F32).astype(BF16)
    place_ref[...] = place
    mix_ref[...] = jnp.where(placed, weight, 0.0)
    rows_ref[...] = jnp.dot(place, res_ref[...], preferred_element_type=F32)


def rest_kernel(
    n_ctx,
    back_count,
    segs_ref,
    acc_ref,
    max_ref,
    sum_ref,
    queries_ref,
    place_ref,
    rows_ref,
    w_ref,
    *refs,
):
    kv_refs, refs = refs[:back_count], refs[back_count + 3 :]
    out_ref, *send_refs = refs[:-1]
    routed_ref = refs[-1]
    rows = queries_ref.shape[1] // GROUPS
    bias = jnp.concatenate(score_bias(segs_ref, range(1, back_count + 1), n_ctx, rows), axis=1)
    keys_count = rows * back_count
    spread = -(-keys_count // HD)
    ones = jnp.ones((keys_count, HD), BF16)
    for kv in range(KVH):
        keys = jnp.concatenate([ref[:, kv * HD : (kv + 1) * HD] for ref in kv_refs], axis=0)
        values = jnp.concatenate(
            [ref[:, (KVH + kv) * HD : (KVH + kv + 1) * HD] for ref in kv_refs], axis=0
        )
        values = jnp.concatenate([values, ones], axis=1)
        scores = group_scores(queries_ref[kv], keys, bias)
        old_max = max_ref[kv]
        new_max = jnp.maximum(old_max, jnp.max(scores, axis=2, keepdims=True))
        shift = jnp.concatenate([new_max] * spread, axis=2)[:, :, :keys_count]
        accum, row_sum = weigh(jnp.exp2(scores - shift), values)
        fix = jnp.exp2(old_max - new_max)
        total = sum_ref[kv] * fix + row_sum
        attended = ((acc_ref[kv] * fix + accum) / total).astype(BF16)
        for group in range(GROUPS):
            head = kv * GROUPS + group
            out_ref[:, head * HD : (head + 1) * HD] = attended[group]
    routed_ref[...] = jnp.dot(place_ref[...], out_ref[...], preferred_element_type=F32)
    me, share = lax.axis_index("ctx"), w_ref.shape[0]

    def quarter(flip):
        return routed_ref[:, pl.ds(pl.multiple_of((me ^ flip) * share, share), share)]

    part = rows_ref[...] + jnp.dot(
        quarter(0).astype(BF16), w_ref[...], preferred_element_type=F32
    )
    blocks = [quarter(flip) for flip in range(1, n_ctx)] + [part]
    for step, ref in enumerate(send_refs):
        for place, block in enumerate(blocks):
            ref[:, place * share : place * share + block.shape[1]] = block[
                step * CAP : (step + 1) * CAP, :
            ].astype(BF16)


def stack(parts):
    return jnp.concatenate([part.astype(F32) for part in parts], axis=0).astype(BF16)


def project(total, att_ref, entries, piece_refs, moved):
    me, core = lax.axis_index("ctx"), lax.axis_index("dp")
    share = att_ref.shape[1] // (lax.axis_size("ctx") - moved)
    for piece, size, flip, offset, row in entries:
        quarter = flip(core) - 1 if moved else me ^ flip(core)
        lead = pl.multiple_of(quarter * share + offset(core), size)
        rows = pl.ds(pl.multiple_of(row(me), size), size)
        total = total + jnp.dot(
            att_ref[:, pl.ds(lead, size)], piece_refs[piece][rows, :], preferred_element_type=F32
        )
    return total


def arrive_kernel(owners, entries, *refs):
    row_refs, piece_refs, (att_ref, hidden_ref) = refs[:owners], refs[owners:-2], refs[-2:]
    row_refs = row_refs[:1] + row_refs[:0:-1]
    wide = att_ref.shape[1]
    att_ref[...] = stack([ref[:, :wide] for ref in row_refs])
    hidden = jnp.concatenate([ref[:, wide:].astype(F32) for ref in row_refs], axis=0)
    hidden_ref[...] = project(hidden, att_ref, entries, piece_refs, True)


def expert_kernel(entries, count, gain_ref, gate_ref, up_ref, down_ref, att_ref, part_ref, *refs):
    piece_refs, out_refs = refs[:count], refs[count:]
    hidden = project(part_ref[...], att_ref, entries, piece_refs, True)
    mean = jnp.mean(hidden * hidden, axis=1, keepdims=True)
    normed = (hidden * lax.rsqrt(mean + 1e-06) * gain_ref[...]).astype(BF16)
    gate = jnp.dot(normed, gate_ref[...], preferred_element_type=F32)
    up = jnp.dot(normed, up_ref[...], preferred_element_type=F32)
    act = (gate / (1.0 + jnp.exp(-gate)) * up).astype(BF16)
    out = jnp.dot(act, down_ref[...], preferred_element_type=F32)
    for step, ref in enumerate(out_refs):
        ref[...] = out[step * CAP : (step + 1) * CAP, :].astype(BF16)


def project_kernel(entries, att_ref, res_ref, *refs):
    hidden = res_ref[...].astype(F32)
    refs[-1][...] = project(hidden, att_ref, entries, refs[:-1], False)


def combine_kernel(owners, hidden_ref, mix_ref, *refs):
    row_refs, out_ref = refs[:1] + refs[owners - 1 : 0 : -1], refs[owners]
    rows = stack([ref[...] for ref in row_refs])
    mix = mix_ref[...]
    high = mix.astype(BF16)
    low = (mix - high.astype(F32)).astype(BF16)
    total = hidden_ref[...]
    for part in (high, low):
        total = total + lax.dot_general(
            part, rows, (((0,), (0,)), ((), ())), preferred_element_type=F32
        )
    out_ref[...] = total.astype(BF16)


def call(kernel, outs, args, micros, scratch=(), limit=24, free_in=0, free_out=0):
    vmem, free = pl.BlockSpec(memory_space=pltpu.VMEM), pl.BlockSpec(memory_space=pl.ANY)
    nbytes = sum(math.prod(a.shape) * a.dtype.itemsize for a in list(args) + list(outs))
    return pl.pallas_call(
        kernel,
        out_shape=outs,
        in_specs=[vmem] * (len(args) - free_in) + [free] * free_in,
        out_specs=[vmem] * (len(outs) - free_out) + [free] * free_out,
        scratch_shapes=list(scratch),
        compiler_params=pltpu.CompilerParams(vmem_limit_bytes=limit << 20),
        cost_estimate=pl.CostEstimate(
            flops=int(micros * 1.15e9), bytes_accessed=nbytes, transcendentals=0
        ),
    )(*args)


def exchange(blocks):
    count = len(blocks)
    return [blocks[0]] + [
        lax.ppermute(blocks[s], "exp", [(i, i ^ s) for i in range(count)])
        for s in range(count - 1, 0, -1)
    ]


def gather_weight(weight, first, second, arrived, attended):
    n_ctx, cores = lax.axis_size("ctx"), lax.axis_size("dp")
    share = weight.shape[0]
    if (n_ctx, cores) != (4, 2):
        whole = lax.all_gather(weight, "ctx", axis=0, tiled=True)
        entries = [
            (0, share, lambda core, f=f: f, lambda core: 0, lambda me, f=f: (me ^ f) * share)
            for f in range(n_ctx)
        ]
        return [whole], entries
    both = ("ctx", "dp")
    devices = [(me, core) for me in range(n_ctx) for core in range(cores)]
    aside = [(me * 2 + core, (me ^ (1 + core)) * 2 + core) for me, core in devices]
    across = [(me * 2 + core, (me ^ (2 - core)) * 2 + core) for me, core in devices]
    near_first = lax.ppermute(first, both, aside)
    near_second = lax.ppermute(after(second, *arrived), both, aside)
    near_first = after(near_first, attended)
    far = lax.ppermute(near_first, both, across)
    (near,) = call(
        join_kernel,
        [jax.ShapeDtypeStruct(weight.shape, BF16)],
        [near_first, near_second, attended],
        micros=1,
        free_in=3,
        free_out=1,
        limit=1,
        scratch=[pltpu.SemaphoreType.DMA((2,))],
    )
    swap = [(0, 1), (1, 0)]
    pieces = [weight, near, far, lax.ppermute(near, "dp", swap), lax.ppermute(far, "dp", swap)]
    half = share // 2
    first_row = lambda me: 0
    entries = [
        (0, share, lambda core: 0, lambda core: 0, first_row),
        (1, share, lambda core: 1 + core, lambda core: 0, first_row),
        (2, half, lambda core: 3, lambda core: core * half, first_row),
        (3, share, lambda core: 2 - core, lambda core: 0, first_row),
        (4, half, lambda core: 3, lambda core: (1 - core) * half, first_row),
    ]
    return pieces, entries


def per_device(
    queries,
    keys,
    values,
    segments,
    residual,
    out_weight,
    gain,
    expert_ids,
    route_weights,
    w_gate,
    w_up,
    w_down,
):
    tok_rows = queries.shape[1]
    width = residual.shape[2]
    att_width = queries.shape[2]
    n_ctx, owners = lax.axis_size("ctx"), lax.axis_size("exp")
    slots = owners * CAP
    moved_width = att_width - out_weight.shape[0]
    longest = segments.shape[1] // 2
    back_count = min(n_ctx - 1, -(-(longest - 1) // tok_rows))
    shape = jax.ShapeDtypeStruct

    own_kv = jnp.concatenate([keys[0], values[0]], axis=1)
    kv_blocks = []
    for back in range(1, back_count + 1):
        pairs = [(i, (i + back) % n_ctx) for i in range(n_ctx)]
        kv_blocks.append(lax.ppermute(own_kv, "ctx", pairs))
    (mark,) = call(mark_kernel, [shape((8, 128), F32)], [own_kv], micros=5, free_in=1, limit=1)
    half = shape((out_weight.shape[0] // 2, width), BF16)
    accum, row_max, row_sum, stacked, first, second = call(
        functools.partial(own_kernel, n_ctx),
        [
            shape((KVH, GROUPS, tok_rows, HD), F32),
            shape((KVH, GROUPS, tok_rows, HD), F32),
            shape((KVH, GROUPS, tok_rows, HD), F32),
            shape((KVH, GROUPS * tok_rows, HD), BF16),
            half,
            half,
        ],
        [queries[0], own_kv, segments, mark, out_weight],
        micros=3,
        free_in=1,
        free_out=2,
        scratch=[pltpu.SemaphoreType.DMA((2,))],
    )
    place, mix, res_rows = call(
        route_kernel,
        [
            shape((slots, tok_rows), BF16),
            shape((slots, tok_rows), F32),
            shape((slots, width), F32),
        ],
        [expert_ids[0].T, route_weights[0].T, residual[0]],
        micros=1,
    )
    attended, *routed = call(
        functools.partial(rest_kernel, n_ctx, back_count),
        [shape((tok_rows, att_width), BF16)]
        + [shape((CAP, moved_width + width), BF16)] * owners,
        [segments, accum, row_max, row_sum, stacked, place, res_rows, out_weight, *kv_blocks]
        + [w_gate[0], w_up[0], w_down[0]],
        micros=5,
        scratch=[pltpu.VMEM((slots, att_width), F32)],
    )
    pieces, entries = gather_weight(out_weight, first, second, kv_blocks, attended)
    early = pieces[1:2]
    late = pieces[2:] or pieces
    now = [(0, *entry[1:]) for entry in entries[1:] if early and entry[0] == 1]
    skipped = len(pieces) - len(late)
    then = [(entry[0] - skipped, *entry[1:]) for entry in entries[1:] if entry[0] >= skipped]
    arrived, part = call(
        functools.partial(arrive_kernel, owners, now),
        [shape((slots, moved_width), BF16), shape((slots, width), F32)],
        [*exchange(routed), *early],
        micros=10,
    )
    done = call(
        functools.partial(expert_kernel, then, len(late)),
        [shape((CAP, width), BF16)] * owners,
        [gain[None, :], w_gate[0], w_up[0], w_down[0], arrived, part, *late],
        micros=2,
    )
    back = exchange(done)
    (hidden,) = call(
        functools.partial(project_kernel, entries),
        [shape((tok_rows, width), F32)],
        [attended, residual[0], *pieces],
        micros=2,
    )
    (out,) = call(
        functools.partial(combine_kernel, owners),
        [shape((tok_rows, width), BF16)],
        [hidden, mix, *back],
        micros=1,
    )
    return out[None]


def solution(mesh):
    return jax.shard_map(
        per_device,
        mesh=mesh,
        in_specs=(
            P(("dp", "exp"), "ctx", None),
            P(("dp", "exp"), "ctx", None),
            P(("dp", "exp"), "ctx", None),
            P(("dp", "exp"), None),
            P(("dp", "exp"), "ctx", None),
            P("ctx", None),
            P(),
            P(("dp", "exp"), "ctx", None),
            P(("dp", "exp"), "ctx", None),
            P("exp", None, None),
            P("exp", None, None),
            P("exp", None, None),
        ),
        out_specs=P(("dp", "exp"), "ctx", None),
        check_vma=False,
    )
```

```python
import functools
import math

import jax
import jax.numpy as jnp
from jax import lax
from jax.experimental import pallas as pl
from jax.experimental.pallas import tpu as pltpu
from jax.sharding import PartitionSpec as P

HQ = 16
KVH = 2
HD = 128
GROUPS = HQ // KVH
CAP = 24
NEG = -1e30
SCORE_SCALE = math.log2(math.e) / math.sqrt(HD)
F32 = jnp.float32
BF16 = jnp.bfloat16


def slab_segments(segs_ref, index, count, rows):
    found = segs_ref[:, 0:rows]
    for slab in range(1, count):
        found = jnp.where(index == slab, segs_ref[:, slab * rows : (slab + 1) * rows], found)
    return found


def score_bias(segs_ref, backs, count, rows):
    me = lax.axis_index("ctx")
    row = lax.broadcasted_iota(jnp.int32, (rows, rows), 0)
    col = lax.broadcasted_iota(jnp.int32, (rows, rows), 1)
    own_seg = slab_segments(segs_ref, me, count, rows)
    query_seg = jnp.sum(jnp.where(row == col, own_seg, 0), axis=1, keepdims=True)
    parts = []
    for back in backs:
        if back == 0:
            allowed = (col <= row) & (own_seg == query_seg)
        else:
            key_seg = slab_segments(segs_ref, jnp.maximum(me - back, 0), count, rows)
            allowed = (key_seg == query_seg) & (me >= back)
        parts.append(jnp.where(allowed, 0.0, NEG))
    return parts


def group_scores(stacked, keys, bias):
    scores = lax.dot_general(
        stacked, keys, (((1,), (1,)), ((), ())), preferred_element_type=F32
    )
    return scores.reshape(GROUPS, *bias.shape) * SCORE_SCALE + bias


def weigh(expo, values):
    rows = expo.shape[0] * expo.shape[1]
    mixed = jnp.dot(
        expo.astype(BF16).reshape(rows, expo.shape[2]), values, preferred_element_type=F32
    ).reshape(*expo.shape[:2], 2 * HD)
    return mixed[:, :, :HD], mixed[:, :, HD:]


def mark_kernel(*refs):
    refs[-1][...] = jnp.zeros_like(refs[-1])


def gate_kernel(*refs):
    del refs


def after(piece, *marks):
    spec = pl.BlockSpec(memory_space=pl.ANY)
    return pl.pallas_call(
        gate_kernel,
        out_shape=jax.ShapeDtypeStruct(piece.shape, piece.dtype),
        in_specs=[spec] * (1 + len(marks)),
        out_specs=spec,
        input_output_aliases={0: 0},
        compiler_params=pltpu.CompilerParams(vmem_limit_bytes=1 << 20),
    )(piece, *marks)


def join_kernel(first_ref, second_ref, mark_ref, whole_ref, sems):
    del mark_ref
    half = first_ref.shape[0]
    core = lax.rem(lax.axis_index("dp"), 2)
    copies = []
    for index, (lead, ref) in enumerate([(core, first_ref), (1 - core, second_ref)]):
        target = whole_ref.at[pl.ds(pl.multiple_of(lead * half, half), half)]
        copies.append(pltpu.make_async_copy(ref, target, sems.at[index]))
        copies[-1].start()
    for copy in copies:
        copy.wait()


def own_kernel(
    n_ctx,
    q_ref,
    kv_ref,
    segs_ref,
    mark_ref,
    w_ref,
    acc_ref,
    max_ref,
    sum_ref,
    queries_ref,
    first_ref,
    second_ref,
    sems,
):
    del mark_ref
    half = first_ref.shape[0]
    core = lax.rem(lax.axis_index("dp"), 2)
    copies = []
    for index, (lead, ref) in enumerate([(core, first_ref), (1 - core, second_ref)]):
        source = w_ref.at[pl.ds(pl.multiple_of(lead * half, half), half)]
        copies.append(pltpu.make_async_copy(source, ref, sems.at[index]))
        copies[-1].start()
    rows = q_ref.shape[0]
    (bias,) = score_bias(segs_ref, (0,), n_ctx, rows)
    ones = jnp.ones((rows, HD), BF16)
    for kv in range(KVH):
        keys = kv_ref[:, kv * HD : (kv + 1) * HD]
        values = jnp.concatenate([kv_ref[:, (KVH + kv) * HD : (KVH + kv + 1) * HD], ones], axis=1)
        heads = range(kv * GROUPS, (kv + 1) * GROUPS)
        stacked = jnp.concatenate([q_ref[:, h * HD : (h + 1) * HD] for h in heads], axis=0)
        queries_ref[kv] = stacked
        scores = group_scores(stacked, keys, bias)
        row_max = jnp.max(scores, axis=2, keepdims=True)
        accum, row_sum = weigh(jnp.exp2(scores - row_max), values)
        acc_ref[kv] = accum
        max_ref[kv] = jnp.broadcast_to(row_max, max_ref.shape[1:])
        sum_ref[kv] = row_sum
    for copy in copies:
        copy.wait()


def route_kernel(ids_ref, rw_ref, res_ref, place_ref, mix_ref, rows_ref):
    slots, rows = mix_ref.shape
    slot = lax.broadcasted_iota(jnp.int32, (slots, rows), 0)
    owner = (slot // CAP) ^ lax.axis_index("exp")
    hit = jnp.zeros((slots, rows), jnp.bool_)
    weight = jnp.zeros((slots, rows), F32)
    for choice in range(ids_ref.shape[0]):
        same = ids_ref[choice : choice + 1, :] == owner
        hit = hit | same
        weight = jnp.where(same, rw_ref[choice : choice + 1, :], weight)
    row = lax.broadcasted_iota(jnp.int32, (rows, rows), 0)
    col = lax.broadcasted_iota(jnp.int32, (rows, rows), 1)
    before = (row < col).astype(F32).astype(BF16)
    rank = jnp.dot(hit.astype(F32).astype(BF16), before, preferred_element_type=F32)
    placed = hit & (rank == lax.rem(slot, CAP).astype(F32))
    place = placed.astype(F32).astype(BF16)
    place_ref[...] = place
    mix_ref[...] = jnp.where(placed, weight, 0.0)
    rows_ref[...] = jnp.dot(place, res_ref[...], preferred_element_type=F32)


def rest_kernel(
    n_ctx,
    back_count,
    segs_ref,
    acc_ref,
    max_ref,
    sum_ref,
    queries_ref,
    place_ref,
    rows_ref,
    w_ref,
    *refs,
):
    kv_refs, refs = refs[:back_count], refs[back_count + 4 :]
    out_ref, *send_refs = refs[:-1]
    routed_ref = refs[-1]
    rows = queries_ref.shape[1] // GROUPS
    bias = jnp.concatenate(score_bias(segs_ref, range(1, back_count + 1), n_ctx, rows), axis=1)
    keys_count = rows * back_count
    spread = -(-keys_count // HD)
    ones = jnp.ones((keys_count, HD), BF16)
    for kv in range(KVH):
        keys = jnp.concatenate([ref[:, kv * HD : (kv + 1) * HD] for ref in kv_refs], axis=0)
        values = jnp.concatenate(
            [ref[:, (KVH + kv) * HD : (KVH + kv + 1) * HD] for ref in kv_refs], axis=0
        )
        values = jnp.concatenate([values, ones], axis=1)
        scores = group_scores(queries_ref[kv], keys, bias)
        old_max = max_ref[kv]
        new_max = jnp.maximum(old_max, jnp.max(scores, axis=2, keepdims=True))
        shift = jnp.concatenate([new_max] * spread, axis=2)[:, :, :keys_count]
        accum, row_sum = weigh(jnp.exp2(scores - shift), values)
        fix = jnp.exp2(old_max - new_max)
        total = sum_ref[kv] * fix + row_sum
        attended = ((acc_ref[kv] * fix + accum) / total).astype(BF16)
        for group in range(GROUPS):
            head = kv * GROUPS + group
            out_ref[:, head * HD : (head + 1) * HD] = attended[group]
    routed_ref[...] = jnp.dot(place_ref[...], out_ref[...], preferred_element_type=F32)
    me, share = lax.axis_index("ctx"), w_ref.shape[0]

    def quarter(flip):
        return routed_ref[:, pl.ds(pl.multiple_of((me ^ flip) * share, share), share)]

    part = rows_ref[...] + jnp.dot(
        quarter(0).astype(BF16), w_ref[...], preferred_element_type=F32
    )
    blocks = [quarter(flip) for flip in range(1, n_ctx)] + [part]
    for step, ref in enumerate(send_refs):
        for place, block in enumerate(blocks):
            ref[:, place * share : place * share + block.shape[1]] = block[
                step * CAP : (step + 1) * CAP, :
            ].astype(BF16)


def stack(parts):
    return jnp.concatenate([part.astype(F32) for part in parts], axis=0).astype(BF16)


def project(total, att_ref, entries, piece_refs, moved):
    me, core = lax.axis_index("ctx"), lax.axis_index("dp")
    share = att_ref.shape[1] // (lax.axis_size("ctx") - moved)
    for piece, size, flip, offset, row in entries:
        quarter = flip(core) - 1 if moved else me ^ flip(core)
        lead = pl.multiple_of(quarter * share + offset(core), size)
        rows = pl.ds(pl.multiple_of(row(me), size), size)
        total = total + jnp.dot(
            att_ref[:, pl.ds(lead, size)], piece_refs[piece][rows, :], preferred_element_type=F32
        )
    return total


def arrive_kernel(owners, entries, *refs):
    row_refs, piece_refs, (att_ref, hidden_ref) = refs[:owners], refs[owners:-2], refs[-2:]
    row_refs = row_refs[:1] + row_refs[:0:-1]
    wide = att_ref.shape[1]
    att_ref[...] = stack([ref[:, :wide] for ref in row_refs])
    hidden = jnp.concatenate([ref[:, wide:].astype(F32) for ref in row_refs], axis=0)
    hidden_ref[...] = project(hidden, att_ref, entries, piece_refs, True)


def expert_kernel(entries, count, gain_ref, gate_ref, up_ref, down_ref, att_ref, part_ref, *refs):
    piece_refs, out_refs = refs[:count], refs[count:]
    hidden = project(part_ref[...], att_ref, entries, piece_refs, True)
    mean = jnp.mean(hidden * hidden, axis=1, keepdims=True)
    normed = (hidden * lax.rsqrt(mean + 1e-06) * gain_ref[...]).astype(BF16)
    gate = jnp.dot(normed, gate_ref[...], preferred_element_type=F32)
    up = jnp.dot(normed, up_ref[...], preferred_element_type=F32)
    act = (gate / (1.0 + jnp.exp(-gate)) * up).astype(BF16)
    out = jnp.dot(act, down_ref[...], preferred_element_type=F32)
    for step, ref in enumerate(out_refs):
        ref[...] = out[step * CAP : (step + 1) * CAP, :].astype(BF16)


def project_kernel(entries, att_ref, res_ref, *refs):
    hidden = res_ref[...].astype(F32)
    refs[-1][...] = project(hidden, att_ref, entries, refs[:-1], False)


def combine_kernel(owners, hidden_ref, mix_ref, *refs):
    row_refs, out_ref = refs[:1] + refs[owners - 1 : 0 : -1], refs[owners]
    rows = stack([ref[...] for ref in row_refs])
    mix = mix_ref[...]
    high = mix.astype(BF16)
    low = (mix - high.astype(F32)).astype(BF16)
    total = hidden_ref[...]
    for part in (high, low):
        total = total + lax.dot_general(
            part, rows, (((0,), (0,)), ((), ())), preferred_element_type=F32
        )
    out_ref[...] = total.astype(BF16)


def call(kernel, outs, args, micros, scratch=(), limit=24, free_in=0, free_out=0):
    vmem, free = pl.BlockSpec(memory_space=pltpu.VMEM), pl.BlockSpec(memory_space=pl.ANY)
    nbytes = sum(math.prod(a.shape) * a.dtype.itemsize for a in list(args) + list(outs))
    return pl.pallas_call(
        kernel,
        out_shape=outs,
        in_specs=[vmem] * (len(args) - free_in) + [free] * free_in,
        out_specs=[vmem] * (len(outs) - free_out) + [free] * free_out,
        scratch_shapes=list(scratch),
        compiler_params=pltpu.CompilerParams(vmem_limit_bytes=limit << 20),
        cost_estimate=pl.CostEstimate(
            flops=int(micros * 1.15e9), bytes_accessed=nbytes, transcendentals=0
        ),
    )(*args)


def exchange(blocks):
    count = len(blocks)
    return [blocks[0]] + [
        lax.ppermute(blocks[s], "exp", [(i, i ^ s) for i in range(count)])
        for s in range(count - 1, 0, -1)
    ]


def gather_weight(weight, first, second, attended):
    n_ctx, cores = lax.axis_size("ctx"), lax.axis_size("dp")
    share = weight.shape[0]
    if (n_ctx, cores) != (4, 2):
        whole = lax.all_gather(weight, "ctx", axis=0, tiled=True)
        entries = [
            (0, share, lambda core, f=f: f, lambda core: 0, lambda me, f=f: (me ^ f) * share)
            for f in range(n_ctx)
        ]
        return [whole], entries
    both = ("ctx", "dp")
    devices = [(me, core) for me in range(n_ctx) for core in range(cores)]
    aside = [(me * 2 + core, (me ^ (1 + core)) * 2 + core) for me, core in devices]
    across = [(me * 2 + core, (me ^ (2 - core)) * 2 + core) for me, core in devices]
    near_first = lax.ppermute(first, both, aside)
    near_second = lax.ppermute(after(second, attended), both, aside)
    near_first = after(near_first, attended)
    far = lax.ppermute(near_first, both, across)
    (near,) = call(
        join_kernel,
        [jax.ShapeDtypeStruct(weight.shape, BF16)],
        [near_first, near_second, attended],
        micros=1,
        free_in=3,
        free_out=1,
        limit=1,
        scratch=[pltpu.SemaphoreType.DMA((2,))],
    )
    swap = [(0, 1), (1, 0)]
    pieces = [weight, near, far, lax.ppermute(near, "dp", swap), lax.ppermute(far, "dp", swap)]
    half = share // 2
    first_row = lambda me: 0
    entries = [
        (0, share, lambda core: 0, lambda core: 0, first_row),
        (1, share, lambda core: 1 + core, lambda core: 0, first_row),
        (2, half, lambda core: 3, lambda core: core * half, first_row),
        (3, share, lambda core: 2 - core, lambda core: 0, first_row),
        (4, half, lambda core: 3, lambda core: (1 - core) * half, first_row),
    ]
    return pieces, entries


def per_device(
    queries,
    keys,
    values,
    segments,
    residual,
    out_weight,
    gain,
    expert_ids,
    route_weights,
    w_gate,
    w_up,
    w_down,
):
    tok_rows = queries.shape[1]
    width = residual.shape[2]
    att_width = queries.shape[2]
    n_ctx, owners = lax.axis_size("ctx"), lax.axis_size("exp")
    slots = owners * CAP
    moved_width = att_width - out_weight.shape[0]
    longest = segments.shape[1] // 2
    back_count = min(n_ctx - 1, -(-(longest - 1) // tok_rows))
    shape = jax.ShapeDtypeStruct

    own_kv = jnp.concatenate([keys[0], values[0]], axis=1)
    kv_blocks = []
    for back in range(1, back_count + 1):
        pairs = [(i, (i + back) % n_ctx) for i in range(n_ctx)]
        kv_blocks.append(lax.ppermute(own_kv, "ctx", pairs))
    (mark,) = call(mark_kernel, [shape((8, 128), F32)], [own_kv], micros=5, free_in=1, limit=1)
    half = shape((out_weight.shape[0] // 2, width), BF16)
    accum, row_max, row_sum, stacked, first, second = call(
        functools.partial(own_kernel, n_ctx),
        [
            shape((KVH, GROUPS, tok_rows, HD), F32),
            shape((KVH, GROUPS, tok_rows, HD), F32),
            shape((KVH, GROUPS, tok_rows, HD), F32),
            shape((KVH, GROUPS * tok_rows, HD), BF16),
            half,
            half,
        ],
        [queries[0], own_kv, segments, mark, out_weight],
        micros=3,
        free_in=1,
        free_out=2,
        scratch=[pltpu.SemaphoreType.DMA((2,))],
    )
    place, mix, res_rows = call(
        route_kernel,
        [
            shape((slots, tok_rows), BF16),
            shape((slots, tok_rows), F32),
            shape((slots, width), F32),
        ],
        [expert_ids[0].T, route_weights[0].T, residual[0]],
        micros=1,
    )
    attended, *routed = call(
        functools.partial(rest_kernel, n_ctx, back_count),
        [shape((tok_rows, att_width), BF16)]
        + [shape((CAP, moved_width + width), BF16)] * owners,
        [segments, accum, row_max, row_sum, stacked, place, res_rows, out_weight, *kv_blocks]
        + [gain[None, :], w_gate[0], w_up[0], w_down[0]],
        micros=5,
        scratch=[pltpu.VMEM((slots, att_width), F32)],
    )
    pieces, entries = gather_weight(out_weight, first, second, attended)
    early = pieces[1:2]
    late = pieces[2:] or pieces
    now = [(0, *entry[1:]) for entry in entries[1:] if early and entry[0] == 1]
    skipped = len(pieces) - len(late)
    then = [(entry[0] - skipped, *entry[1:]) for entry in entries[1:] if entry[0] >= skipped]
    arrived, part = call(
        functools.partial(arrive_kernel, owners, now),
        [shape((slots, moved_width), BF16), shape((slots, width), F32)],
        [*exchange(routed), *early],
        micros=10,
    )
    done = call(
        functools.partial(expert_kernel, then, len(late)),
        [shape((CAP, width), BF16)] * owners,
        [gain[None, :], w_gate[0], w_up[0], w_down[0], arrived, part, *late],
        micros=2,
    )
    back = exchange(done)
    (hidden,) = call(
        functools.partial(project_kernel, entries),
        [shape((tok_rows, width), F32)],
        [attended, residual[0], *pieces],
        micros=2,
    )
    (out,) = call(
        functools.partial(combine_kernel, owners),
        [shape((tok_rows, width), BF16)],
        [hidden, mix, *back],
        micros=1,
    )
    return out[None]


def solution(mesh):
    return jax.shard_map(
        per_device,
        mesh=mesh,
        in_specs=(
            P(("dp", "exp"), "ctx", None),
            P(("dp", "exp"), "ctx", None),
            P(("dp", "exp"), "ctx", None),
            P(("dp", "exp"), None),
            P(("dp", "exp"), "ctx", None),
            P("ctx", None),
            P(),
            P(("dp", "exp"), "ctx", None),
            P(("dp", "exp"), "ctx", None),
            P("exp", None, None),
            P("exp", None, None),
            P("exp", None, None),
        ),
        out_specs=P(("dp", "exp"), "ctx", None),
        check_vma=False,
    )
```

```python
import functools
import math

import jax
import jax.numpy as jnp
from jax import lax
from jax.experimental import pallas as pl
from jax.experimental.pallas import tpu as pltpu
from jax.sharding import PartitionSpec as P

HQ = 16
KVH = 2
HD = 128
GROUPS = HQ // KVH
CAP = 24
NEG = -1e30
SCORE_SCALE = math.log2(math.e) / math.sqrt(HD)
F32 = jnp.float32
BF16 = jnp.bfloat16


def slab_segments(segs_ref, index, count, rows):
    found = segs_ref[:, 0:rows]
    for slab in range(1, count):
        found = jnp.where(index == slab, segs_ref[:, slab * rows : (slab + 1) * rows], found)
    return found


def score_bias(segs_ref, backs, count, rows):
    me = lax.axis_index("ctx")
    row = lax.broadcasted_iota(jnp.int32, (rows, rows), 0)
    col = lax.broadcasted_iota(jnp.int32, (rows, rows), 1)
    own_seg = slab_segments(segs_ref, me, count, rows)
    query_seg = jnp.sum(jnp.where(row == col, own_seg, 0), axis=1, keepdims=True)
    parts = []
    for back in backs:
        if back == 0:
            allowed = (col <= row) & (own_seg == query_seg)
        else:
            key_seg = slab_segments(segs_ref, jnp.maximum(me - back, 0), count, rows)
            allowed = (key_seg == query_seg) & (me >= back)
        parts.append(jnp.where(allowed, 0.0, NEG))
    return parts


def group_scores(stacked, keys, bias):
    scores = lax.dot_general(
        stacked, keys, (((1,), (1,)), ((), ())), preferred_element_type=F32
    )
    return scores.reshape(GROUPS, *bias.shape) * SCORE_SCALE + bias


def weigh(expo, values):
    rows = expo.shape[0] * expo.shape[1]
    mixed = jnp.dot(
        expo.astype(BF16).reshape(rows, expo.shape[2]), values, preferred_element_type=F32
    ).reshape(*expo.shape[:2], 2 * HD)
    return mixed[:, :, :HD], mixed[:, :, HD:]


def mark_kernel(*refs):
    refs[-1][...] = jnp.zeros_like(refs[-1])


def gate_kernel(*refs):
    del refs


def after(piece, *marks):
    spec = pl.BlockSpec(memory_space=pl.ANY)
    return pl.pallas_call(
        gate_kernel,
        out_shape=jax.ShapeDtypeStruct(piece.shape, piece.dtype),
        in_specs=[spec] * (1 + len(marks)),
        out_specs=spec,
        input_output_aliases={0: 0},
        compiler_params=pltpu.CompilerParams(vmem_limit_bytes=1 << 20),
    )(piece, *marks)


def join_kernel(first_ref, second_ref, mark_ref, whole_ref, sems):
    del mark_ref
    half = first_ref.shape[0]
    core = lax.rem(lax.axis_index("dp"), 2)
    copies = []
    for index, (lead, ref) in enumerate([(core, first_ref), (1 - core, second_ref)]):
        target = whole_ref.at[pl.ds(pl.multiple_of(lead * half, half), half)]
        copies.append(pltpu.make_async_copy(ref, target, sems.at[index]))
        copies[-1].start()
    for copy in copies:
        copy.wait()


def own_kernel(
    n_ctx,
    q_ref,
    kv_ref,
    segs_ref,
    mark_ref,
    w_ref,
    acc_ref,
    max_ref,
    sum_ref,
    queries_ref,
    first_ref,
    second_ref,
    sems,
):
    del mark_ref
    half = first_ref.shape[0]
    core = lax.rem(lax.axis_index("dp"), 2)
    copies = []
    for index, (lead, ref) in enumerate([(core, first_ref), (1 - core, second_ref)]):
        source = w_ref.at[pl.ds(pl.multiple_of(lead * half, half), half)]
        copies.append(pltpu.make_async_copy(source, ref, sems.at[index]))
        copies[-1].start()
    rows = q_ref.shape[0]
    (bias,) = score_bias(segs_ref, (0,), n_ctx, rows)
    ones = jnp.ones((rows, HD), BF16)
    for kv in range(KVH):
        keys = kv_ref[:, kv * HD : (kv + 1) * HD]
        values = jnp.concatenate([kv_ref[:, (KVH + kv) * HD : (KVH + kv + 1) * HD], ones], axis=1)
        heads = range(kv * GROUPS, (kv + 1) * GROUPS)
        stacked = jnp.concatenate([q_ref[:, h * HD : (h + 1) * HD] for h in heads], axis=0)
        queries_ref[kv] = stacked
        scores = group_scores(stacked, keys, bias)
        row_max = jnp.max(scores, axis=2, keepdims=True)
        accum, row_sum = weigh(jnp.exp2(scores - row_max), values)
        acc_ref[kv] = accum
        max_ref[kv] = jnp.broadcast_to(row_max, max_ref.shape[1:])
        sum_ref[kv] = row_sum
    for copy in copies:
        copy.wait()


def route_kernel(ids_ref, rw_ref, res_ref, place_ref, mix_ref, rows_ref):
    slots, rows = place_ref.shape
    slot = lax.broadcasted_iota(jnp.int32, (slots, rows), 0)
    owner = (slot // CAP) ^ lax.axis_index("exp")
    hit = jnp.zeros((slots, rows), jnp.bool_)
    weight = jnp.zeros((slots, rows), F32)
    for choice in range(ids_ref.shape[0]):
        same = ids_ref[choice : choice + 1, :] == owner
        hit = hit | same
        weight = jnp.where(same, rw_ref[choice : choice + 1, :], weight)
    row = lax.broadcasted_iota(jnp.int32, (rows, rows), 0)
    col = lax.broadcasted_iota(jnp.int32, (rows, rows), 1)
    before = (row < col).astype(F32).astype(BF16)
    rank = jnp.dot(hit.astype(F32).astype(BF16), before, preferred_element_type=F32)
    placed = hit & (rank == lax.rem(slot, CAP).astype(F32))
    place = placed.astype(F32).astype(BF16)
    place_ref[...] = place
    mix = jnp.where(placed, weight, 0.0)
    high = mix.astype(BF16).astype(F32)
    mix_ref[...] = jnp.concatenate([high, mix - high], axis=0).T.astype(BF16)
    rows_ref[...] = jnp.dot(place, res_ref[...], preferred_element_type=F32)


def rest_kernel(
    n_ctx,
    back_count,
    segs_ref,
    acc_ref,
    max_ref,
    sum_ref,
    queries_ref,
    place_ref,
    rows_ref,
    w_ref,
    *refs,
):
    kv_refs, refs = refs[:back_count], refs[back_count + 4 :]
    out_ref, *send_refs = refs[:-1]
    routed_ref = refs[-1]
    rows = queries_ref.shape[1] // GROUPS
    bias = jnp.concatenate(score_bias(segs_ref, range(1, back_count + 1), n_ctx, rows), axis=1)
    keys_count = rows * back_count
    spread = -(-keys_count // HD)
    ones = jnp.ones((keys_count, HD), BF16)
    scores = []
    for kv in range(KVH):
        keys = jnp.concatenate([ref[:, kv * HD : (kv + 1) * HD] for ref in kv_refs], axis=0)
        scores.append(group_scores(queries_ref[kv], keys, bias))
    for kv in range(KVH):
        values = jnp.concatenate(
            [ref[:, (KVH + kv) * HD : (KVH + kv + 1) * HD] for ref in kv_refs], axis=0
        )
        values = jnp.concatenate([values, ones], axis=1)
        old_max = max_ref[kv]
        new_max = jnp.maximum(old_max, jnp.max(scores[kv], axis=2, keepdims=True))
        shift = jnp.concatenate([new_max] * spread, axis=2)[:, :, :keys_count]
        accum, row_sum = weigh(jnp.exp2(scores[kv] - shift), values)
        fix = jnp.exp2(old_max - new_max)
        total = sum_ref[kv] * fix + row_sum
        attended = ((acc_ref[kv] * fix + accum) / total).astype(BF16)
        for group in range(GROUPS):
            head = kv * GROUPS + group
            out_ref[:, head * HD : (head + 1) * HD] = attended[group]
    routed_ref[...] = jnp.dot(place_ref[...], out_ref[...], preferred_element_type=F32)
    me, share = lax.axis_index("ctx"), w_ref.shape[0]

    def quarter(flip):
        return routed_ref[:, pl.ds(pl.multiple_of((me ^ flip) * share, share), share)]

    part = rows_ref[...] + jnp.dot(
        quarter(0).astype(BF16), w_ref[...], preferred_element_type=F32
    )
    blocks = [quarter(flip) for flip in range(1, n_ctx)] + [part]
    for step, ref in enumerate(send_refs):
        for place, block in enumerate(blocks):
            ref[:, place * share : place * share + block.shape[1]] = block[
                step * CAP : (step + 1) * CAP, :
            ].astype(BF16)


def stack(parts):
    return jnp.concatenate([part.astype(F32) for part in parts], axis=0).astype(BF16)


def project(total, att_ref, entries, piece_refs, moved):
    me, core = lax.axis_index("ctx"), lax.axis_index("dp")
    share = att_ref.shape[1] // (lax.axis_size("ctx") - moved)
    for piece, size, flip, offset, row in entries:
        quarter = flip(core) - 1 if moved else me ^ flip(core)
        lead = pl.multiple_of(quarter * share + offset(core), size)
        rows = pl.ds(pl.multiple_of(row(me), size), size)
        total = total + jnp.dot(
            att_ref[:, pl.ds(lead, size)], piece_refs[piece][rows, :], preferred_element_type=F32
        )
    return total


def arrive_kernel(owners, entries, *refs):
    row_refs, piece_refs, (att_ref, hidden_ref) = refs[:owners], refs[owners:-2], refs[-2:]
    row_refs = row_refs[:1] + row_refs[:0:-1]
    wide = att_ref.shape[1]
    att_ref[...] = stack([ref[:, :wide] for ref in row_refs])
    hidden = jnp.concatenate([ref[:, wide:].astype(F32) for ref in row_refs], axis=0)
    hidden_ref[...] = project(hidden, att_ref, entries, piece_refs, True)


def expert_kernel(entries, count, gain_ref, gate_ref, up_ref, down_ref, att_ref, part_ref, *refs):
    piece_refs, out_refs = refs[:count], refs[count:]
    hidden = project(part_ref[...], att_ref, entries, piece_refs, True)
    mean = jnp.mean(hidden * hidden, axis=1, keepdims=True)
    normed = (hidden * lax.rsqrt(mean + 1e-06) * gain_ref[...]).astype(BF16)
    gate = jnp.dot(normed, gate_ref[...], preferred_element_type=F32)
    up = jnp.dot(normed, up_ref[...], preferred_element_type=F32)
    act = (gate / (1.0 + jnp.exp(-gate)) * up).astype(BF16)
    out = jnp.dot(act, down_ref[...], preferred_element_type=F32)
    for step, ref in enumerate(out_refs):
        ref[...] = out[step * CAP : (step + 1) * CAP, :].astype(BF16)


def project_kernel(entries, att_ref, res_ref, *refs):
    hidden = res_ref[...].astype(F32)
    refs[-1][...] = project(hidden, att_ref, entries, refs[:-1], False)


def combine_kernel(owners, hidden_ref, mix_ref, *refs):
    row_refs, out_ref = refs[:1] + refs[owners - 1 : 0 : -1], refs[owners]
    rows = stack([ref[...] for ref in row_refs])
    total = hidden_ref[...] + jnp.dot(
        mix_ref[...], jnp.concatenate([rows, rows], axis=0), preferred_element_type=F32
    )
    out_ref[...] = total.astype(BF16)


def call(kernel, outs, args, micros, scratch=(), limit=24, free_in=0, free_out=0):
    vmem, free = pl.BlockSpec(memory_space=pltpu.VMEM), pl.BlockSpec(memory_space=pl.ANY)
    nbytes = sum(math.prod(a.shape) * a.dtype.itemsize for a in list(args) + list(outs))
    return pl.pallas_call(
        kernel,
        out_shape=outs,
        in_specs=[vmem] * (len(args) - free_in) + [free] * free_in,
        out_specs=[vmem] * (len(outs) - free_out) + [free] * free_out,
        scratch_shapes=list(scratch),
        compiler_params=pltpu.CompilerParams(vmem_limit_bytes=limit << 20),
        cost_estimate=pl.CostEstimate(
            flops=int(micros * 1.15e9), bytes_accessed=nbytes, transcendentals=0
        ),
    )(*args)


def exchange(blocks):
    count = len(blocks)
    return [blocks[0]] + [
        lax.ppermute(blocks[s], "exp", [(i, i ^ s) for i in range(count)])
        for s in range(count - 1, 0, -1)
    ]


def gather_weight(weight, first, second, arrived, attended):
    n_ctx, cores = lax.axis_size("ctx"), lax.axis_size("dp")
    share = weight.shape[0]
    if (n_ctx, cores) != (4, 2):
        whole = lax.all_gather(weight, "ctx", axis=0, tiled=True)
        entries = [
            (0, share, lambda core, f=f: f, lambda core: 0, lambda me, f=f: (me ^ f) * share)
            for f in range(n_ctx)
        ]
        return [whole], entries
    both = ("ctx", "dp")
    devices = [(me, core) for me in range(n_ctx) for core in range(cores)]
    aside = [(me * 2 + core, (me ^ (1 + core)) * 2 + core) for me, core in devices]
    across = [(me * 2 + core, (me ^ (2 - core)) * 2 + core) for me, core in devices]
    near_first = lax.ppermute(first, both, aside)
    near_second = lax.ppermute(after(second, *arrived), both, aside)
    near_first = after(near_first, attended)
    far = lax.ppermute(near_first, both, across)
    (near,) = call(
        join_kernel,
        [jax.ShapeDtypeStruct(weight.shape, BF16)],
        [near_first, near_second, attended],
        micros=1,
        free_in=3,
        free_out=1,
        limit=1,
        scratch=[pltpu.SemaphoreType.DMA((2,))],
    )
    swap = [(0, 1), (1, 0)]
    pieces = [weight, near, far, lax.ppermute(near, "dp", swap), lax.ppermute(far, "dp", swap)]
    half = share // 2
    first_row = lambda me: 0
    entries = [
        (0, share, lambda core: 0, lambda core: 0, first_row),
        (1, share, lambda core: 1 + core, lambda core: 0, first_row),
        (2, half, lambda core: 3, lambda core: core * half, first_row),
        (3, share, lambda core: 2 - core, lambda core: 0, first_row),
        (4, half, lambda core: 3, lambda core: (1 - core) * half, first_row),
    ]
    return pieces, entries


def per_device(
    queries,
    keys,
    values,
    segments,
    residual,
    out_weight,
    gain,
    expert_ids,
    route_weights,
    w_gate,
    w_up,
    w_down,
):
    tok_rows = queries.shape[1]
    width = residual.shape[2]
    att_width = queries.shape[2]
    n_ctx, owners = lax.axis_size("ctx"), lax.axis_size("exp")
    slots = owners * CAP
    moved_width = att_width - out_weight.shape[0]
    longest = segments.shape[1] // 2
    back_count = min(n_ctx - 1, -(-(longest - 1) // tok_rows))
    shape = jax.ShapeDtypeStruct

    own_kv = jnp.concatenate([keys[0], values[0]], axis=1)
    kv_blocks = []
    for back in range(1, back_count + 1):
        pairs = [(i, (i + back) % n_ctx) for i in range(n_ctx)]
        kv_blocks.append(lax.ppermute(own_kv, "ctx", pairs))
    (mark,) = call(mark_kernel, [shape((8, 128), F32)], [own_kv], micros=5, free_in=1, limit=1)
    half = shape((out_weight.shape[0] // 2, width), BF16)
    accum, row_max, row_sum, stacked, first, second = call(
        functools.partial(own_kernel, n_ctx),
        [
            shape((KVH, GROUPS, tok_rows, HD), F32),
            shape((KVH, GROUPS, tok_rows, HD), F32),
            shape((KVH, GROUPS, tok_rows, HD), F32),
            shape((KVH, GROUPS * tok_rows, HD), BF16),
            half,
            half,
        ],
        [queries[0], own_kv, segments, mark, out_weight],
        micros=3,
        free_in=1,
        free_out=2,
        scratch=[pltpu.SemaphoreType.DMA((2,))],
    )
    place, mix, res_rows = call(
        route_kernel,
        [
            shape((slots, tok_rows), BF16),
            shape((tok_rows, 2 * slots), BF16),
            shape((slots, width), F32),
        ],
        [expert_ids[0].T, route_weights[0].T, residual[0]],
        micros=1,
    )
    attended, *routed = call(
        functools.partial(rest_kernel, n_ctx, back_count),
        [shape((tok_rows, att_width), BF16)]
        + [shape((CAP, moved_width + width), BF16)] * owners,
        [segments, accum, row_max, row_sum, stacked, place, res_rows, out_weight, *kv_blocks]
        + [gain[None, :], w_gate[0], w_up[0], w_down[0]],
        micros=5,
        scratch=[pltpu.VMEM((slots, att_width), F32)],
    )
    pieces, entries = gather_weight(out_weight, first, second, kv_blocks, attended)
    early = pieces[1:2]
    late = pieces[2:] or pieces
    now = [(0, *entry[1:]) for entry in entries[1:] if early and entry[0] == 1]
    skipped = len(pieces) - len(late)
    then = [(entry[0] - skipped, *entry[1:]) for entry in entries[1:] if entry[0] >= skipped]
    arrived, part = call(
        functools.partial(arrive_kernel, owners, now),
        [shape((slots, moved_width), BF16), shape((slots, width), F32)],
        [*exchange(routed), *early],
        micros=10,
    )
    done = call(
        functools.partial(expert_kernel, then, len(late)),
        [shape((CAP, width), BF16)] * owners,
        [gain[None, :], w_gate[0], w_up[0], w_down[0], arrived, part, *late],
        micros=2,
    )
    back = exchange(done)
    (hidden,) = call(
        functools.partial(project_kernel, entries),
        [shape((tok_rows, width), F32)],
        [attended, residual[0], *pieces],
        micros=2,
    )
    (out,) = call(
        functools.partial(combine_kernel, owners),
        [shape((tok_rows, width), BF16)],
        [hidden, mix, *back],
        micros=1,
    )
    return out[None]


def solution(mesh):
    return jax.shard_map(
        per_device,
        mesh=mesh,
        in_specs=(
            P(("dp", "exp"), "ctx", None),
            P(("dp", "exp"), "ctx", None),
            P(("dp", "exp"), "ctx", None),
            P(("dp", "exp"), None),
            P(("dp", "exp"), "ctx", None),
            P("ctx", None),
            P(),
            P(("dp", "exp"), "ctx", None),
            P(("dp", "exp"), "ctx", None),
            P("exp", None, None),
            P("exp", None, None),
            P("exp", None, None),
        ),
        out_specs=P(("dp", "exp"), "ctx", None),
        check_vma=False,
    )
```

```python
import functools
import math

import jax
import jax.numpy as jnp
from jax import lax
from jax.experimental import pallas as pl
from jax.experimental.pallas import tpu as pltpu
from jax.sharding import PartitionSpec as P

HQ = 16
KVH = 2
HD = 128
GROUPS = HQ // KVH
CAP = 24
NEG = -1e30
SCORE_SCALE = math.log2(math.e) / math.sqrt(HD)
F32 = jnp.float32
BF16 = jnp.bfloat16


def slab_segments(segs_ref, index, count, rows):
    found = segs_ref[:, 0:rows]
    for slab in range(1, count):
        found = jnp.where(index == slab, segs_ref[:, slab * rows : (slab + 1) * rows], found)
    return found


def score_bias(segs_ref, backs, count, rows):
    me = lax.axis_index("ctx")
    row = lax.broadcasted_iota(jnp.int32, (rows, rows), 0)
    col = lax.broadcasted_iota(jnp.int32, (rows, rows), 1)
    own_seg = slab_segments(segs_ref, me, count, rows)
    query_seg = jnp.sum(jnp.where(row == col, own_seg, 0), axis=1, keepdims=True)
    parts = []
    for back in backs:
        if back == 0:
            allowed = (col <= row) & (own_seg == query_seg)
        else:
            key_seg = slab_segments(segs_ref, jnp.maximum(me - back, 0), count, rows)
            allowed = (key_seg == query_seg) & (me >= back)
        parts.append(jnp.where(allowed, 0.0, NEG))
    return parts


def group_scores(stacked, keys, bias):
    scores = lax.dot_general(
        stacked, keys, (((1,), (1,)), ((), ())), preferred_element_type=F32
    )
    return scores.reshape(GROUPS, *bias.shape) * SCORE_SCALE + bias


def weigh(expo, values):
    rows = expo.shape[0] * expo.shape[1]
    mixed = jnp.dot(
        expo.astype(BF16).reshape(rows, expo.shape[2]), values, preferred_element_type=F32
    ).reshape(*expo.shape[:2], 2 * HD)
    return mixed[:, :, :HD], mixed[:, :, HD:]


def mark_kernel(*refs):
    refs[-1][...] = jnp.zeros_like(refs[-1])


def gate_kernel(*refs):
    del refs


def after(piece, *marks):
    spec = pl.BlockSpec(memory_space=pl.ANY)
    return pl.pallas_call(
        gate_kernel,
        out_shape=jax.ShapeDtypeStruct(piece.shape, piece.dtype),
        in_specs=[spec] * (1 + len(marks)),
        out_specs=spec,
        input_output_aliases={0: 0},
        compiler_params=pltpu.CompilerParams(vmem_limit_bytes=1 << 20),
    )(piece, *marks)


def join_kernel(first_ref, second_ref, mark_ref, whole_ref, sems):
    del mark_ref
    half = first_ref.shape[0]
    core = lax.rem(lax.axis_index("dp"), 2)
    copies = []
    for index, (lead, ref) in enumerate([(core, first_ref), (1 - core, second_ref)]):
        target = whole_ref.at[pl.ds(pl.multiple_of(lead * half, half), half)]
        copies.append(pltpu.make_async_copy(ref, target, sems.at[index]))
        copies[-1].start()
    for copy in copies:
        copy.wait()


def own_kernel(
    n_ctx,
    q_ref,
    kv_ref,
    segs_ref,
    mark_ref,
    w_ref,
    acc_ref,
    max_ref,
    sum_ref,
    queries_ref,
    first_ref,
    second_ref,
    sems,
):
    del mark_ref
    half = first_ref.shape[0]
    core = lax.rem(lax.axis_index("dp"), 2)
    copies = []
    for index, (lead, ref) in enumerate([(core, first_ref), (1 - core, second_ref)]):
        source = w_ref.at[pl.ds(pl.multiple_of(lead * half, half), half)]
        copies.append(pltpu.make_async_copy(source, ref, sems.at[index]))
        copies[-1].start()
    rows = q_ref.shape[0]
    (bias,) = score_bias(segs_ref, (0,), n_ctx, rows)
    ones = jnp.ones((rows, HD), BF16)
    for kv in range(KVH):
        keys = kv_ref[:, kv * HD : (kv + 1) * HD]
        values = jnp.concatenate([kv_ref[:, (KVH + kv) * HD : (KVH + kv + 1) * HD], ones], axis=1)
        heads = range(kv * GROUPS, (kv + 1) * GROUPS)
        stacked = jnp.concatenate([q_ref[:, h * HD : (h + 1) * HD] for h in heads], axis=0)
        queries_ref[kv] = stacked
        scores = group_scores(stacked, keys, bias)
        row_max = jnp.max(scores, axis=2, keepdims=True)
        accum, row_sum = weigh(jnp.exp2(scores - row_max), values)
        acc_ref[kv] = accum
        max_ref[kv] = jnp.broadcast_to(row_max, max_ref.shape[1:])
        sum_ref[kv] = row_sum
    for copy in copies:
        copy.wait()


def route_kernel(ids_ref, rw_ref, res_ref, place_ref, mix_ref, rows_ref):
    slots, rows = place_ref.shape
    slot = lax.broadcasted_iota(jnp.int32, (slots, rows), 0)
    owner = (slot // CAP) ^ lax.axis_index("exp")
    hit = jnp.zeros((slots, rows), jnp.bool_)
    weight = jnp.zeros((slots, rows), F32)
    for choice in range(ids_ref.shape[0]):
        same = ids_ref[choice : choice + 1, :] == owner
        hit = hit | same
        weight = jnp.where(same, rw_ref[choice : choice + 1, :], weight)
    row = lax.broadcasted_iota(jnp.int32, (rows, rows), 0)
    col = lax.broadcasted_iota(jnp.int32, (rows, rows), 1)
    before = (row < col).astype(F32).astype(BF16)
    rank = jnp.dot(hit.astype(F32).astype(BF16), before, preferred_element_type=F32)
    placed = hit & (rank == lax.rem(slot, CAP).astype(F32))
    place = placed.astype(F32).astype(BF16)
    place_ref[...] = place
    mix = jnp.where(placed, weight, 0.0)
    high = mix.astype(BF16).astype(F32)
    mix_ref[...] = jnp.concatenate([high, mix - high], axis=0).T.astype(BF16)
    rows_ref[...] = jnp.dot(place, res_ref[...], preferred_element_type=F32)


def rest_kernel(
    n_ctx,
    back_count,
    segs_ref,
    acc_ref,
    max_ref,
    sum_ref,
    queries_ref,
    place_ref,
    rows_ref,
    w_ref,
    *refs,
):
    kv_refs, refs = refs[:back_count], refs[back_count + 4 :]
    out_ref, *send_refs = refs[:-1]
    routed_ref = refs[-1]
    rows = queries_ref.shape[1] // GROUPS
    bias = jnp.concatenate(score_bias(segs_ref, range(1, back_count + 1), n_ctx, rows), axis=1)
    keys_count = rows * back_count
    spread = -(-keys_count // HD)
    ones = jnp.ones((keys_count, HD), BF16)
    scores = []
    for kv in range(KVH):
        keys = jnp.concatenate([ref[:, kv * HD : (kv + 1) * HD] for ref in kv_refs], axis=0)
        scores.append(group_scores(queries_ref[kv], keys, bias))
    for kv in range(KVH):
        values = jnp.concatenate(
            [ref[:, (KVH + kv) * HD : (KVH + kv + 1) * HD] for ref in kv_refs], axis=0
        )
        values = jnp.concatenate([values, ones], axis=1)
        old_max = max_ref[kv]
        new_max = jnp.maximum(old_max, jnp.max(scores[kv], axis=2, keepdims=True))
        shift = jnp.concatenate([new_max] * spread, axis=2)[:, :, :keys_count]
        accum, row_sum = weigh(jnp.exp2(scores[kv] - shift), values)
        fix = jnp.exp2(old_max - new_max)
        total = sum_ref[kv] * fix + row_sum
        attended = ((acc_ref[kv] * fix + accum) / total).astype(BF16)
        for group in range(GROUPS):
            head = kv * GROUPS + group
            out_ref[:, head * HD : (head + 1) * HD] = attended[group]
    routed_ref[...] = jnp.dot(place_ref[...], out_ref[...], preferred_element_type=F32)
    me, share = lax.axis_index("ctx"), w_ref.shape[0]

    def quarter(flip):
        return routed_ref[:, pl.ds(pl.multiple_of((me ^ flip) * share, share), share)]

    part = rows_ref[...] + jnp.dot(
        quarter(0).astype(BF16), w_ref[...], preferred_element_type=F32
    )
    blocks = [quarter(flip) for flip in range(1, n_ctx)] + [part]
    for step, ref in enumerate(send_refs):
        for place, block in enumerate(blocks):
            ref[:, place * share : place * share + block.shape[1]] = block[
                step * CAP : (step + 1) * CAP, :
            ].astype(BF16)


def stack(parts):
    return jnp.concatenate([part.astype(F32) for part in parts], axis=0).astype(BF16)


def project(total, att_ref, entries, piece_refs, moved):
    me, core = lax.axis_index("ctx"), lax.axis_index("dp")
    share = att_ref.shape[1] // (lax.axis_size("ctx") - moved)
    for piece, size, flip, offset, row in entries:
        quarter = flip(core) - 1 if moved else me ^ flip(core)
        lead = pl.multiple_of(quarter * share + offset(core), size)
        rows = pl.ds(pl.multiple_of(row(me), size), size)
        total = total + jnp.dot(
            att_ref[:, pl.ds(lead, size)], piece_refs[piece][rows, :], preferred_element_type=F32
        )
    return total


def arrive_kernel(owners, entries, *refs):
    row_refs, piece_refs, (att_ref, hidden_ref) = refs[:owners], refs[owners:-2], refs[-2:]
    row_refs = row_refs[:1] + row_refs[:0:-1]
    wide = att_ref.shape[1]
    att_ref[...] = stack([ref[:, :wide] for ref in row_refs])
    hidden = jnp.concatenate([ref[:, wide:].astype(F32) for ref in row_refs], axis=0)
    hidden_ref[...] = project(hidden, att_ref, entries, piece_refs, True)


def expert_kernel(entries, count, gain_ref, gate_ref, up_ref, down_ref, att_ref, part_ref, *refs):
    piece_refs, out_refs = refs[:count], refs[count:]
    hidden = project(part_ref[...], att_ref, entries, piece_refs, True)
    mean = jnp.mean(hidden * hidden, axis=1, keepdims=True)
    normed = (hidden * lax.rsqrt(mean + 1e-06) * gain_ref[...]).astype(BF16)
    gate = jnp.dot(normed, gate_ref[...], preferred_element_type=F32)
    up = jnp.dot(normed, up_ref[...], preferred_element_type=F32)
    act = (gate / (1.0 + jnp.exp(-gate)) * up).astype(BF16)
    out = jnp.dot(act, down_ref[...], preferred_element_type=F32)
    for step, ref in enumerate(out_refs):
        ref[...] = out[step * CAP : (step + 1) * CAP, :].astype(BF16)


def project_kernel(entries, att_ref, res_ref, *refs):
    hidden = res_ref[...].astype(F32)
    refs[-1][...] = project(hidden, att_ref, entries, refs[:-1], False)


def combine_kernel(owners, hidden_ref, mix_ref, *refs):
    row_refs, out_ref = refs[:1] + refs[owners - 1 : 0 : -1], refs[owners]
    rows = stack([ref[...] for ref in row_refs])
    total = hidden_ref[...] + jnp.dot(
        mix_ref[...], jnp.concatenate([rows, rows], axis=0), preferred_element_type=F32
    )
    out_ref[...] = total.astype(BF16)


def call(kernel, outs, args, micros, scratch=(), limit=24, free_in=0, free_out=0):
    vmem, free = pl.BlockSpec(memory_space=pltpu.VMEM), pl.BlockSpec(memory_space=pl.ANY)
    nbytes = sum(math.prod(a.shape) * a.dtype.itemsize for a in list(args) + list(outs))
    return pl.pallas_call(
        kernel,
        out_shape=outs,
        in_specs=[vmem] * (len(args) - free_in) + [free] * free_in,
        out_specs=[vmem] * (len(outs) - free_out) + [free] * free_out,
        scratch_shapes=list(scratch),
        compiler_params=pltpu.CompilerParams(vmem_limit_bytes=limit << 20),
        cost_estimate=pl.CostEstimate(
            flops=int(micros * 1.15e9), bytes_accessed=nbytes, transcendentals=0
        ),
    )(*args)


def exchange(blocks):
    count = len(blocks)
    return [blocks[0]] + [
        lax.ppermute(blocks[s], "exp", [(i, i ^ s) for i in range(count)])
        for s in range(count - 1, 0, -1)
    ]


def gather_weight(weight, first, second, attended):
    n_ctx, cores = lax.axis_size("ctx"), lax.axis_size("dp")
    share = weight.shape[0]
    if (n_ctx, cores) != (4, 2):
        whole = lax.all_gather(weight, "ctx", axis=0, tiled=True)
        entries = [
            (0, share, lambda core, f=f: f, lambda core: 0, lambda me, f=f: (me ^ f) * share)
            for f in range(n_ctx)
        ]
        return [whole], entries
    both = ("ctx", "dp")
    devices = [(me, core) for me in range(n_ctx) for core in range(cores)]
    aside = [(me * 2 + core, (me ^ (1 + core)) * 2 + core) for me, core in devices]
    across = [(me * 2 + core, (me ^ (2 - core)) * 2 + core) for me, core in devices]
    near_first = lax.ppermute(first, both, aside)
    near_second = lax.ppermute(second, both, aside)
    near_first = after(near_first, attended)
    far = lax.ppermute(near_first, both, across)
    (near,) = call(
        join_kernel,
        [jax.ShapeDtypeStruct(weight.shape, BF16)],
        [near_first, near_second, attended],
        micros=1,
        free_in=3,
        free_out=1,
        limit=1,
        scratch=[pltpu.SemaphoreType.DMA((2,))],
    )
    swap = [(0, 1), (1, 0)]
    pieces = [weight, near, far, lax.ppermute(near, "dp", swap), lax.ppermute(far, "dp", swap)]
    half = share // 2
    first_row = lambda me: 0
    entries = [
        (0, share, lambda core: 0, lambda core: 0, first_row),
        (1, share, lambda core: 1 + core, lambda core: 0, first_row),
        (2, half, lambda core: 3, lambda core: core * half, first_row),
        (3, share, lambda core: 2 - core, lambda core: 0, first_row),
        (4, half, lambda core: 3, lambda core: (1 - core) * half, first_row),
    ]
    return pieces, entries


def per_device(
    queries,
    keys,
    values,
    segments,
    residual,
    out_weight,
    gain,
    expert_ids,
    route_weights,
    w_gate,
    w_up,
    w_down,
):
    tok_rows = queries.shape[1]
    width = residual.shape[2]
    att_width = queries.shape[2]
    n_ctx, owners = lax.axis_size("ctx"), lax.axis_size("exp")
    slots = owners * CAP
    moved_width = att_width - out_weight.shape[0]
    longest = segments.shape[1] // 2
    back_count = min(n_ctx - 1, -(-(longest - 1) // tok_rows))
    shape = jax.ShapeDtypeStruct

    own_kv = jnp.concatenate([keys[0], values[0]], axis=1)
    kv_blocks = []
    for back in range(1, back_count + 1):
        pairs = [(i, (i + back) % n_ctx) for i in range(n_ctx)]
        kv_blocks.append(lax.ppermute(own_kv, "ctx", pairs))
    (mark,) = call(mark_kernel, [shape((8, 128), F32)], [own_kv], micros=5, free_in=1, limit=1)
    half = shape((out_weight.shape[0] // 2, width), BF16)
    accum, row_max, row_sum, stacked, first, second = call(
        functools.partial(own_kernel, n_ctx),
        [
            shape((KVH, GROUPS, tok_rows, HD), F32),
            shape((KVH, GROUPS, tok_rows, HD), F32),
            shape((KVH, GROUPS, tok_rows, HD), F32),
            shape((KVH, GROUPS * tok_rows, HD), BF16),
            half,
            half,
        ],
        [queries[0], own_kv, segments, mark, out_weight],
        micros=3,
        free_in=1,
        free_out=2,
        scratch=[pltpu.SemaphoreType.DMA((2,))],
    )
    place, mix, res_rows = call(
        route_kernel,
        [
            shape((slots, tok_rows), BF16),
            shape((tok_rows, 2 * slots), BF16),
            shape((slots, width), F32),
        ],
        [expert_ids[0].T, route_weights[0].T, residual[0]],
        micros=1,
    )
    attended, *routed = call(
        functools.partial(rest_kernel, n_ctx, back_count),
        [shape((tok_rows, att_width), BF16)]
        + [shape((CAP, moved_width + width), BF16)] * owners,
        [segments, accum, row_max, row_sum, stacked, place, res_rows, out_weight, *kv_blocks]
        + [gain[None, :], w_gate[0], w_up[0], w_down[0]],
        micros=5,
        scratch=[pltpu.VMEM((slots, att_width), F32)],
    )
    pieces, entries = gather_weight(out_weight, first, second, attended)
    early = pieces[1:2]
    late = pieces[2:] or pieces
    now = [(0, *entry[1:]) for entry in entries[1:] if early and entry[0] == 1]
    skipped = len(pieces) - len(late)
    then = [(entry[0] - skipped, *entry[1:]) for entry in entries[1:] if entry[0] >= skipped]
    arrived, part = call(
        functools.partial(arrive_kernel, owners, now),
        [shape((slots, moved_width), BF16), shape((slots, width), F32)],
        [*exchange(routed), *early],
        micros=10,
    )
    done = call(
        functools.partial(expert_kernel, then, len(late)),
        [shape((CAP, width), BF16)] * owners,
        [gain[None, :], w_gate[0], w_up[0], w_down[0], arrived, part, *late],
        micros=2,
    )
    back = exchange(done)
    (hidden,) = call(
        functools.partial(project_kernel, entries),
        [shape((tok_rows, width), F32)],
        [attended, residual[0], *pieces],
        micros=2,
    )
    (out,) = call(
        functools.partial(combine_kernel, owners),
        [shape((tok_rows, width), BF16)],
        [hidden, mix, *back],
        micros=1,
    )
    return out[None]


def solution(mesh):
    return jax.shard_map(
        per_device,
        mesh=mesh,
        in_specs=(
            P(("dp", "exp"), "ctx", None),
            P(("dp", "exp"), "ctx", None),
            P(("dp", "exp"), "ctx", None),
            P(("dp", "exp"), None),
            P(("dp", "exp"), "ctx", None),
            P("ctx", None),
            P(),
            P(("dp", "exp"), "ctx", None),
            P(("dp", "exp"), "ctx", None),
            P("exp", None, None),
            P("exp", None, None),
            P("exp", None, None),
        ),
        out_specs=P(("dp", "exp"), "ctx", None),
        check_vma=False,
    )
```

```python
import functools
import math

import jax
import jax.numpy as jnp
from jax import lax
from jax.experimental import pallas as pl
from jax.experimental.pallas import tpu as pltpu
from jax.sharding import PartitionSpec as P

HQ = 16
KVH = 2
HD = 128
GROUPS = HQ // KVH
CAP = 24
NEG = -1e30
SCORE_SCALE = math.log2(math.e) / math.sqrt(HD)
F32 = jnp.float32
BF16 = jnp.bfloat16


def slab_segments(segs_ref, index, count, rows):
    found = segs_ref[:, 0:rows]
    for slab in range(1, count):
        found = jnp.where(index == slab, segs_ref[:, slab * rows : (slab + 1) * rows], found)
    return found


def score_bias(segs_ref, backs, count, rows):
    me = lax.axis_index("ctx")
    row = lax.broadcasted_iota(jnp.int32, (rows, rows), 0)
    col = lax.broadcasted_iota(jnp.int32, (rows, rows), 1)
    own_seg = slab_segments(segs_ref, me, count, rows)
    query_seg = jnp.sum(jnp.where(row == col, own_seg, 0), axis=1, keepdims=True)
    parts = []
    for back in backs:
        if back == 0:
            allowed = (col <= row) & (own_seg == query_seg)
        else:
            key_seg = slab_segments(segs_ref, jnp.maximum(me - back, 0), count, rows)
            allowed = (key_seg == query_seg) & (me >= back)
        parts.append(jnp.where(allowed, 0.0, NEG))
    return parts


def group_scores(stacked, keys, bias):
    scores = lax.dot_general(
        stacked, keys, (((1,), (1,)), ((), ())), preferred_element_type=F32
    )
    return scores.reshape(GROUPS, *bias.shape) * SCORE_SCALE + bias


def weigh(expo, values):
    rows = expo.shape[0] * expo.shape[1]
    mixed = jnp.dot(
        expo.astype(BF16).reshape(rows, expo.shape[2]), values, preferred_element_type=F32
    ).reshape(*expo.shape[:2], 2 * HD)
    return mixed[:, :, :HD], mixed[:, :, HD:]


def mark_kernel(*refs):
    refs[-1][...] = jnp.zeros_like(refs[-1])


def gate_kernel(*refs):
    del refs


def after(piece, *marks):
    spec = pl.BlockSpec(memory_space=pl.ANY)
    return pl.pallas_call(
        gate_kernel,
        out_shape=jax.ShapeDtypeStruct(piece.shape, piece.dtype),
        in_specs=[spec] * (1 + len(marks)),
        out_specs=spec,
        input_output_aliases={0: 0},
        compiler_params=pltpu.CompilerParams(vmem_limit_bytes=1 << 20),
    )(piece, *marks)


def join_kernel(first_ref, second_ref, mark_ref, whole_ref, sems):
    del mark_ref
    half = first_ref.shape[0]
    core = lax.rem(lax.axis_index("dp"), 2)
    copies = []
    for index, (lead, ref) in enumerate([(core, first_ref), (1 - core, second_ref)]):
        target = whole_ref.at[pl.ds(pl.multiple_of(lead * half, half), half)]
        copies.append(pltpu.make_async_copy(ref, target, sems.at[index]))
        copies[-1].start()
    for copy in copies:
        copy.wait()


def own_kernel(
    n_ctx,
    q_ref,
    kv_ref,
    segs_ref,
    mark_ref,
    w_ref,
    acc_ref,
    max_ref,
    sum_ref,
    queries_ref,
    first_ref,
    second_ref,
    sems,
):
    del mark_ref
    half = first_ref.shape[0]
    core = lax.rem(lax.axis_index("dp"), 2)
    copies = []
    for index, (lead, ref) in enumerate([(core, first_ref), (1 - core, second_ref)]):
        source = w_ref.at[pl.ds(pl.multiple_of(lead * half, half), half)]
        copies.append(pltpu.make_async_copy(source, ref, sems.at[index]))
        copies[-1].start()
    rows = q_ref.shape[0]
    (bias,) = score_bias(segs_ref, (0,), n_ctx, rows)
    ones = jnp.ones((rows, HD), BF16)
    for kv in range(KVH):
        keys = kv_ref[:, kv * HD : (kv + 1) * HD]
        values = jnp.concatenate([kv_ref[:, (KVH + kv) * HD : (KVH + kv + 1) * HD], ones], axis=1)
        heads = range(kv * GROUPS, (kv + 1) * GROUPS)
        stacked = jnp.concatenate([q_ref[:, h * HD : (h + 1) * HD] for h in heads], axis=0)
        queries_ref[kv] = stacked
        scores = group_scores(stacked, keys, bias)
        row_max = jnp.max(scores, axis=2, keepdims=True)
        accum, row_sum = weigh(jnp.exp2(scores - row_max), values)
        acc_ref[kv] = accum
        max_ref[kv] = jnp.broadcast_to(row_max, max_ref.shape[1:])
        sum_ref[kv] = row_sum
    for copy in copies:
        copy.wait()


def route_kernel(ids_ref, rw_ref, res_ref, place_ref, mix_ref, rows_ref):
    slots, rows = place_ref.shape
    slot = lax.broadcasted_iota(jnp.int32, (slots, rows), 0)
    owner = (slot // CAP) ^ lax.axis_index("exp")
    hit = jnp.zeros((slots, rows), jnp.bool_)
    weight = jnp.zeros((slots, rows), F32)
    for choice in range(ids_ref.shape[0]):
        same = ids_ref[choice : choice + 1, :] == owner
        hit = hit | same
        weight = jnp.where(same, rw_ref[choice : choice + 1, :], weight)
    row = lax.broadcasted_iota(jnp.int32, (rows, rows), 0)
    col = lax.broadcasted_iota(jnp.int32, (rows, rows), 1)
    before = (row < col).astype(F32).astype(BF16)
    rank = jnp.dot(hit.astype(F32).astype(BF16), before, preferred_element_type=F32)
    placed = hit & (rank == lax.rem(slot, CAP).astype(F32))
    place = placed.astype(F32).astype(BF16)
    place_ref[...] = place
    mix = jnp.where(placed, weight, 0.0)
    high = mix.astype(BF16).astype(F32)
    mix_ref[...] = jnp.concatenate([high, mix - high], axis=0).T.astype(BF16)
    rows_ref[...] = jnp.dot(place, res_ref[...], preferred_element_type=F32)


def rest_kernel(
    n_ctx,
    back_count,
    segs_ref,
    acc_ref,
    max_ref,
    sum_ref,
    queries_ref,
    place_ref,
    *refs,
):
    kv_refs, (out_ref, routed_ref) = refs[:back_count], refs[-2:]
    rows = queries_ref.shape[1] // GROUPS
    bias = jnp.concatenate(score_bias(segs_ref, range(1, back_count + 1), n_ctx, rows), axis=1)
    keys_count = rows * back_count
    spread = -(-keys_count // HD)
    ones = jnp.ones((keys_count, HD), BF16)
    scores = []
    for kv in range(KVH):
        keys = jnp.concatenate([ref[:, kv * HD : (kv + 1) * HD] for ref in kv_refs], axis=0)
        scores.append(group_scores(queries_ref[kv], keys, bias))
    for kv in range(KVH):
        values = jnp.concatenate(
            [ref[:, (KVH + kv) * HD : (KVH + kv + 1) * HD] for ref in kv_refs], axis=0
        )
        values = jnp.concatenate([values, ones], axis=1)
        old_max = max_ref[kv]
        new_max = jnp.maximum(old_max, jnp.max(scores[kv], axis=2, keepdims=True))
        shift = jnp.concatenate([new_max] * spread, axis=2)[:, :, :keys_count]
        accum, row_sum = weigh(jnp.exp2(scores[kv] - shift), values)
        fix = jnp.exp2(old_max - new_max)
        total = sum_ref[kv] * fix + row_sum
        attended = ((acc_ref[kv] * fix + accum) / total).astype(BF16)
        for group in range(GROUPS):
            head = kv * GROUPS + group
            out_ref[:, head * HD : (head + 1) * HD] = attended[group]
    routed_ref[...] = jnp.dot(place_ref[...], out_ref[...], preferred_element_type=F32)


def send_kernel(blocks, entries, owners, routed_ref, rows_ref, *refs):
    piece_refs, send_refs = refs[:-owners], refs[-owners:]
    me, core = lax.axis_index("ctx"), lax.axis_index("dp")
    share = routed_ref.shape[1] // lax.axis_size("ctx")
    part = project(rows_ref[...], routed_ref, entries, piece_refs, False)
    for step, ref in enumerate(send_refs):
        rows = pl.ds(step * CAP, CAP)
        filled = 0
        for size, flip, offset in blocks:
            lead = pl.multiple_of((me ^ flip(core)) * share + offset(core), size)
            ref[:, filled : filled + size] = routed_ref[rows, pl.ds(lead, size)].astype(BF16)
            filled += size
        ref[:, filled:] = part[step * CAP : (step + 1) * CAP, :].astype(BF16)


def stack(parts):
    return jnp.concatenate([part.astype(F32) for part in parts], axis=0).astype(BF16)


def project(total, att_ref, entries, piece_refs, moved):
    me, core = lax.axis_index("ctx"), lax.axis_index("dp")
    share = att_ref.shape[1] // lax.axis_size("ctx")
    for piece, size, flip, offset, row, column in entries:
        lead = column(core) if moved else (me ^ flip(core)) * share + offset(core)
        columns = pl.ds(pl.multiple_of(lead, size), size)
        rows = pl.ds(pl.multiple_of(row(me, core), size), size)
        total = total + jnp.dot(
            att_ref[:, columns].astype(BF16),
            piece_refs[piece][rows, :],
            preferred_element_type=F32,
        )
    return total


def arrive_kernel(owners, entries, *refs):
    row_refs, piece_refs, (att_ref, hidden_ref) = refs[:owners], refs[owners:-2], refs[-2:]
    row_refs = row_refs[:1] + row_refs[:0:-1]
    wide = att_ref.shape[1]
    att_ref[...] = stack([ref[:, :wide] for ref in row_refs])
    hidden = jnp.concatenate([ref[:, wide:].astype(F32) for ref in row_refs], axis=0)
    hidden_ref[...] = project(hidden, att_ref, entries, piece_refs, True)


def expert_kernel(entries, count, gain_ref, gate_ref, up_ref, down_ref, att_ref, part_ref, *refs):
    piece_refs, out_refs = refs[:count], refs[count:]
    hidden = project(part_ref[...], att_ref, entries, piece_refs, True)
    mean = jnp.mean(hidden * hidden, axis=1, keepdims=True)
    normed = (hidden * lax.rsqrt(mean + 1e-06) * gain_ref[...]).astype(BF16)
    gate = jnp.dot(normed, gate_ref[...], preferred_element_type=F32)
    up = jnp.dot(normed, up_ref[...], preferred_element_type=F32)
    act = (gate / (1.0 + jnp.exp(-gate)) * up).astype(BF16)
    out = jnp.dot(act, down_ref[...], preferred_element_type=F32)
    for step, ref in enumerate(out_refs):
        ref[...] = out[step * CAP : (step + 1) * CAP, :].astype(BF16)


def project_kernel(entries, att_ref, res_ref, *refs):
    hidden = res_ref[...].astype(F32)
    refs[-1][...] = project(hidden, att_ref, entries, refs[:-1], False)


def combine_kernel(owners, hidden_ref, mix_ref, *refs):
    row_refs, out_ref = refs[:1] + refs[owners - 1 : 0 : -1], refs[owners]
    rows = stack([ref[...] for ref in row_refs])
    total = hidden_ref[...] + jnp.dot(
        mix_ref[...], jnp.concatenate([rows, rows], axis=0), preferred_element_type=F32
    )
    out_ref[...] = total.astype(BF16)


def call(kernel, outs, args, micros, scratch=(), limit=24, free_in=0, free_out=0):
    vmem, free = pl.BlockSpec(memory_space=pltpu.VMEM), pl.BlockSpec(memory_space=pl.ANY)
    nbytes = sum(math.prod(a.shape) * a.dtype.itemsize for a in list(args) + list(outs))
    return pl.pallas_call(
        kernel,
        out_shape=outs,
        in_specs=[vmem] * (len(args) - free_in) + [free] * free_in,
        out_specs=[vmem] * (len(outs) - free_out) + [free] * free_out,
        scratch_shapes=list(scratch),
        compiler_params=pltpu.CompilerParams(vmem_limit_bytes=limit << 20),
        cost_estimate=pl.CostEstimate(
            flops=int(micros * 1.15e9), bytes_accessed=nbytes, transcendentals=0
        ),
    )(*args)


def exchange(blocks):
    count = len(blocks)
    return [blocks[0]] + [
        lax.ppermute(blocks[s], "exp", [(i, i ^ s) for i in range(count)])
        for s in range(count - 1, 0, -1)
    ]


def gather_weight(weight, first, second, attended):
    n_ctx, cores = lax.axis_size("ctx"), lax.axis_size("dp")
    share = weight.shape[0]
    if (n_ctx, cores) != (4, 2):
        whole = lax.all_gather(weight, "ctx", axis=0, tiled=True)
        entries = [
            (
                0,
                share,
                lambda core, f=f: f,
                lambda core: 0,
                lambda me, core, f=f: (me ^ f) * share,
                lambda core, f=f: (f - 1) * share,
            )
            for f in range(n_ctx)
        ]
        home = [(0, share, lambda core: 0, lambda core: 0, lambda me, core: 0, None)]
        blocks = [(share, lambda core, f=f: f, lambda core: 0) for f in range(1, n_ctx)]
        return [whole], entries, entries[1:], [weight], home, blocks
    both = ("ctx", "dp")
    devices = [(me, core) for me in range(n_ctx) for core in range(cores)]
    aside = [(me * 2 + core, (me ^ (1 + core)) * 2 + core) for me, core in devices]
    across = [(me * 2 + core, (me ^ (2 - core)) * 2 + core) for me, core in devices]
    near_first = lax.ppermute(first, both, aside)
    near_second = lax.ppermute(second, both, aside)
    near_first = after(near_first, attended)
    far = lax.ppermute(near_first, both, across)
    (near,) = call(
        join_kernel,
        [jax.ShapeDtypeStruct(weight.shape, BF16)],
        [near_first, near_second, attended],
        micros=1,
        free_in=3,
        free_out=1,
        limit=1,
        scratch=[pltpu.SemaphoreType.DMA((2,))],
    )
    swap = [(0, 1), (1, 0)]
    pieces = [weight, near, far, lax.ppermute(near, "dp", swap), lax.ppermute(far, "dp", swap)]
    half = share // 2
    top = lambda me, core: 0
    entries = [
        (0, share, lambda core: 0, lambda core: 0, top, None),
        (1, share, lambda core: 1 + core, lambda core: 0, top, None),
        (2, half, lambda core: 3, lambda core: core * half, top, None),
        (3, share, lambda core: 2 - core, lambda core: 0, top, None),
        (4, half, lambda core: 3, lambda core: (1 - core) * half, top, None),
    ]
    moved = [
        (1, half, None, None, lambda me, core: (1 - core) * half, lambda core: 0),
        (2, half, None, None, top, lambda core: (3 + core) * half),
        (3, half, None, None, top, lambda core: half),
        (3, half, None, None, lambda me, core: half, lambda core: 2 * half),
        (4, half, None, None, top, lambda core: (4 - core) * half),
    ]
    home = [
        (0, share, lambda core: 0, lambda core: 0, top, None),
        (1, half, lambda core: 1 + core, lambda core: core * half, top, None),
    ]
    blocks = [
        (half, lambda core: 1 + core, lambda core: (1 - core) * half),
        (share, lambda core: 2 - core, lambda core: 0),
        (share, lambda core: 3, lambda core: 0),
    ]
    return pieces, entries, moved, [weight, near_first], home, blocks


def per_device(
    queries,
    keys,
    values,
    segments,
    residual,
    out_weight,
    gain,
    expert_ids,
    route_weights,
    w_gate,
    w_up,
    w_down,
):
    tok_rows = queries.shape[1]
    width = residual.shape[2]
    att_width = queries.shape[2]
    n_ctx, owners = lax.axis_size("ctx"), lax.axis_size("exp")
    slots = owners * CAP
    longest = segments.shape[1] // 2
    back_count = min(n_ctx - 1, -(-(longest - 1) // tok_rows))
    shape = jax.ShapeDtypeStruct

    own_kv = jnp.concatenate([keys[0], values[0]], axis=1)
    kv_blocks = []
    for back in range(1, back_count + 1):
        pairs = [(i, (i + back) % n_ctx) for i in range(n_ctx)]
        kv_blocks.append(lax.ppermute(own_kv, "ctx", pairs))
    (mark,) = call(mark_kernel, [shape((8, 128), F32)], [own_kv], micros=5, free_in=1, limit=1)
    half = shape((out_weight.shape[0] // 2, width), BF16)
    accum, row_max, row_sum, stacked, first, second = call(
        functools.partial(own_kernel, n_ctx),
        [
            shape((KVH, GROUPS, tok_rows, HD), F32),
            shape((KVH, GROUPS, tok_rows, HD), F32),
            shape((KVH, GROUPS, tok_rows, HD), F32),
            shape((KVH, GROUPS * tok_rows, HD), BF16),
            half,
            half,
        ],
        [queries[0], own_kv, segments, mark, out_weight],
        micros=3,
        free_in=1,
        free_out=2,
        scratch=[pltpu.SemaphoreType.DMA((2,))],
    )
    place, mix, res_rows = call(
        route_kernel,
        [
            shape((slots, tok_rows), BF16),
            shape((tok_rows, 2 * slots), BF16),
            shape((slots, width), F32),
        ],
        [expert_ids[0].T, route_weights[0].T, residual[0]],
        micros=1,
    )
    attended, chosen = call(
        functools.partial(rest_kernel, n_ctx, back_count),
        [shape((tok_rows, att_width), BF16), shape((slots, att_width), F32)],
        [segments, accum, row_max, row_sum, stacked, place, *kv_blocks]
        + [gain[None, :], w_gate[0], w_up[0], w_down[0]],
        micros=5,
    )
    pieces, entries, moved, near, home, blocks = gather_weight(
        out_weight, first, second, attended
    )
    moved_width = sum(size for size, _, _ in blocks)
    routed = call(
        functools.partial(send_kernel, blocks, home, owners),
        [shape((CAP, moved_width + width), BF16)] * owners,
        [chosen, res_rows, *near],
        micros=1,
    )
    early = pieces[1:2]
    late = pieces[2:] or pieces
    now = [(0, *entry[1:]) for entry in moved if early and entry[0] == 1]
    skipped = len(pieces) - len(late)
    then = [(entry[0] - skipped, *entry[1:]) for entry in moved if entry[0] >= skipped]
    arrived, part = call(
        functools.partial(arrive_kernel, owners, now),
        [shape((slots, moved_width), BF16), shape((slots, width), F32)],
        [*exchange(routed), *early],
        micros=10,
    )
    done = call(
        functools.partial(expert_kernel, then, len(late)),
        [shape((CAP, width), BF16)] * owners,
        [gain[None, :], w_gate[0], w_up[0], w_down[0], arrived, part, *late],
        micros=2,
    )
    back = exchange(done)
    (hidden,) = call(
        functools.partial(project_kernel, entries),
        [shape((tok_rows, width), F32)],
        [attended, residual[0], *pieces],
        micros=2,
    )
    (out,) = call(
        functools.partial(combine_kernel, owners),
        [shape((tok_rows, width), BF16)],
        [hidden, mix, *back],
        micros=1,
    )
    return out[None]


def solution(mesh):
    return jax.shard_map(
        per_device,
        mesh=mesh,
        in_specs=(
            P(("dp", "exp"), "ctx", None),
            P(("dp", "exp"), "ctx", None),
            P(("dp", "exp"), "ctx", None),
            P(("dp", "exp"), None),
            P(("dp", "exp"), "ctx", None),
            P("ctx", None),
            P(),
            P(("dp", "exp"), "ctx", None),
            P(("dp", "exp"), "ctx", None),
            P("exp", None, None),
            P("exp", None, None),
            P("exp", None, None),
        ),
        out_specs=P(("dp", "exp"), "ctx", None),
        check_vma=False,
    )
```

```python
import functools
import math

import jax
import jax.numpy as jnp
from jax import lax
from jax.experimental import pallas as pl
from jax.experimental.pallas import tpu as pltpu
from jax.sharding import PartitionSpec as P

HQ = 16
KVH = 2
HD = 128
GROUPS = HQ // KVH
CAP = 24
NEG = -1e30
SCORE_SCALE = math.log2(math.e) / math.sqrt(HD)
F32 = jnp.float32
BF16 = jnp.bfloat16


def slab_segments(segs_ref, index, count, rows):
    found = segs_ref[:, 0:rows]
    for slab in range(1, count):
        found = jnp.where(index == slab, segs_ref[:, slab * rows : (slab + 1) * rows], found)
    return found


def score_bias(segs_ref, backs, count, rows):
    me = lax.axis_index("ctx")
    row = lax.broadcasted_iota(jnp.int32, (rows, rows), 0)
    col = lax.broadcasted_iota(jnp.int32, (rows, rows), 1)
    own_seg = slab_segments(segs_ref, me, count, rows)
    query_seg = jnp.sum(jnp.where(row == col, own_seg, 0), axis=1, keepdims=True)
    parts = []
    for back in backs:
        if back == 0:
            allowed = (col <= row) & (own_seg == query_seg)
        else:
            key_seg = slab_segments(segs_ref, jnp.maximum(me - back, 0), count, rows)
            allowed = (key_seg == query_seg) & (me >= back)
        parts.append(jnp.where(allowed, 0.0, NEG))
    return parts


def group_scores(stacked, keys, bias):
    scores = lax.dot_general(
        stacked, keys, (((1,), (1,)), ((), ())), preferred_element_type=F32
    )
    return scores.reshape(GROUPS, *bias.shape) * SCORE_SCALE + bias


def weigh(expo, values):
    rows = expo.shape[0] * expo.shape[1]
    mixed = jnp.dot(
        expo.astype(BF16).reshape(rows, expo.shape[2]), values, preferred_element_type=F32
    ).reshape(*expo.shape[:2], 2 * HD)
    return mixed[:, :, :HD], mixed[:, :, HD:]


def mark_kernel(*refs):
    refs[-1][...] = jnp.zeros_like(refs[-1])


def gate_kernel(*refs):
    del refs


def after(piece, *marks):
    spec = pl.BlockSpec(memory_space=pl.ANY)
    return pl.pallas_call(
        gate_kernel,
        out_shape=jax.ShapeDtypeStruct(piece.shape, piece.dtype),
        in_specs=[spec] * (1 + len(marks)),
        out_specs=spec,
        input_output_aliases={0: 0},
        compiler_params=pltpu.CompilerParams(vmem_limit_bytes=1 << 20),
    )(piece, *marks)


def join_kernel(first_ref, second_ref, mark_ref, whole_ref, sems):
    del mark_ref
    half = first_ref.shape[0]
    core = lax.rem(lax.axis_index("dp"), 2)
    copies = []
    for index, (lead, ref) in enumerate([(core, first_ref), (1 - core, second_ref)]):
        target = whole_ref.at[pl.ds(pl.multiple_of(lead * half, half), half)]
        copies.append(pltpu.make_async_copy(ref, target, sems.at[index]))
        copies[-1].start()
    for copy in copies:
        copy.wait()


def own_kernel(
    n_ctx,
    q_ref,
    kv_ref,
    segs_ref,
    mark_ref,
    w_ref,
    acc_ref,
    max_ref,
    sum_ref,
    queries_ref,
    first_ref,
    second_ref,
    sems,
):
    del mark_ref
    half = first_ref.shape[0]
    core = lax.rem(lax.axis_index("dp"), 2)
    copies = []
    for index, (lead, ref) in enumerate([(core, first_ref), (1 - core, second_ref)]):
        source = w_ref.at[pl.ds(pl.multiple_of(lead * half, half), half)]
        copies.append(pltpu.make_async_copy(source, ref, sems.at[index]))
        copies[-1].start()
    rows = q_ref.shape[0]
    (bias,) = score_bias(segs_ref, (0,), n_ctx, rows)
    ones = jnp.ones((rows, HD), BF16)
    for kv in range(KVH):
        keys = kv_ref[:, kv * HD : (kv + 1) * HD]
        values = jnp.concatenate([kv_ref[:, (KVH + kv) * HD : (KVH + kv + 1) * HD], ones], axis=1)
        heads = range(kv * GROUPS, (kv + 1) * GROUPS)
        stacked = jnp.concatenate([q_ref[:, h * HD : (h + 1) * HD] for h in heads], axis=0)
        queries_ref[kv] = stacked
        scores = group_scores(stacked, keys, bias)
        row_max = jnp.max(scores, axis=2, keepdims=True)
        accum, row_sum = weigh(jnp.exp2(scores - row_max), values)
        acc_ref[kv] = accum
        max_ref[kv] = jnp.broadcast_to(row_max, max_ref.shape[1:])
        sum_ref[kv] = row_sum
    for copy in copies:
        copy.wait()


def route_kernel(
    n_ctx, back_count, segs_ref, ids_ref, rw_ref, res_ref, bias_ref, place_ref, mix_ref, rows_ref
):
    for back, bias in enumerate(
        score_bias(segs_ref, range(1, back_count + 1), n_ctx, rw_ref.shape[1])
    ):
        bias_ref[:, back * bias.shape[1] : (back + 1) * bias.shape[1]] = bias
    slots, rows = place_ref.shape
    slot = lax.broadcasted_iota(jnp.int32, (slots, rows), 0)
    owner = (slot // CAP) ^ lax.axis_index("exp")
    hit = jnp.zeros((slots, rows), jnp.bool_)
    weight = jnp.zeros((slots, rows), F32)
    for choice in range(ids_ref.shape[0]):
        same = ids_ref[choice : choice + 1, :] == owner
        hit = hit | same
        weight = jnp.where(same, rw_ref[choice : choice + 1, :], weight)
    row = lax.broadcasted_iota(jnp.int32, (rows, rows), 0)
    col = lax.broadcasted_iota(jnp.int32, (rows, rows), 1)
    before = (row < col).astype(F32).astype(BF16)
    rank = jnp.dot(hit.astype(F32).astype(BF16), before, preferred_element_type=F32)
    placed = hit & (rank == lax.rem(slot, CAP).astype(F32))
    place = placed.astype(F32).astype(BF16)
    place_ref[...] = place
    mix = jnp.where(placed, weight, 0.0)
    high = mix.astype(BF16).astype(F32)
    mix_ref[...] = jnp.concatenate([high, mix - high], axis=0).T.astype(BF16)
    rows_ref[...] = jnp.dot(place, res_ref[...], preferred_element_type=F32)


def rest_kernel(
    back_count,
    bias_ref,
    acc_ref,
    max_ref,
    sum_ref,
    queries_ref,
    place_ref,
    *refs,
):
    kv_refs, (out_ref, routed_ref) = refs[:back_count], refs[-2:]
    rows = queries_ref.shape[1] // GROUPS
    bias = bias_ref[...]
    keys_count = rows * back_count
    spread = -(-keys_count // HD)
    ones = jnp.ones((keys_count, HD), BF16)
    scores = []
    for kv in range(KVH):
        keys = jnp.concatenate([ref[:, kv * HD : (kv + 1) * HD] for ref in kv_refs], axis=0)
        scores.append(group_scores(queries_ref[kv], keys, bias))
    for kv in range(KVH):
        values = jnp.concatenate(
            [ref[:, (KVH + kv) * HD : (KVH + kv + 1) * HD] for ref in kv_refs], axis=0
        )
        values = jnp.concatenate([values, ones], axis=1)
        old_max = max_ref[kv]
        new_max = jnp.maximum(old_max, jnp.max(scores[kv], axis=2, keepdims=True))
        shift = jnp.concatenate([new_max] * spread, axis=2)[:, :, :keys_count]
        accum, row_sum = weigh(jnp.exp2(scores[kv] - shift), values)
        fix = jnp.exp2(old_max - new_max)
        total = sum_ref[kv] * fix + row_sum
        attended = ((acc_ref[kv] * fix + accum) / total).astype(BF16)
        for group in range(GROUPS):
            head = kv * GROUPS + group
            out_ref[:, head * HD : (head + 1) * HD] = attended[group]
    routed_ref[...] = jnp.dot(place_ref[...], out_ref[...], preferred_element_type=F32)


def send_kernel(blocks, entries, owners, routed_ref, rows_ref, *refs):
    piece_refs, send_refs = refs[:-owners], refs[-owners:]
    me, core = lax.axis_index("ctx"), lax.axis_index("dp")
    share = routed_ref.shape[1] // lax.axis_size("ctx")
    part = project(rows_ref[...], routed_ref, entries, piece_refs, False)
    for step, ref in enumerate(send_refs):
        rows = pl.ds(step * CAP, CAP)
        filled = 0
        for size, flip, offset in blocks:
            lead = pl.multiple_of((me ^ flip(core)) * share + offset(core), size)
            ref[:, filled : filled + size] = routed_ref[rows, pl.ds(lead, size)].astype(BF16)
            filled += size
        ref[:, filled:] = part[step * CAP : (step + 1) * CAP, :].astype(BF16)


def stack(parts):
    return jnp.concatenate([part.astype(F32) for part in parts], axis=0).astype(BF16)


def project(total, att_ref, entries, piece_refs, moved):
    me, core = lax.axis_index("ctx"), lax.axis_index("dp")
    share = att_ref.shape[1] // lax.axis_size("ctx")
    for piece, size, flip, offset, row, column in entries:
        lead = column(core) if moved else (me ^ flip(core)) * share + offset(core)
        columns = pl.ds(pl.multiple_of(lead, size), size)
        rows = pl.ds(pl.multiple_of(row(me, core), size), size)
        total = total + jnp.dot(
            att_ref[:, columns].astype(BF16),
            piece_refs[piece][rows, :],
            preferred_element_type=F32,
        )
    return total


def arrive_kernel(owners, entries, *refs):
    row_refs, piece_refs, (att_ref, hidden_ref) = refs[:owners], refs[owners:-2], refs[-2:]
    row_refs = row_refs[:1] + row_refs[:0:-1]
    wide = att_ref.shape[1]
    att_ref[...] = stack([ref[:, :wide] for ref in row_refs])
    hidden = jnp.concatenate([ref[:, wide:].astype(F32) for ref in row_refs], axis=0)
    hidden_ref[...] = project(hidden, att_ref, entries, piece_refs, True)


def expert_kernel(entries, count, gain_ref, gate_ref, up_ref, down_ref, att_ref, part_ref, *refs):
    piece_refs, out_refs = refs[:count], refs[count:]
    hidden = project(part_ref[...], att_ref, entries, piece_refs, True)
    mean = jnp.mean(hidden * hidden, axis=1, keepdims=True)
    normed = (hidden * lax.rsqrt(mean + 1e-06) * gain_ref[...]).astype(BF16)
    gate = jnp.dot(normed, gate_ref[...], preferred_element_type=F32)
    up = jnp.dot(normed, up_ref[...], preferred_element_type=F32)
    act = (gate / (1.0 + jnp.exp(-gate)) * up).astype(BF16)
    out = jnp.dot(act, down_ref[...], preferred_element_type=F32)
    for step, ref in enumerate(out_refs):
        ref[...] = out[step * CAP : (step + 1) * CAP, :].astype(BF16)


def project_kernel(entries, att_ref, res_ref, *refs):
    hidden = res_ref[...].astype(F32)
    refs[-1][...] = project(hidden, att_ref, entries, refs[:-1], False)


def combine_kernel(owners, parts, hidden_ref, mix_ref, *refs):
    row_refs, (out_ref, out_buf, sems) = refs[:1] + refs[owners - 1 : 0 : -1], refs[owners:]
    rows = stack([ref[...] for ref in row_refs])
    rows = jnp.concatenate([rows, rows], axis=0)
    size = out_buf.shape[0] // parts
    copies = []
    for part in range(parts):
        span = pl.ds(part * size, size)
        total = hidden_ref[span, :] + jnp.dot(
            mix_ref[span, :], rows, preferred_element_type=F32
        )
        out_buf[span, :] = total.astype(BF16)
        copies.append(pltpu.make_async_copy(out_buf.at[span], out_ref.at[span], sems.at[part]))
        copies[-1].start()
    for copy in copies:
        copy.wait()


def call(kernel, outs, args, micros, scratch=(), limit=24, free_in=0, free_out=0):
    vmem, free = pl.BlockSpec(memory_space=pltpu.VMEM), pl.BlockSpec(memory_space=pl.ANY)
    nbytes = sum(math.prod(a.shape) * a.dtype.itemsize for a in list(args) + list(outs))
    return pl.pallas_call(
        kernel,
        out_shape=outs,
        in_specs=[vmem] * (len(args) - free_in) + [free] * free_in,
        out_specs=[vmem] * (len(outs) - free_out) + [free] * free_out,
        scratch_shapes=list(scratch),
        compiler_params=pltpu.CompilerParams(vmem_limit_bytes=limit << 20),
        cost_estimate=pl.CostEstimate(
            flops=int(micros * 1.15e9), bytes_accessed=nbytes, transcendentals=0
        ),
    )(*args)


def exchange(blocks):
    count = len(blocks)
    return [blocks[0]] + [
        lax.ppermute(blocks[s], "exp", [(i, i ^ s) for i in range(count)])
        for s in range(count - 1, 0, -1)
    ]


def gather_weight(weight, first, second, attended):
    n_ctx, cores = lax.axis_size("ctx"), lax.axis_size("dp")
    share = weight.shape[0]
    if (n_ctx, cores) != (4, 2):
        whole = lax.all_gather(weight, "ctx", axis=0, tiled=True)
        entries = [
            (
                0,
                share,
                lambda core, f=f: f,
                lambda core: 0,
                lambda me, core, f=f: (me ^ f) * share,
                lambda core, f=f: (f - 1) * share,
            )
            for f in range(n_ctx)
        ]
        home = [(0, share, lambda core: 0, lambda core: 0, lambda me, core: 0, None)]
        blocks = [(share, lambda core, f=f: f, lambda core: 0) for f in range(1, n_ctx)]
        return [whole], entries, entries[1:], [weight], home, blocks
    both = ("ctx", "dp")
    devices = [(me, core) for me in range(n_ctx) for core in range(cores)]
    aside = [(me * 2 + core, (me ^ (1 + core)) * 2 + core) for me, core in devices]
    across = [(me * 2 + core, (me ^ (2 - core)) * 2 + core) for me, core in devices]
    near_first = lax.ppermute(first, both, aside)
    near_second = lax.ppermute(second, both, aside)
    near_first = after(near_first, attended)
    far = lax.ppermute(near_first, both, across)
    (near,) = call(
        join_kernel,
        [jax.ShapeDtypeStruct(weight.shape, BF16)],
        [near_first, near_second, attended],
        micros=1,
        free_in=3,
        free_out=1,
        limit=1,
        scratch=[pltpu.SemaphoreType.DMA((2,))],
    )
    swap = [(0, 1), (1, 0)]
    pieces = [weight, near, far, lax.ppermute(near, "dp", swap), lax.ppermute(far, "dp", swap)]
    half = share // 2
    top = lambda me, core: 0
    entries = [
        (0, share, lambda core: 0, lambda core: 0, top, None),
        (1, share, lambda core: 1 + core, lambda core: 0, top, None),
        (2, half, lambda core: 3, lambda core: core * half, top, None),
        (3, share, lambda core: 2 - core, lambda core: 0, top, None),
        (4, half, lambda core: 3, lambda core: (1 - core) * half, top, None),
    ]
    moved = [
        (1, half, None, None, lambda me, core: (1 - core) * half, lambda core: 0),
        (2, half, None, None, top, lambda core: (3 + core) * half),
        (3, half, None, None, top, lambda core: half),
        (3, half, None, None, lambda me, core: half, lambda core: 2 * half),
        (4, half, None, None, top, lambda core: (4 - core) * half),
    ]
    home = [
        (0, share, lambda core: 0, lambda core: 0, top, None),
        (1, half, lambda core: 1 + core, lambda core: core * half, top, None),
    ]
    blocks = [
        (half, lambda core: 1 + core, lambda core: (1 - core) * half),
        (share, lambda core: 2 - core, lambda core: 0),
        (share, lambda core: 3, lambda core: 0),
    ]
    return pieces, entries, moved, [weight, near_first], home, blocks


def per_device(
    queries,
    keys,
    values,
    segments,
    residual,
    out_weight,
    gain,
    expert_ids,
    route_weights,
    w_gate,
    w_up,
    w_down,
):
    tok_rows = queries.shape[1]
    width = residual.shape[2]
    att_width = queries.shape[2]
    n_ctx, owners = lax.axis_size("ctx"), lax.axis_size("exp")
    slots = owners * CAP
    longest = segments.shape[1] // 2
    back_count = min(n_ctx - 1, -(-(longest - 1) // tok_rows))
    shape = jax.ShapeDtypeStruct

    own_kv = jnp.concatenate([keys[0], values[0]], axis=1)
    kv_blocks = []
    for back in range(1, back_count + 1):
        pairs = [(i, (i + back) % n_ctx) for i in range(n_ctx)]
        kv_blocks.append(lax.ppermute(own_kv, "ctx", pairs))
    (mark,) = call(mark_kernel, [shape((8, 128), F32)], [own_kv], micros=5, free_in=1, limit=1)
    half = shape((out_weight.shape[0] // 2, width), BF16)
    accum, row_max, row_sum, stacked, first, second = call(
        functools.partial(own_kernel, n_ctx),
        [
            shape((KVH, GROUPS, tok_rows, HD), F32),
            shape((KVH, GROUPS, tok_rows, HD), F32),
            shape((KVH, GROUPS, tok_rows, HD), F32),
            shape((KVH, GROUPS * tok_rows, HD), BF16),
            half,
            half,
        ],
        [queries[0], own_kv, segments, mark, out_weight],
        micros=3,
        free_in=1,
        free_out=2,
        scratch=[pltpu.SemaphoreType.DMA((2,))],
    )
    bias, place, mix, res_rows = call(
        functools.partial(route_kernel, n_ctx, back_count),
        [
            shape((tok_rows, back_count * tok_rows), F32),
            shape((slots, tok_rows), BF16),
            shape((tok_rows, 2 * slots), BF16),
            shape((slots, width), F32),
        ],
        [segments, expert_ids[0].T, route_weights[0].T, residual[0]],
        micros=1,
    )
    attended, chosen = call(
        functools.partial(rest_kernel, back_count),
        [shape((tok_rows, att_width), BF16), shape((slots, att_width), F32)],
        [bias, accum, row_max, row_sum, stacked, place, *kv_blocks]
        + [gain[None, :], w_gate[0], w_up[0], w_down[0]],
        micros=5,
    )
    pieces, entries, moved, near, home, blocks = gather_weight(
        out_weight, first, second, attended
    )
    moved_width = sum(size for size, _, _ in blocks)
    routed = call(
        functools.partial(send_kernel, blocks, home, owners),
        [shape((CAP, moved_width + width), BF16)] * owners,
        [chosen, res_rows, *near],
        micros=1,
    )
    early = pieces[1:2]
    late = pieces[2:] or pieces
    now = [(0, *entry[1:]) for entry in moved if early and entry[0] == 1]
    skipped = len(pieces) - len(late)
    then = [(entry[0] - skipped, *entry[1:]) for entry in moved if entry[0] >= skipped]
    arrived, part = call(
        functools.partial(arrive_kernel, owners, now),
        [shape((slots, moved_width), BF16), shape((slots, width), F32)],
        [*exchange(routed), *early],
        micros=10,
    )
    done = call(
        functools.partial(expert_kernel, then, len(late)),
        [shape((CAP, width), BF16)] * owners,
        [gain[None, :], w_gate[0], w_up[0], w_down[0], arrived, part, *late],
        micros=2,
    )
    back = exchange(done)
    (hidden,) = call(
        functools.partial(project_kernel, entries),
        [shape((tok_rows, width), F32)],
        [attended, residual[0], *pieces],
        micros=2,
    )
    parts = math.gcd(tok_rows // 16, 4)
    (out,) = call(
        functools.partial(combine_kernel, owners, parts),
        [shape((tok_rows, width), BF16)],
        [hidden, mix, *back],
        micros=1,
        free_out=1,
        scratch=[pltpu.VMEM((tok_rows, width), BF16), pltpu.SemaphoreType.DMA((parts,))],
    )
    return out[None]


def solution(mesh):
    return jax.shard_map(
        per_device,
        mesh=mesh,
        in_specs=(
            P(("dp", "exp"), "ctx", None),
            P(("dp", "exp"), "ctx", None),
            P(("dp", "exp"), "ctx", None),
            P(("dp", "exp"), None),
            P(("dp", "exp"), "ctx", None),
            P("ctx", None),
            P(),
            P(("dp", "exp"), "ctx", None),
            P(("dp", "exp"), "ctx", None),
            P("exp", None, None),
            P("exp", None, None),
            P("exp", None, None),
        ),
        out_specs=P(("dp", "exp"), "ctx", None),
        check_vma=False,
    )
```

```python
import functools
import math

import jax
import jax.numpy as jnp
from jax import lax
from jax.experimental import pallas as pl
from jax.experimental.pallas import tpu as pltpu
from jax.sharding import PartitionSpec as P

HQ = 16
KVH = 2
HD = 128
GROUPS = HQ // KVH
CAP = 24
NEG = -1e30
SCORE_SCALE = math.log2(math.e) / math.sqrt(HD)
F32 = jnp.float32
BF16 = jnp.bfloat16


def slab_segments(segs_ref, index, count, rows):
    found = segs_ref[:, 0:rows]
    for slab in range(1, count):
        found = jnp.where(index == slab, segs_ref[:, slab * rows : (slab + 1) * rows], found)
    return found


def score_bias(segs_ref, backs, count, rows):
    me = lax.axis_index("ctx")
    row = lax.broadcasted_iota(jnp.int32, (rows, rows), 0)
    col = lax.broadcasted_iota(jnp.int32, (rows, rows), 1)
    own_seg = slab_segments(segs_ref, me, count, rows)
    query_seg = jnp.sum(jnp.where(row == col, own_seg, 0), axis=1, keepdims=True)
    parts = []
    for back in backs:
        if back == 0:
            allowed = (col <= row) & (own_seg == query_seg)
        else:
            key_seg = slab_segments(segs_ref, jnp.maximum(me - back, 0), count, rows)
            allowed = (key_seg == query_seg) & (me >= back)
        parts.append(jnp.where(allowed, 0.0, NEG))
    return parts


def group_scores(stacked, keys, bias):
    scores = lax.dot_general(
        stacked, keys, (((1,), (1,)), ((), ())), preferred_element_type=F32
    )
    return scores.reshape(GROUPS, *bias.shape) * SCORE_SCALE + bias


def weigh(expo, values):
    rows = expo.shape[0] * expo.shape[1]
    mixed = jnp.dot(
        expo.astype(BF16).reshape(rows, expo.shape[2]), values, preferred_element_type=F32
    ).reshape(*expo.shape[:2], 2 * HD)
    return mixed[:, :, :HD], mixed[:, :, HD:]


def mark_kernel(*refs):
    refs[-1][...] = jnp.zeros_like(refs[-1])


def gate_kernel(*refs):
    del refs


def after(piece, *marks):
    spec = pl.BlockSpec(memory_space=pl.ANY)
    return pl.pallas_call(
        gate_kernel,
        out_shape=jax.ShapeDtypeStruct(piece.shape, piece.dtype),
        in_specs=[spec] * (1 + len(marks)),
        out_specs=spec,
        input_output_aliases={0: 0},
        compiler_params=pltpu.CompilerParams(vmem_limit_bytes=1 << 20),
    )(piece, *marks)


def join_kernel(first_ref, second_ref, mark_ref, whole_ref, sems):
    del mark_ref
    half = first_ref.shape[0]
    core = lax.rem(lax.axis_index("dp"), 2)
    copies = []
    for index, (lead, ref) in enumerate([(core, first_ref), (1 - core, second_ref)]):
        target = whole_ref.at[pl.ds(pl.multiple_of(lead * half, half), half)]
        copies.append(pltpu.make_async_copy(ref, target, sems.at[index]))
        copies[-1].start()
    for copy in copies:
        copy.wait()


def own_kernel(
    n_ctx,
    q_ref,
    kv_ref,
    segs_ref,
    mark_ref,
    w_ref,
    acc_ref,
    max_ref,
    sum_ref,
    queries_ref,
    first_ref,
    second_ref,
    sems,
):
    del mark_ref
    half = first_ref.shape[0]
    core = lax.rem(lax.axis_index("dp"), 2)
    copies = []
    for index, (lead, ref) in enumerate([(core, first_ref), (1 - core, second_ref)]):
        source = w_ref.at[pl.ds(pl.multiple_of(lead * half, half), half)]
        copies.append(pltpu.make_async_copy(source, ref, sems.at[index]))
        copies[-1].start()
    rows = q_ref.shape[0]
    (bias,) = score_bias(segs_ref, (0,), n_ctx, rows)
    ones = jnp.ones((rows, HD), BF16)
    for kv in range(KVH):
        keys = kv_ref[:, kv * HD : (kv + 1) * HD]
        values = jnp.concatenate([kv_ref[:, (KVH + kv) * HD : (KVH + kv + 1) * HD], ones], axis=1)
        heads = range(kv * GROUPS, (kv + 1) * GROUPS)
        stacked = jnp.concatenate([q_ref[:, h * HD : (h + 1) * HD] for h in heads], axis=0)
        queries_ref[kv] = stacked
        scores = group_scores(stacked, keys, bias)
        row_max = jnp.max(scores, axis=2, keepdims=True)
        accum, row_sum = weigh(jnp.exp2(scores - row_max), values)
        acc_ref[kv] = accum
        max_ref[kv] = jnp.broadcast_to(row_max, max_ref.shape[1:])
        sum_ref[kv] = row_sum
    for copy in copies:
        copy.wait()


def route_kernel(ids_ref, rw_ref, res_ref, place_ref, mix_ref, rows_ref):
    slots, rows = place_ref.shape
    slot = lax.broadcasted_iota(jnp.int32, (slots, rows), 0)
    owner = (slot // CAP) ^ lax.axis_index("exp")
    hit = jnp.zeros((slots, rows), jnp.bool_)
    weight = jnp.zeros((slots, rows), F32)
    for choice in range(ids_ref.shape[0]):
        same = ids_ref[choice : choice + 1, :] == owner
        hit = hit | same
        weight = jnp.where(same, rw_ref[choice : choice + 1, :], weight)
    row = lax.broadcasted_iota(jnp.int32, (rows, rows), 0)
    col = lax.broadcasted_iota(jnp.int32, (rows, rows), 1)
    before = (row < col).astype(F32).astype(BF16)
    rank = jnp.dot(hit.astype(F32).astype(BF16), before, preferred_element_type=F32)
    placed = hit & (rank == lax.rem(slot, CAP).astype(F32))
    place = placed.astype(F32).astype(BF16)
    place_ref[...] = place
    mix = jnp.where(placed, weight, 0.0)
    high = mix.astype(BF16).astype(F32)
    mix_ref[...] = jnp.concatenate([high, mix - high], axis=0).T.astype(BF16)
    rows_ref[...] = jnp.dot(place, res_ref[...], preferred_element_type=F32)


def rest_kernel(
    n_ctx,
    back_count,
    segs_ref,
    acc_ref,
    max_ref,
    sum_ref,
    queries_ref,
    place_ref,
    *refs,
):
    kv_refs, (out_ref, routed_ref) = refs[:back_count], refs[-2:]
    rows = queries_ref.shape[1] // GROUPS
    bias = jnp.concatenate(score_bias(segs_ref, range(1, back_count + 1), n_ctx, rows), axis=1)
    keys_count = rows * back_count
    spread = -(-keys_count // HD)
    ones = jnp.ones((keys_count, HD), BF16)
    scores = []
    for kv in range(KVH):
        keys = jnp.concatenate([ref[:, kv * HD : (kv + 1) * HD] for ref in kv_refs], axis=0)
        scores.append(group_scores(queries_ref[kv], keys, bias))
    for kv in range(KVH):
        values = jnp.concatenate(
            [ref[:, (KVH + kv) * HD : (KVH + kv + 1) * HD] for ref in kv_refs], axis=0
        )
        values = jnp.concatenate([values, ones], axis=1)
        old_max = max_ref[kv]
        new_max = jnp.maximum(old_max, jnp.max(scores[kv], axis=2, keepdims=True))
        shift = jnp.concatenate([new_max] * spread, axis=2)[:, :, :keys_count]
        accum, row_sum = weigh(jnp.exp2(scores[kv] - shift), values)
        fix = jnp.exp2(old_max - new_max)
        total = sum_ref[kv] * fix + row_sum
        attended = ((acc_ref[kv] * fix + accum) / total).astype(BF16)
        for group in range(GROUPS):
            head = kv * GROUPS + group
            out_ref[:, head * HD : (head + 1) * HD] = attended[group]
    routed_ref[...] = jnp.dot(place_ref[...], out_ref[...], preferred_element_type=F32)


def send_kernel(blocks, entries, owners, routed_ref, rows_ref, *refs):
    piece_refs, send_refs = refs[:-owners], refs[-owners:]
    me, core = lax.axis_index("ctx"), lax.axis_index("dp")
    share = routed_ref.shape[1] // lax.axis_size("ctx")
    part = project(rows_ref[...], routed_ref, entries, piece_refs, False)
    for step, ref in enumerate(send_refs):
        rows = pl.ds(step * CAP, CAP)
        filled = 0
        for size, flip, offset in blocks:
            lead = pl.multiple_of((me ^ flip(core)) * share + offset(core), size)
            ref[:, filled : filled + size] = routed_ref[rows, pl.ds(lead, size)].astype(BF16)
            filled += size
        ref[:, filled:] = part[step * CAP : (step + 1) * CAP, :].astype(BF16)


def stack(parts):
    return jnp.concatenate([part.astype(F32) for part in parts], axis=0).astype(BF16)


def project(total, att_ref, entries, piece_refs, moved):
    me, core = lax.axis_index("ctx"), lax.axis_index("dp")
    share = att_ref.shape[1] // lax.axis_size("ctx")
    for piece, size, flip, offset, row, column in entries:
        lead = column(core) if moved else (me ^ flip(core)) * share + offset(core)
        columns = pl.ds(pl.multiple_of(lead, size), size)
        rows = pl.ds(pl.multiple_of(row(me, core), size), size)
        total = total + jnp.dot(
            att_ref[:, columns].astype(BF16),
            piece_refs[piece][rows, :],
            preferred_element_type=F32,
        )
    return total


def arrive_kernel(owners, entries, *refs):
    row_refs, piece_refs, (att_ref, hidden_ref) = refs[:owners], refs[owners:-2], refs[-2:]
    row_refs = in_order(row_refs)
    wide = att_ref.shape[1]
    att_ref[...] = stack([ref[:, :wide] for ref in row_refs])
    hidden = jnp.concatenate([ref[:, wide:].astype(F32) for ref in row_refs], axis=0)
    hidden_ref[...] = project(hidden, att_ref, entries, piece_refs, True)


def expert_kernel(entries, count, gain_ref, gate_ref, up_ref, down_ref, att_ref, part_ref, *refs):
    piece_refs, out_refs = refs[:count], refs[count:]
    hidden = project(part_ref[...], att_ref, entries, piece_refs, True)
    mean = jnp.mean(hidden * hidden, axis=1, keepdims=True)
    normed = (hidden * lax.rsqrt(mean + 1e-06) * gain_ref[...]).astype(BF16)
    gate = jnp.dot(normed, gate_ref[...], preferred_element_type=F32)
    up = jnp.dot(normed, up_ref[...], preferred_element_type=F32)
    act = (gate / (1.0 + jnp.exp(-gate)) * up).astype(BF16)
    out = jnp.dot(act, down_ref[...], preferred_element_type=F32)
    for step, ref in enumerate(out_refs):
        ref[...] = out[step * CAP : (step + 1) * CAP, :].astype(BF16)


def project_kernel(entries, att_ref, res_ref, *refs):
    hidden = res_ref[...].astype(F32)
    refs[-1][...] = project(hidden, att_ref, entries, refs[:-1], False)


def combine_kernel(owners, hidden_ref, mix_ref, *refs):
    row_refs, out_ref = in_order(refs[:owners]), refs[owners]
    rows = stack([ref[...] for ref in row_refs])
    total = hidden_ref[...] + jnp.dot(
        mix_ref[...], jnp.concatenate([rows, rows], axis=0), preferred_element_type=F32
    )
    out_ref[...] = total.astype(BF16)


def call(kernel, outs, args, micros, scratch=(), limit=24, free_in=0, free_out=0):
    vmem, free = pl.BlockSpec(memory_space=pltpu.VMEM), pl.BlockSpec(memory_space=pl.ANY)
    nbytes = sum(math.prod(a.shape) * a.dtype.itemsize for a in list(args) + list(outs))
    return pl.pallas_call(
        kernel,
        out_shape=outs,
        in_specs=[vmem] * (len(args) - free_in) + [free] * free_in,
        out_specs=[vmem] * (len(outs) - free_out) + [free] * free_out,
        scratch_shapes=list(scratch),
        compiler_params=pltpu.CompilerParams(vmem_limit_bytes=limit << 20),
        cost_estimate=pl.CostEstimate(
            flops=int(micros * 1.15e9), bytes_accessed=nbytes, transcendentals=0
        ),
    )(*args)


def far_first(count):
    return sorted(range(1, count), key=lambda s: (-s.bit_length(), s))


def in_order(refs):
    order = far_first(len(refs))
    return [refs[0]] + [refs[1 + order.index(s)] for s in range(1, len(refs))]


def exchange(blocks):
    count = len(blocks)
    return [blocks[0]] + [
        lax.ppermute(blocks[s], "exp", [(i, i ^ s) for i in range(count)])
        for s in far_first(count)
    ]


def gather_weight(weight, first, second, attended):
    n_ctx, cores = lax.axis_size("ctx"), lax.axis_size("dp")
    share = weight.shape[0]
    if (n_ctx, cores) != (4, 2):
        whole = lax.all_gather(weight, "ctx", axis=0, tiled=True)
        entries = [
            (
                0,
                share,
                lambda core, f=f: f,
                lambda core: 0,
                lambda me, core, f=f: (me ^ f) * share,
                lambda core, f=f: (f - 1) * share,
            )
            for f in range(n_ctx)
        ]
        home = [(0, share, lambda core: 0, lambda core: 0, lambda me, core: 0, None)]
        blocks = [(share, lambda core, f=f: f, lambda core: 0) for f in range(1, n_ctx)]
        return [whole], entries, entries[1:], [weight], home, blocks
    both = ("ctx", "dp")
    devices = [(me, core) for me in range(n_ctx) for core in range(cores)]
    aside = [(me * 2 + core, (me ^ (1 + core)) * 2 + core) for me, core in devices]
    across = [(me * 2 + core, (me ^ (2 - core)) * 2 + core) for me, core in devices]
    near_first = lax.ppermute(first, both, aside)
    near_second = lax.ppermute(second, both, aside)
    near_first = after(near_first, attended)
    far = lax.ppermute(near_first, both, across)
    (near,) = call(
        join_kernel,
        [jax.ShapeDtypeStruct(weight.shape, BF16)],
        [near_first, near_second, attended],
        micros=1,
        free_in=3,
        free_out=1,
        limit=1,
        scratch=[pltpu.SemaphoreType.DMA((2,))],
    )
    swap = [(0, 1), (1, 0)]
    pieces = [weight, near, far, lax.ppermute(near, "dp", swap), lax.ppermute(far, "dp", swap)]
    half = share // 2
    top = lambda me, core: 0
    entries = [
        (0, share, lambda core: 0, lambda core: 0, top, None),
        (1, share, lambda core: 1 + core, lambda core: 0, top, None),
        (2, half, lambda core: 3, lambda core: core * half, top, None),
        (3, share, lambda core: 2 - core, lambda core: 0, top, None),
        (4, half, lambda core: 3, lambda core: (1 - core) * half, top, None),
    ]
    moved = [
        (1, half, None, None, lambda me, core: (1 - core) * half, lambda core: 0),
        (2, half, None, None, top, lambda core: (3 + core) * half),
        (3, half, None, None, top, lambda core: half),
        (3, half, None, None, lambda me, core: half, lambda core: 2 * half),
        (4, half, None, None, top, lambda core: (4 - core) * half),
    ]
    home = [
        (0, share, lambda core: 0, lambda core: 0, top, None),
        (1, half, lambda core: 1 + core, lambda core: core * half, top, None),
    ]
    blocks = [
        (half, lambda core: 1 + core, lambda core: (1 - core) * half),
        (share, lambda core: 2 - core, lambda core: 0),
        (share, lambda core: 3, lambda core: 0),
    ]
    return pieces, entries, moved, [weight, near_first], home, blocks


def per_device(
    queries,
    keys,
    values,
    segments,
    residual,
    out_weight,
    gain,
    expert_ids,
    route_weights,
    w_gate,
    w_up,
    w_down,
):
    tok_rows = queries.shape[1]
    width = residual.shape[2]
    att_width = queries.shape[2]
    n_ctx, owners = lax.axis_size("ctx"), lax.axis_size("exp")
    slots = owners * CAP
    longest = segments.shape[1] // 2
    back_count = min(n_ctx - 1, -(-(longest - 1) // tok_rows))
    shape = jax.ShapeDtypeStruct

    own_kv = jnp.concatenate([keys[0], values[0]], axis=1)
    kv_blocks = []
    for back in range(1, back_count + 1):
        pairs = [(i, (i + back) % n_ctx) for i in range(n_ctx)]
        kv_blocks.append(lax.ppermute(own_kv, "ctx", pairs))
    (mark,) = call(mark_kernel, [shape((8, 128), F32)], [own_kv], micros=5, free_in=1, limit=1)
    half = shape((out_weight.shape[0] // 2, width), BF16)
    accum, row_max, row_sum, stacked, first, second = call(
        functools.partial(own_kernel, n_ctx),
        [
            shape((KVH, GROUPS, tok_rows, HD), F32),
            shape((KVH, GROUPS, tok_rows, HD), F32),
            shape((KVH, GROUPS, tok_rows, HD), F32),
            shape((KVH, GROUPS * tok_rows, HD), BF16),
            half,
            half,
        ],
        [queries[0], own_kv, segments, mark, out_weight],
        micros=3,
        free_in=1,
        free_out=2,
        scratch=[pltpu.SemaphoreType.DMA((2,))],
    )
    place, mix, res_rows = call(
        route_kernel,
        [
            shape((slots, tok_rows), BF16),
            shape((tok_rows, 2 * slots), BF16),
            shape((slots, width), F32),
        ],
        [expert_ids[0].T, route_weights[0].T, residual[0]],
        micros=1,
    )
    attended, chosen = call(
        functools.partial(rest_kernel, n_ctx, back_count),
        [shape((tok_rows, att_width), BF16), shape((slots, att_width), F32)],
        [segments, accum, row_max, row_sum, stacked, place, *kv_blocks]
        + [gain[None, :], w_gate[0], w_up[0], w_down[0]],
        micros=5,
    )
    pieces, entries, moved, near, home, blocks = gather_weight(
        out_weight, first, second, attended
    )
    moved_width = sum(size for size, _, _ in blocks)
    routed = call(
        functools.partial(send_kernel, blocks, home, owners),
        [shape((CAP, moved_width + width), BF16)] * owners,
        [chosen, res_rows, *near],
        micros=1,
    )
    early = pieces[1:2]
    late = pieces[2:] or pieces
    now = [(0, *entry[1:]) for entry in moved if early and entry[0] == 1]
    skipped = len(pieces) - len(late)
    then = [(entry[0] - skipped, *entry[1:]) for entry in moved if entry[0] >= skipped]
    arrived, part = call(
        functools.partial(arrive_kernel, owners, now),
        [shape((slots, moved_width), BF16), shape((slots, width), F32)],
        [*exchange(routed), *early],
        micros=10,
    )
    done = call(
        functools.partial(expert_kernel, then, len(late)),
        [shape((CAP, width), BF16)] * owners,
        [gain[None, :], w_gate[0], w_up[0], w_down[0], arrived, part, *late],
        micros=2,
    )
    back = exchange(done)
    (hidden,) = call(
        functools.partial(project_kernel, entries),
        [shape((tok_rows, width), F32)],
        [attended, residual[0], *pieces],
        micros=2,
    )
    (out,) = call(
        functools.partial(combine_kernel, owners),
        [shape((tok_rows, width), BF16)],
        [hidden, mix, *back],
        micros=1,
    )
    return out[None]


def solution(mesh):
    return jax.shard_map(
        per_device,
        mesh=mesh,
        in_specs=(
            P(("dp", "exp"), "ctx", None),
            P(("dp", "exp"), "ctx", None),
            P(("dp", "exp"), "ctx", None),
            P(("dp", "exp"), None),
            P(("dp", "exp"), "ctx", None),
            P("ctx", None),
            P(),
            P(("dp", "exp"), "ctx", None),
            P(("dp", "exp"), "ctx", None),
            P("exp", None, None),
            P("exp", None, None),
            P("exp", None, None),
        ),
        out_specs=P(("dp", "exp"), "ctx", None),
        check_vma=False,
    )
```

```python
import functools
import math

import jax
import jax.numpy as jnp
from jax import lax
from jax.experimental import pallas as pl
from jax.experimental.pallas import tpu as pltpu
from jax.sharding import PartitionSpec as P

HQ = 16
KVH = 2
HD = 128
GROUPS = HQ // KVH
CAP = 24
NEG = -1e30
SCORE_SCALE = math.log2(math.e) / math.sqrt(HD)
F32 = jnp.float32
BF16 = jnp.bfloat16


def slab_segments(segs_ref, index, count, rows):
    found = segs_ref[:, 0:rows]
    for slab in range(1, count):
        found = jnp.where(index == slab, segs_ref[:, slab * rows : (slab + 1) * rows], found)
    return found


def score_bias(segs_ref, backs, count, rows):
    me = lax.axis_index("ctx")
    row = lax.broadcasted_iota(jnp.int32, (rows, rows), 0)
    col = lax.broadcasted_iota(jnp.int32, (rows, rows), 1)
    own_seg = slab_segments(segs_ref, me, count, rows)
    query_seg = jnp.sum(jnp.where(row == col, own_seg, 0), axis=1, keepdims=True)
    parts = []
    for back in backs:
        if back == 0:
            allowed = (col <= row) & (own_seg == query_seg)
        else:
            key_seg = slab_segments(segs_ref, jnp.maximum(me - back, 0), count, rows)
            allowed = (key_seg == query_seg) & (me >= back)
        parts.append(jnp.where(allowed, 0.0, NEG))
    return parts


def group_scores(stacked, keys, bias):
    scores = lax.dot_general(
        stacked, keys, (((1,), (1,)), ((), ())), preferred_element_type=F32
    )
    return scores.reshape(GROUPS, *bias.shape) * SCORE_SCALE + bias


def weigh(expo, values):
    rows = expo.shape[0] * expo.shape[1]
    mixed = jnp.dot(
        expo.astype(BF16).reshape(rows, expo.shape[2]), values, preferred_element_type=F32
    ).reshape(*expo.shape[:2], 2 * HD)
    return mixed[:, :, :HD], mixed[:, :, HD:]


def mark_kernel(*refs):
    refs[-1][...] = jnp.zeros_like(refs[-1])


def gate_kernel(*refs):
    del refs


def after(piece, *marks):
    spec = pl.BlockSpec(memory_space=pl.ANY)
    return pl.pallas_call(
        gate_kernel,
        out_shape=jax.ShapeDtypeStruct(piece.shape, piece.dtype),
        in_specs=[spec] * (1 + len(marks)),
        out_specs=spec,
        input_output_aliases={0: 0},
        compiler_params=pltpu.CompilerParams(vmem_limit_bytes=1 << 20),
    )(piece, *marks)


def join_kernel(first_ref, second_ref, mark_ref, whole_ref, sems):
    del mark_ref
    half = first_ref.shape[0]
    core = lax.rem(lax.axis_index("dp"), 2)
    copies = []
    for index, (lead, ref) in enumerate([(core, first_ref), (1 - core, second_ref)]):
        target = whole_ref.at[pl.ds(pl.multiple_of(lead * half, half), half)]
        copies.append(pltpu.make_async_copy(ref, target, sems.at[index]))
        copies[-1].start()
    for copy in copies:
        copy.wait()


def own_kernel(
    n_ctx,
    q_ref,
    kv_ref,
    segs_ref,
    mark_ref,
    w_ref,
    acc_ref,
    max_ref,
    sum_ref,
    queries_ref,
    first_ref,
    second_ref,
    sems,
):
    del mark_ref
    half = first_ref.shape[0]
    core = lax.rem(lax.axis_index("dp"), 2)
    copies = []
    for index, (lead, ref) in enumerate([(core, first_ref), (1 - core, second_ref)]):
        source = w_ref.at[pl.ds(pl.multiple_of(lead * half, half), half)]
        copies.append(pltpu.make_async_copy(source, ref, sems.at[index]))
        copies[-1].start()
    rows = q_ref.shape[0]
    (bias,) = score_bias(segs_ref, (0,), n_ctx, rows)
    ones = jnp.ones((rows, HD), BF16)
    for kv in range(KVH):
        keys = kv_ref[:, kv * HD : (kv + 1) * HD]
        values = jnp.concatenate([kv_ref[:, (KVH + kv) * HD : (KVH + kv + 1) * HD], ones], axis=1)
        heads = range(kv * GROUPS, (kv + 1) * GROUPS)
        stacked = jnp.concatenate([q_ref[:, h * HD : (h + 1) * HD] for h in heads], axis=0)
        queries_ref[kv] = stacked
        scores = group_scores(stacked, keys, bias)
        row_max = jnp.max(scores, axis=2, keepdims=True)
        accum, row_sum = weigh(jnp.exp2(scores - row_max), values)
        acc_ref[kv] = accum
        max_ref[kv] = jnp.broadcast_to(row_max, max_ref.shape[1:])
        sum_ref[kv] = row_sum
    for copy in copies:
        copy.wait()


def route_kernel(ids_ref, rw_ref, res_ref, place_ref, mix_ref, rows_ref):
    slots, rows = place_ref.shape
    slot = lax.broadcasted_iota(jnp.int32, (slots, rows), 0)
    owner = lax.rem(slot // CAP + lax.axis_index("exp"), slots // CAP)
    hit = jnp.zeros((slots, rows), jnp.bool_)
    weight = jnp.zeros((slots, rows), F32)
    for choice in range(ids_ref.shape[0]):
        same = ids_ref[choice : choice + 1, :] == owner
        hit = hit | same
        weight = jnp.where(same, rw_ref[choice : choice + 1, :], weight)
    row = lax.broadcasted_iota(jnp.int32, (rows, rows), 0)
    col = lax.broadcasted_iota(jnp.int32, (rows, rows), 1)
    before = (row < col).astype(F32).astype(BF16)
    rank = jnp.dot(hit.astype(F32).astype(BF16), before, preferred_element_type=F32)
    placed = hit & (rank == lax.rem(slot, CAP).astype(F32))
    place = placed.astype(F32).astype(BF16)
    place_ref[...] = place
    mix = jnp.where(placed, weight, 0.0)
    high = mix.astype(BF16).astype(F32)
    mix_ref[...] = jnp.concatenate([high, mix - high], axis=0).T.astype(BF16)
    rows_ref[...] = jnp.dot(place, res_ref[...], preferred_element_type=F32)


def rest_kernel(
    n_ctx,
    back_count,
    segs_ref,
    acc_ref,
    max_ref,
    sum_ref,
    queries_ref,
    place_ref,
    *refs,
):
    kv_refs, (out_ref, routed_ref) = refs[:back_count], refs[-2:]
    rows = queries_ref.shape[1] // GROUPS
    bias = jnp.concatenate(score_bias(segs_ref, range(1, back_count + 1), n_ctx, rows), axis=1)
    keys_count = rows * back_count
    spread = -(-keys_count // HD)
    ones = jnp.ones((keys_count, HD), BF16)
    scores = []
    for kv in range(KVH):
        keys = jnp.concatenate([ref[:, kv * HD : (kv + 1) * HD] for ref in kv_refs], axis=0)
        scores.append(group_scores(queries_ref[kv], keys, bias))
    for kv in range(KVH):
        values = jnp.concatenate(
            [ref[:, (KVH + kv) * HD : (KVH + kv + 1) * HD] for ref in kv_refs], axis=0
        )
        values = jnp.concatenate([values, ones], axis=1)
        old_max = max_ref[kv]
        new_max = jnp.maximum(old_max, jnp.max(scores[kv], axis=2, keepdims=True))
        shift = jnp.concatenate([new_max] * spread, axis=2)[:, :, :keys_count]
        accum, row_sum = weigh(jnp.exp2(scores[kv] - shift), values)
        fix = jnp.exp2(old_max - new_max)
        total = sum_ref[kv] * fix + row_sum
        attended = ((acc_ref[kv] * fix + accum) / total).astype(BF16)
        for group in range(GROUPS):
            head = kv * GROUPS + group
            out_ref[:, head * HD : (head + 1) * HD] = attended[group]
    routed_ref[...] = jnp.dot(place_ref[...], out_ref[...], preferred_element_type=F32)


def send_kernel(blocks, entries, owners, routed_ref, rows_ref, *refs):
    piece_refs, send_refs = refs[:-owners], refs[-owners:]
    me, core = lax.axis_index("ctx"), lax.axis_index("dp")
    share = routed_ref.shape[1] // lax.axis_size("ctx")
    part = project(rows_ref[...], routed_ref, entries, piece_refs, False)
    for step, ref in enumerate(send_refs):
        rows = pl.ds(step * CAP, CAP)
        filled = 0
        for size, flip, offset in blocks:
            lead = pl.multiple_of((me ^ flip(core)) * share + offset(core), size)
            ref[:, filled : filled + size] = routed_ref[rows, pl.ds(lead, size)].astype(BF16)
            filled += size
        ref[:, filled:] = part[step * CAP : (step + 1) * CAP, :].astype(BF16)


def stack(parts):
    return jnp.concatenate([part.astype(F32) for part in parts], axis=0).astype(BF16)


def project(total, att_ref, entries, piece_refs, moved):
    me, core = lax.axis_index("ctx"), lax.axis_index("dp")
    share = att_ref.shape[1] // lax.axis_size("ctx")
    for piece, size, flip, offset, row, column in entries:
        lead = column(core) if moved else (me ^ flip(core)) * share + offset(core)
        columns = pl.ds(pl.multiple_of(lead, size), size)
        rows = pl.ds(pl.multiple_of(row(me, core), size), size)
        total = total + jnp.dot(
            att_ref[:, columns].astype(BF16),
            piece_refs[piece][rows, :],
            preferred_element_type=F32,
        )
    return total


def arrive_kernel(owners, entries, *refs):
    row_refs, piece_refs, (att_ref, hidden_ref) = refs[:owners], refs[owners:-2], refs[-2:]
    row_refs = in_order(row_refs, list(range(1, owners)))
    wide = att_ref.shape[1]
    att_ref[...] = stack([ref[:, :wide] for ref in row_refs])
    hidden = jnp.concatenate([ref[:, wide:].astype(F32) for ref in row_refs], axis=0)
    hidden_ref[...] = project(hidden, att_ref, entries, piece_refs, True)


def expert_kernel(entries, count, gain_ref, gate_ref, up_ref, down_ref, att_ref, part_ref, *refs):
    piece_refs, out_refs = refs[:count], refs[count:]
    hidden = project(part_ref[...], att_ref, entries, piece_refs, True)
    mean = jnp.mean(hidden * hidden, axis=1, keepdims=True)
    normed = (hidden * lax.rsqrt(mean + 1e-06) * gain_ref[...]).astype(BF16)
    gate = jnp.dot(normed, gate_ref[...], preferred_element_type=F32)
    up = jnp.dot(normed, up_ref[...], preferred_element_type=F32)
    act = (gate / (1.0 + jnp.exp(-gate)) * up).astype(BF16)
    out = jnp.dot(act, down_ref[...], preferred_element_type=F32)
    for step, ref in enumerate(out_refs):
        ref[...] = out[step * CAP : (step + 1) * CAP, :].astype(BF16)


def project_kernel(entries, att_ref, res_ref, *refs):
    hidden = res_ref[...].astype(F32)
    refs[-1][...] = project(hidden, att_ref, entries, refs[:-1], False)


def combine_kernel(owners, hidden_ref, mix_ref, *refs):
    row_refs, out_ref = in_order(refs[:owners], list(range(owners - 1, 0, -1))), refs[owners]
    rows = stack([ref[...] for ref in row_refs])
    total = hidden_ref[...] + jnp.dot(
        mix_ref[...], jnp.concatenate([rows, rows], axis=0), preferred_element_type=F32
    )
    out_ref[...] = total.astype(BF16)


def call(kernel, outs, args, micros, scratch=(), limit=24, free_in=0, free_out=0):
    vmem, free = pl.BlockSpec(memory_space=pltpu.VMEM), pl.BlockSpec(memory_space=pl.ANY)
    nbytes = sum(math.prod(a.shape) * a.dtype.itemsize for a in list(args) + list(outs))
    return pl.pallas_call(
        kernel,
        out_shape=outs,
        in_specs=[vmem] * (len(args) - free_in) + [free] * free_in,
        out_specs=[vmem] * (len(outs) - free_out) + [free] * free_out,
        scratch_shapes=list(scratch),
        compiler_params=pltpu.CompilerParams(vmem_limit_bytes=limit << 20),
        cost_estimate=pl.CostEstimate(
            flops=int(micros * 1.15e9), bytes_accessed=nbytes, transcendentals=0
        ),
    )(*args)


def in_order(refs, order):
    return [refs[0]] + [refs[1 + order.index(s)] for s in range(1, len(refs))]


def exchange(blocks, sign, order):
    count = len(blocks)
    return [blocks[0]] + [
        lax.ppermute(blocks[s], "exp", [(i, (i + sign * s) % count) for i in range(count)])
        for s in order
    ]


def gather_weight(weight, first, second, attended):
    n_ctx, cores = lax.axis_size("ctx"), lax.axis_size("dp")
    share = weight.shape[0]
    if (n_ctx, cores) != (4, 2):
        whole = lax.all_gather(weight, "ctx", axis=0, tiled=True)
        entries = [
            (
                0,
                share,
                lambda core, f=f: f,
                lambda core: 0,
                lambda me, core, f=f: (me ^ f) * share,
                lambda core, f=f: (f - 1) * share,
            )
            for f in range(n_ctx)
        ]
        home = [(0, share, lambda core: 0, lambda core: 0, lambda me, core: 0, None)]
        blocks = [(share, lambda core, f=f: f, lambda core: 0) for f in range(1, n_ctx)]
        return [whole], entries, entries[1:], [weight], home, blocks
    both = ("ctx", "dp")
    devices = [(me, core) for me in range(n_ctx) for core in range(cores)]
    aside = [(me * 2 + core, (me ^ (1 + core)) * 2 + core) for me, core in devices]
    across = [(me * 2 + core, (me ^ (2 - core)) * 2 + core) for me, core in devices]
    near_first = lax.ppermute(first, both, aside)
    near_second = lax.ppermute(second, both, aside)
    near_first = after(near_first, attended)
    far = lax.ppermute(near_first, both, across)
    (near,) = call(
        join_kernel,
        [jax.ShapeDtypeStruct(weight.shape, BF16)],
        [near_first, near_second, attended],
        micros=1,
        free_in=3,
        free_out=1,
        limit=1,
        scratch=[pltpu.SemaphoreType.DMA((2,))],
    )
    swap = [(0, 1), (1, 0)]
    pieces = [weight, near, far, lax.ppermute(near, "dp", swap), lax.ppermute(far, "dp", swap)]
    half = share // 2
    top = lambda me, core: 0
    entries = [
        (0, share, lambda core: 0, lambda core: 0, top, None),
        (1, share, lambda core: 1 + core, lambda core: 0, top, None),
        (2, half, lambda core: 3, lambda core: core * half, top, None),
        (3, share, lambda core: 2 - core, lambda core: 0, top, None),
        (4, half, lambda core: 3, lambda core: (1 - core) * half, top, None),
    ]
    moved = [
        (1, half, None, None, lambda me, core: (1 - core) * half, lambda core: 0),
        (2, half, None, None, top, lambda core: (3 + core) * half),
        (3, half, None, None, top, lambda core: half),
        (3, half, None, None, lambda me, core: half, lambda core: 2 * half),
        (4, half, None, None, top, lambda core: (4 - core) * half),
    ]
    home = [
        (0, share, lambda core: 0, lambda core: 0, top, None),
        (1, half, lambda core: 1 + core, lambda core: core * half, top, None),
    ]
    blocks = [
        (half, lambda core: 1 + core, lambda core: (1 - core) * half),
        (share, lambda core: 2 - core, lambda core: 0),
        (share, lambda core: 3, lambda core: 0),
    ]
    return pieces, entries, moved, [weight, near_first], home, blocks


def per_device(
    queries,
    keys,
    values,
    segments,
    residual,
    out_weight,
    gain,
    expert_ids,
    route_weights,
    w_gate,
    w_up,
    w_down,
):
    tok_rows = queries.shape[1]
    width = residual.shape[2]
    att_width = queries.shape[2]
    n_ctx, owners = lax.axis_size("ctx"), lax.axis_size("exp")
    slots = owners * CAP
    longest = segments.shape[1] // 2
    back_count = min(n_ctx - 1, -(-(longest - 1) // tok_rows))
    shape = jax.ShapeDtypeStruct

    own_kv = jnp.concatenate([keys[0], values[0]], axis=1)
    kv_blocks = []
    for back in range(1, back_count + 1):
        pairs = [(i, (i + back) % n_ctx) for i in range(n_ctx)]
        kv_blocks.append(lax.ppermute(own_kv, "ctx", pairs))
    (mark,) = call(mark_kernel, [shape((8, 128), F32)], [own_kv], micros=5, free_in=1, limit=1)
    half = shape((out_weight.shape[0] // 2, width), BF16)
    accum, row_max, row_sum, stacked, first, second = call(
        functools.partial(own_kernel, n_ctx),
        [
            shape((KVH, GROUPS, tok_rows, HD), F32),
            shape((KVH, GROUPS, tok_rows, HD), F32),
            shape((KVH, GROUPS, tok_rows, HD), F32),
            shape((KVH, GROUPS * tok_rows, HD), BF16),
            half,
            half,
        ],
        [queries[0], own_kv, segments, mark, out_weight],
        micros=3,
        free_in=1,
        free_out=2,
        scratch=[pltpu.SemaphoreType.DMA((2,))],
    )
    place, mix, res_rows = call(
        route_kernel,
        [
            shape((slots, tok_rows), BF16),
            shape((tok_rows, 2 * slots), BF16),
            shape((slots, width), F32),
        ],
        [expert_ids[0].T, route_weights[0].T, residual[0]],
        micros=1,
    )
    attended, chosen = call(
        functools.partial(rest_kernel, n_ctx, back_count),
        [shape((tok_rows, att_width), BF16), shape((slots, att_width), F32)],
        [segments, accum, row_max, row_sum, stacked, place, *kv_blocks]
        + [gain[None, :], w_gate[0], w_up[0], w_down[0]],
        micros=5,
    )
    pieces, entries, moved, near, home, blocks = gather_weight(
        out_weight, first, second, attended
    )
    moved_width = sum(size for size, _, _ in blocks)
    routed = call(
        functools.partial(send_kernel, blocks, home, owners),
        [shape((CAP, moved_width + width), BF16)] * owners,
        [chosen, res_rows, *near],
        micros=1,
    )
    early = pieces[1:2]
    late = pieces[2:] or pieces
    now = [(0, *entry[1:]) for entry in moved if early and entry[0] == 1]
    skipped = len(pieces) - len(late)
    then = [(entry[0] - skipped, *entry[1:]) for entry in moved if entry[0] >= skipped]
    arrived, part = call(
        functools.partial(arrive_kernel, owners, now),
        [shape((slots, moved_width), BF16), shape((slots, width), F32)],
        [*exchange(routed, 1, range(1, owners)), *early],
        micros=10,
    )
    done = call(
        functools.partial(expert_kernel, then, len(late)),
        [shape((CAP, width), BF16)] * owners,
        [gain[None, :], w_gate[0], w_up[0], w_down[0], arrived, part, *late],
        micros=2,
    )
    back = exchange(done, -1, range(owners - 1, 0, -1))
    (hidden,) = call(
        functools.partial(project_kernel, entries),
        [shape((tok_rows, width), F32)],
        [attended, residual[0], *pieces],
        micros=2,
    )
    (out,) = call(
        functools.partial(combine_kernel, owners),
        [shape((tok_rows, width), BF16)],
        [hidden, mix, *back],
        micros=1,
    )
    return out[None]


def solution(mesh):
    return jax.shard_map(
        per_device,
        mesh=mesh,
        in_specs=(
            P(("dp", "exp"), "ctx", None),
            P(("dp", "exp"), "ctx", None),
            P(("dp", "exp"), "ctx", None),
            P(("dp", "exp"), None),
            P(("dp", "exp"), "ctx", None),
            P("ctx", None),
            P(),
            P(("dp", "exp"), "ctx", None),
            P(("dp", "exp"), "ctx", None),
            P("exp", None, None),
            P("exp", None, None),
            P("exp", None, None),
        ),
        out_specs=P(("dp", "exp"), "ctx", None),
        check_vma=False,
    )
```

```python
import functools
import math

import jax
import jax.numpy as jnp
from jax import lax
from jax.experimental import pallas as pl
from jax.experimental.pallas import tpu as pltpu
from jax.sharding import PartitionSpec as P

HQ = 16
KVH = 2
HD = 128
GROUPS = HQ // KVH
CAP = 24
NEG = -1e30
SCORE_SCALE = math.log2(math.e) / math.sqrt(HD)
F32 = jnp.float32
BF16 = jnp.bfloat16


def slab_segments(segs_ref, index, count, rows):
    found = segs_ref[:, 0:rows]
    for slab in range(1, count):
        found = jnp.where(index == slab, segs_ref[:, slab * rows : (slab + 1) * rows], found)
    return found


def score_bias(segs_ref, backs, count, rows):
    me = lax.axis_index("ctx")
    row = lax.broadcasted_iota(jnp.int32, (rows, rows), 0)
    col = lax.broadcasted_iota(jnp.int32, (rows, rows), 1)
    own_seg = slab_segments(segs_ref, me, count, rows)
    query_seg = jnp.sum(jnp.where(row == col, own_seg, 0), axis=1, keepdims=True)
    parts = []
    for back in backs:
        if back == 0:
            allowed = (col <= row) & (own_seg == query_seg)
        else:
            key_seg = slab_segments(segs_ref, jnp.maximum(me - back, 0), count, rows)
            allowed = (key_seg == query_seg) & (me >= back)
        parts.append(jnp.where(allowed, 0.0, NEG))
    return parts


def group_scores(stacked, keys, bias):
    scores = lax.dot_general(
        stacked, keys, (((1,), (1,)), ((), ())), preferred_element_type=F32
    )
    return scores.reshape(GROUPS, *bias.shape) * SCORE_SCALE + bias


def weigh(expo, values):
    rows = expo.shape[0] * expo.shape[1]
    mixed = jnp.dot(
        expo.astype(BF16).reshape(rows, expo.shape[2]), values, preferred_element_type=F32
    ).reshape(*expo.shape[:2], 2 * HD)
    return mixed[:, :, :HD], mixed[:, :, HD:]


def mark_kernel(*refs):
    refs[-1][...] = jnp.zeros_like(refs[-1])


def gate_kernel(*refs):
    del refs


def after(piece, *marks):
    spec = pl.BlockSpec(memory_space=pl.ANY)
    return pl.pallas_call(
        gate_kernel,
        out_shape=jax.ShapeDtypeStruct(piece.shape, piece.dtype),
        in_specs=[spec] * (1 + len(marks)),
        out_specs=spec,
        input_output_aliases={0: 0},
        compiler_params=pltpu.CompilerParams(vmem_limit_bytes=1 << 20),
    )(piece, *marks)


def join_kernel(first_ref, second_ref, mark_ref, whole_ref, sems):
    del mark_ref
    half = first_ref.shape[0]
    core = lax.rem(lax.axis_index("dp"), 2)
    copies = []
    for index, (lead, ref) in enumerate([(core, first_ref), (1 - core, second_ref)]):
        target = whole_ref.at[pl.ds(pl.multiple_of(lead * half, half), half)]
        copies.append(pltpu.make_async_copy(ref, target, sems.at[index]))
        copies[-1].start()
    for copy in copies:
        copy.wait()


def own_kernel(
    n_ctx,
    q_ref,
    kv_ref,
    segs_ref,
    mark_ref,
    w_ref,
    acc_ref,
    max_ref,
    sum_ref,
    queries_ref,
    first_ref,
    second_ref,
    sems,
):
    del mark_ref
    half = first_ref.shape[0]
    core = lax.rem(lax.axis_index("dp"), 2)
    copies = []
    for index, (lead, ref) in enumerate([(core, first_ref), (1 - core, second_ref)]):
        source = w_ref.at[pl.ds(pl.multiple_of(lead * half, half), half)]
        copies.append(pltpu.make_async_copy(source, ref, sems.at[index]))
        copies[-1].start()
    rows = q_ref.shape[0]
    (bias,) = score_bias(segs_ref, (0,), n_ctx, rows)
    ones = jnp.ones((rows, HD), BF16)
    for kv in range(KVH):
        keys = kv_ref[:, kv * HD : (kv + 1) * HD]
        values = jnp.concatenate([kv_ref[:, (KVH + kv) * HD : (KVH + kv + 1) * HD], ones], axis=1)
        heads = range(kv * GROUPS, (kv + 1) * GROUPS)
        stacked = jnp.concatenate([q_ref[:, h * HD : (h + 1) * HD] for h in heads], axis=0)
        queries_ref[kv] = stacked
        scores = group_scores(stacked, keys, bias)
        row_max = jnp.max(scores, axis=2, keepdims=True)
        accum, row_sum = weigh(jnp.exp2(scores - row_max), values)
        acc_ref[kv] = accum
        max_ref[kv] = jnp.broadcast_to(row_max, max_ref.shape[1:])
        sum_ref[kv] = row_sum
    for copy in copies:
        copy.wait()


def route_kernel(ids_ref, rw_ref, res_ref, place_ref, mix_ref, rows_ref):
    slots, rows = place_ref.shape
    slot = lax.broadcasted_iota(jnp.int32, (slots, rows), 0)
    owner = lax.rem(slot // CAP + lax.axis_index("exp"), slots // CAP)
    hit = jnp.zeros((slots, rows), jnp.bool_)
    weight = jnp.zeros((slots, rows), F32)
    for choice in range(ids_ref.shape[0]):
        same = ids_ref[choice : choice + 1, :] == owner
        hit = hit | same
        weight = jnp.where(same, rw_ref[choice : choice + 1, :], weight)
    row = lax.broadcasted_iota(jnp.int32, (rows, rows), 0)
    col = lax.broadcasted_iota(jnp.int32, (rows, rows), 1)
    before = (row < col).astype(F32).astype(BF16)
    rank = jnp.dot(hit.astype(F32).astype(BF16), before, preferred_element_type=F32)
    placed = hit & (rank == lax.rem(slot, CAP).astype(F32))
    place = placed.astype(F32).astype(BF16)
    place_ref[...] = place
    mix = jnp.where(placed, weight, 0.0)
    high = mix.astype(BF16).astype(F32)
    mix_ref[...] = jnp.concatenate([high, mix - high], axis=0).T.astype(BF16)
    rows_ref[...] = jnp.dot(place, res_ref[...], preferred_element_type=F32)


def rest_kernel(
    n_ctx,
    back_count,
    segs_ref,
    acc_ref,
    max_ref,
    sum_ref,
    queries_ref,
    place_ref,
    *refs,
):
    kv_refs, (out_ref, routed_ref) = refs[:back_count], refs[-2:]
    rows = queries_ref.shape[1] // GROUPS
    bias = jnp.concatenate(score_bias(segs_ref, range(1, back_count + 1), n_ctx, rows), axis=1)
    keys_count = rows * back_count
    spread = -(-keys_count // HD)
    ones = jnp.ones((keys_count, HD), BF16)
    scores = []
    for kv in range(KVH):
        keys = jnp.concatenate([ref[:, kv * HD : (kv + 1) * HD] for ref in kv_refs], axis=0)
        scores.append(group_scores(queries_ref[kv], keys, bias))
    for kv in range(KVH):
        values = jnp.concatenate(
            [ref[:, (KVH + kv) * HD : (KVH + kv + 1) * HD] for ref in kv_refs], axis=0
        )
        values = jnp.concatenate([values, ones], axis=1)
        old_max = max_ref[kv]
        new_max = jnp.maximum(old_max, jnp.max(scores[kv], axis=2, keepdims=True))
        shift = jnp.concatenate([new_max] * spread, axis=2)[:, :, :keys_count]
        accum, row_sum = weigh(jnp.exp2(scores[kv] - shift), values)
        fix = jnp.exp2(old_max - new_max)
        total = sum_ref[kv] * fix + row_sum
        attended = ((acc_ref[kv] * fix + accum) / total).astype(BF16)
        for group in range(GROUPS):
            head = kv * GROUPS + group
            out_ref[:, head * HD : (head + 1) * HD] = attended[group]
    routed_ref[...] = jnp.dot(place_ref[...], out_ref[...], preferred_element_type=F32)


def send_kernel(blocks, entries, owners, routed_ref, rows_ref, *refs):
    piece_refs, send_refs = refs[:-owners], refs[-owners:]
    me, core = lax.axis_index("ctx"), lax.axis_index("dp")
    share = routed_ref.shape[1] // lax.axis_size("ctx")
    part = project(rows_ref[...], routed_ref, entries, piece_refs, False)
    for step, ref in enumerate(send_refs):
        rows = pl.ds(step * CAP, CAP)
        filled = 0
        for size, flip, offset in blocks:
            lead = pl.multiple_of((me ^ flip(core)) * share + offset(core), size)
            ref[:, filled : filled + size] = routed_ref[rows, pl.ds(lead, size)].astype(BF16)
            filled += size
        ref[:, filled:] = part[step * CAP : (step + 1) * CAP, :].astype(BF16)


def stack(parts):
    return jnp.concatenate([part.astype(F32) for part in parts], axis=0).astype(BF16)


def project(total, att_ref, entries, piece_refs, moved):
    me, core = lax.axis_index("ctx"), lax.axis_index("dp")
    share = att_ref.shape[1] // lax.axis_size("ctx")
    for piece, size, flip, offset, row, column in entries:
        lead = column(core) if moved else (me ^ flip(core)) * share + offset(core)
        columns = pl.ds(pl.multiple_of(lead, size), size)
        rows = pl.ds(pl.multiple_of(row(me, core), size), size)
        total = total + jnp.dot(
            att_ref[:, columns].astype(BF16),
            piece_refs[piece][rows, :],
            preferred_element_type=F32,
        )
    return total


def arrive_kernel(owners, entries, *refs):
    row_refs, piece_refs, (att_ref, hidden_ref) = refs[:owners], refs[owners:-2], refs[-2:]
    row_refs = in_order(row_refs, list(range(1, owners)))
    wide = att_ref.shape[1]
    att_ref[...] = stack([ref[:, :wide] for ref in row_refs])
    hidden = jnp.concatenate([ref[:, wide:].astype(F32) for ref in row_refs], axis=0)
    hidden_ref[...] = project(hidden, att_ref, entries, piece_refs, True)


def more_kernel(entries, att_ref, part_ref, *refs):
    refs[-1][...] = project(part_ref[...], att_ref, entries, refs[:-1], True)


def expert_kernel(entries, count, gain_ref, gate_ref, up_ref, down_ref, att_ref, part_ref, *refs):
    piece_refs, out_refs = refs[:count], refs[count:]
    hidden = project(part_ref[...], att_ref, entries, piece_refs, True)
    mean = jnp.mean(hidden * hidden, axis=1, keepdims=True)
    normed = (hidden * lax.rsqrt(mean + 1e-06) * gain_ref[...]).astype(BF16)
    gate = jnp.dot(normed, gate_ref[...], preferred_element_type=F32)
    up = jnp.dot(normed, up_ref[...], preferred_element_type=F32)
    act = (gate / (1.0 + jnp.exp(-gate)) * up).astype(BF16)
    out = jnp.dot(act, down_ref[...], preferred_element_type=F32)
    for step, ref in enumerate(out_refs):
        ref[...] = out[step * CAP : (step + 1) * CAP, :].astype(BF16)


def project_kernel(entries, att_ref, res_ref, *refs):
    hidden = res_ref[...].astype(F32)
    refs[-1][...] = project(hidden, att_ref, entries, refs[:-1], False)


def combine_kernel(owners, hidden_ref, mix_ref, *refs):
    row_refs, out_ref = in_order(refs[:owners], list(range(owners - 1, 0, -1))), refs[owners]
    rows = stack([ref[...] for ref in row_refs])
    total = hidden_ref[...] + jnp.dot(
        mix_ref[...], jnp.concatenate([rows, rows], axis=0), preferred_element_type=F32
    )
    out_ref[...] = total.astype(BF16)


def call(kernel, outs, args, micros, scratch=(), limit=24, free_in=0, free_out=0):
    vmem, free = pl.BlockSpec(memory_space=pltpu.VMEM), pl.BlockSpec(memory_space=pl.ANY)
    nbytes = sum(math.prod(a.shape) * a.dtype.itemsize for a in list(args) + list(outs))
    return pl.pallas_call(
        kernel,
        out_shape=outs,
        in_specs=[vmem] * (len(args) - free_in) + [free] * free_in,
        out_specs=[vmem] * (len(outs) - free_out) + [free] * free_out,
        scratch_shapes=list(scratch),
        compiler_params=pltpu.CompilerParams(vmem_limit_bytes=limit << 20),
        cost_estimate=pl.CostEstimate(
            flops=int(micros * 1.15e9), bytes_accessed=nbytes, transcendentals=0
        ),
    )(*args)


def in_order(refs, order):
    return [refs[0]] + [refs[1 + order.index(s)] for s in range(1, len(refs))]


def exchange(blocks, sign, order):
    count = len(blocks)
    return [blocks[0]] + [
        lax.ppermute(blocks[s], "exp", [(i, (i + sign * s) % count) for i in range(count)])
        for s in order
    ]


def gather_weight(weight, first, second, attended):
    n_ctx, cores = lax.axis_size("ctx"), lax.axis_size("dp")
    share = weight.shape[0]
    if (n_ctx, cores) != (4, 2):
        whole = lax.all_gather(weight, "ctx", axis=0, tiled=True)
        entries = [
            (
                0,
                share,
                lambda core, f=f: f,
                lambda core: 0,
                lambda me, core, f=f: (me ^ f) * share,
                lambda core, f=f: (f - 1) * share,
            )
            for f in range(n_ctx)
        ]
        home = [(0, share, lambda core: 0, lambda core: 0, lambda me, core: 0, None)]
        blocks = [(share, lambda core, f=f: f, lambda core: 0) for f in range(1, n_ctx)]
        return [whole], entries, entries[1:], [weight], home, blocks
    both = ("ctx", "dp")
    devices = [(me, core) for me in range(n_ctx) for core in range(cores)]
    aside = [(me * 2 + core, (me ^ (1 + core)) * 2 + core) for me, core in devices]
    across = [(me * 2 + core, (me ^ (2 - core)) * 2 + core) for me, core in devices]
    near_first = lax.ppermute(first, both, aside)
    near_second = lax.ppermute(second, both, aside)
    near_first = after(near_first, attended)
    far = lax.ppermute(near_first, both, across)
    (near,) = call(
        join_kernel,
        [jax.ShapeDtypeStruct(weight.shape, BF16)],
        [near_first, near_second, attended],
        micros=1,
        free_in=3,
        free_out=1,
        limit=1,
        scratch=[pltpu.SemaphoreType.DMA((2,))],
    )
    swap = [(0, 1), (1, 0)]
    pieces = [weight, near, far, lax.ppermute(near, "dp", swap), lax.ppermute(far, "dp", swap)]
    half = share // 2
    top = lambda me, core: 0
    entries = [
        (0, share, lambda core: 0, lambda core: 0, top, None),
        (1, share, lambda core: 1 + core, lambda core: 0, top, None),
        (2, half, lambda core: 3, lambda core: core * half, top, None),
        (3, share, lambda core: 2 - core, lambda core: 0, top, None),
        (4, half, lambda core: 3, lambda core: (1 - core) * half, top, None),
    ]
    moved = [
        (1, half, None, None, lambda me, core: (1 - core) * half, lambda core: 0),
        (2, half, None, None, top, lambda core: (3 + core) * half),
        (3, half, None, None, top, lambda core: half),
        (3, half, None, None, lambda me, core: half, lambda core: 2 * half),
        (4, half, None, None, top, lambda core: (4 - core) * half),
    ]
    home = [
        (0, share, lambda core: 0, lambda core: 0, top, None),
        (1, half, lambda core: 1 + core, lambda core: core * half, top, None),
    ]
    blocks = [
        (half, lambda core: 1 + core, lambda core: (1 - core) * half),
        (share, lambda core: 2 - core, lambda core: 0),
        (share, lambda core: 3, lambda core: 0),
    ]
    return pieces, entries, moved, [weight, near_first], home, blocks


def per_device(
    queries,
    keys,
    values,
    segments,
    residual,
    out_weight,
    gain,
    expert_ids,
    route_weights,
    w_gate,
    w_up,
    w_down,
):
    tok_rows = queries.shape[1]
    width = residual.shape[2]
    att_width = queries.shape[2]
    n_ctx, owners = lax.axis_size("ctx"), lax.axis_size("exp")
    slots = owners * CAP
    longest = segments.shape[1] // 2
    back_count = min(n_ctx - 1, -(-(longest - 1) // tok_rows))
    shape = jax.ShapeDtypeStruct

    own_kv = jnp.concatenate([keys[0], values[0]], axis=1)
    kv_blocks = []
    for back in range(1, back_count + 1):
        pairs = [(i, (i + back) % n_ctx) for i in range(n_ctx)]
        kv_blocks.append(lax.ppermute(own_kv, "ctx", pairs))
    (mark,) = call(mark_kernel, [shape((8, 128), F32)], [own_kv], micros=5, free_in=1, limit=1)
    half = shape((out_weight.shape[0] // 2, width), BF16)
    accum, row_max, row_sum, stacked, first, second = call(
        functools.partial(own_kernel, n_ctx),
        [
            shape((KVH, GROUPS, tok_rows, HD), F32),
            shape((KVH, GROUPS, tok_rows, HD), F32),
            shape((KVH, GROUPS, tok_rows, HD), F32),
            shape((KVH, GROUPS * tok_rows, HD), BF16),
            half,
            half,
        ],
        [queries[0], own_kv, segments, mark, out_weight],
        micros=3,
        free_in=1,
        free_out=2,
        scratch=[pltpu.SemaphoreType.DMA((2,))],
    )
    place, mix, res_rows = call(
        route_kernel,
        [
            shape((slots, tok_rows), BF16),
            shape((tok_rows, 2 * slots), BF16),
            shape((slots, width), F32),
        ],
        [expert_ids[0].T, route_weights[0].T, residual[0]],
        micros=1,
    )
    attended, chosen = call(
        functools.partial(rest_kernel, n_ctx, back_count),
        [shape((tok_rows, att_width), BF16), shape((slots, att_width), F32)],
        [segments, accum, row_max, row_sum, stacked, place, *kv_blocks]
        + [gain[None, :], w_gate[0], w_up[0], w_down[0]],
        micros=5,
    )
    pieces, entries, moved, near, home, blocks = gather_weight(
        out_weight, first, second, attended
    )
    moved_width = sum(size for size, _, _ in blocks)
    routed = call(
        functools.partial(send_kernel, blocks, home, owners),
        [shape((CAP, moved_width + width), BF16)] * owners,
        [chosen, res_rows, *near],
        micros=1,
    )
    early, more, late = (pieces[1:2], pieces[2:4], pieces[4:]) if pieces[1:] else ([], [], pieces)

    def listed(part):
        lead = [piece is part[0] for piece in pieces].index(True) if part else 0
        return [(e[0] - lead, *e[1:]) for e in moved if lead <= e[0] < lead + len(part)]

    arrived, part = call(
        functools.partial(arrive_kernel, owners, listed(early)),
        [shape((slots, moved_width), BF16), shape((slots, width), F32)],
        [*exchange(routed, 1, range(1, owners)), *early],
        micros=10,
    )
    if more:
        (part,) = call(
            functools.partial(more_kernel, listed(more)),
            [shape((slots, width), F32)],
            [arrived, part, *more],
            micros=1,
        )
    done = call(
        functools.partial(expert_kernel, listed(late), len(late)),
        [shape((CAP, width), BF16)] * owners,
        [gain[None, :], w_gate[0], w_up[0], w_down[0], arrived, part, *late],
        micros=2,
    )
    back = exchange(done, -1, range(owners - 1, 0, -1))
    (hidden,) = call(
        functools.partial(project_kernel, entries),
        [shape((tok_rows, width), F32)],
        [attended, residual[0], *pieces],
        micros=2,
    )
    (out,) = call(
        functools.partial(combine_kernel, owners),
        [shape((tok_rows, width), BF16)],
        [hidden, mix, *back],
        micros=1,
    )
    return out[None]


def solution(mesh):
    return jax.shard_map(
        per_device,
        mesh=mesh,
        in_specs=(
            P(("dp", "exp"), "ctx", None),
            P(("dp", "exp"), "ctx", None),
            P(("dp", "exp"), "ctx", None),
            P(("dp", "exp"), None),
            P(("dp", "exp"), "ctx", None),
            P("ctx", None),
            P(),
            P(("dp", "exp"), "ctx", None),
            P(("dp", "exp"), "ctx", None),
            P("exp", None, None),
            P("exp", None, None),
            P("exp", None, None),
        ),
        out_specs=P(("dp", "exp"), "ctx", None),
        check_vma=False,
    )
```

```python
import functools
import math

import jax
import jax.numpy as jnp
from jax import lax
from jax.experimental import pallas as pl
from jax.experimental.pallas import tpu as pltpu
from jax.sharding import PartitionSpec as P

HQ = 16
KVH = 2
HD = 128
GROUPS = HQ // KVH
CAP = 24
NEG = -1e30
SCORE_SCALE = math.log2(math.e) / math.sqrt(HD)
F32 = jnp.float32
BF16 = jnp.bfloat16


def slab_segments(segs_ref, index, count, rows):
    found = segs_ref[:, 0:rows]
    for slab in range(1, count):
        found = jnp.where(index == slab, segs_ref[:, slab * rows : (slab + 1) * rows], found)
    return found


def score_bias(segs_ref, backs, count, rows):
    me = lax.axis_index("ctx")
    row = lax.broadcasted_iota(jnp.int32, (rows, rows), 0)
    col = lax.broadcasted_iota(jnp.int32, (rows, rows), 1)
    own_seg = slab_segments(segs_ref, me, count, rows)
    query_seg = jnp.sum(jnp.where(row == col, own_seg, 0), axis=1, keepdims=True)
    parts = []
    for back in backs:
        if back == 0:
            allowed = (col <= row) & (own_seg == query_seg)
        else:
            key_seg = slab_segments(segs_ref, jnp.maximum(me - back, 0), count, rows)
            allowed = (key_seg == query_seg) & (me >= back)
        parts.append(jnp.where(allowed, 0.0, NEG))
    return parts


def group_scores(stacked, keys, bias):
    scores = lax.dot_general(
        stacked, keys, (((1,), (1,)), ((), ())), preferred_element_type=F32
    )
    return scores.reshape(GROUPS, *bias.shape) * SCORE_SCALE + bias


def weigh(expo, values):
    rows = expo.shape[0] * expo.shape[1]
    mixed = jnp.dot(
        expo.astype(BF16).reshape(rows, expo.shape[2]), values, preferred_element_type=F32
    ).reshape(*expo.shape[:2], 2 * HD)
    return mixed[:, :, :HD], mixed[:, :, HD:]


def mark_kernel(*refs):
    refs[-1][...] = jnp.zeros_like(refs[-1])


def gate_kernel(*refs):
    del refs


def after(piece, *marks):
    spec = pl.BlockSpec(memory_space=pl.ANY)
    return pl.pallas_call(
        gate_kernel,
        out_shape=jax.ShapeDtypeStruct(piece.shape, piece.dtype),
        in_specs=[spec] * (1 + len(marks)),
        out_specs=spec,
        input_output_aliases={0: 0},
        compiler_params=pltpu.CompilerParams(vmem_limit_bytes=1 << 20),
    )(piece, *marks)


def join_kernel(first_ref, second_ref, mark_ref, whole_ref, sems):
    del mark_ref
    half = first_ref.shape[0]
    core = lax.rem(lax.axis_index("dp"), 2)
    copies = []
    for index, (lead, ref) in enumerate([(core, first_ref), (1 - core, second_ref)]):
        target = whole_ref.at[pl.ds(pl.multiple_of(lead * half, half), half)]
        copies.append(pltpu.make_async_copy(ref, target, sems.at[index]))
        copies[-1].start()
    for copy in copies:
        copy.wait()


def own_kernel(
    n_ctx,
    q_ref,
    kv_ref,
    segs_ref,
    mark_ref,
    w_ref,
    acc_ref,
    max_ref,
    sum_ref,
    queries_ref,
    first_ref,
    second_ref,
    sems,
):
    del mark_ref
    half = first_ref.shape[0]
    core = lax.rem(lax.axis_index("dp"), 2)
    copies = []
    for index, (lead, ref) in enumerate([(core, first_ref), (1 - core, second_ref)]):
        source = w_ref.at[pl.ds(pl.multiple_of(lead * half, half), half)]
        copies.append(pltpu.make_async_copy(source, ref, sems.at[index]))
        copies[-1].start()
    rows = q_ref.shape[0]
    (bias,) = score_bias(segs_ref, (0,), n_ctx, rows)
    ones = jnp.ones((rows, HD), BF16)
    for kv in range(KVH):
        keys = kv_ref[:, kv * HD : (kv + 1) * HD]
        values = jnp.concatenate([kv_ref[:, (KVH + kv) * HD : (KVH + kv + 1) * HD], ones], axis=1)
        heads = range(kv * GROUPS, (kv + 1) * GROUPS)
        stacked = jnp.concatenate([q_ref[:, h * HD : (h + 1) * HD] for h in heads], axis=0)
        queries_ref[kv] = stacked
        scores = group_scores(stacked, keys, bias)
        row_max = jnp.max(scores, axis=2, keepdims=True)
        accum, row_sum = weigh(jnp.exp2(scores - row_max), values)
        acc_ref[kv] = accum
        max_ref[kv] = jnp.broadcast_to(row_max, max_ref.shape[1:])
        sum_ref[kv] = row_sum
    for copy in copies:
        copy.wait()


def route_kernel(ids_ref, rw_ref, res_ref, place_ref, mix_ref, rows_ref):
    slots, rows = place_ref.shape
    slot = lax.broadcasted_iota(jnp.int32, (slots, rows), 0)
    owner = lax.rem(slot // CAP + lax.axis_index("exp"), slots // CAP)
    hit = jnp.zeros((slots, rows), jnp.bool_)
    weight = jnp.zeros((slots, rows), F32)
    for choice in range(ids_ref.shape[0]):
        same = ids_ref[choice : choice + 1, :] == owner
        hit = hit | same
        weight = jnp.where(same, rw_ref[choice : choice + 1, :], weight)
    row = lax.broadcasted_iota(jnp.int32, (rows, rows), 0)
    col = lax.broadcasted_iota(jnp.int32, (rows, rows), 1)
    before = (row < col).astype(F32).astype(BF16)
    rank = jnp.dot(hit.astype(F32).astype(BF16), before, preferred_element_type=F32)
    placed = hit & (rank == lax.rem(slot, CAP).astype(F32))
    place = placed.astype(F32).astype(BF16)
    place_ref[...] = place
    mix = jnp.where(placed, weight, 0.0)
    high = mix.astype(BF16).astype(F32)
    mix_ref[...] = jnp.concatenate([high, mix - high], axis=0).T.astype(BF16)
    rows_ref[...] = jnp.dot(place, res_ref[...], preferred_element_type=F32)


def rest_kernel(
    n_ctx,
    back_count,
    segs_ref,
    acc_ref,
    max_ref,
    sum_ref,
    queries_ref,
    place_ref,
    *refs,
):
    kv_refs, (out_ref, routed_ref) = refs[:back_count], refs[-2:]
    rows = queries_ref.shape[1] // GROUPS
    bias = jnp.concatenate(score_bias(segs_ref, range(1, back_count + 1), n_ctx, rows), axis=1)
    keys_count = rows * back_count
    spread = -(-keys_count // HD)
    ones = jnp.ones((keys_count, HD), BF16)
    scores = []
    for kv in range(KVH):
        keys = jnp.concatenate([ref[:, kv * HD : (kv + 1) * HD] for ref in kv_refs], axis=0)
        scores.append(group_scores(queries_ref[kv], keys, bias))
    for kv in range(KVH):
        values = jnp.concatenate(
            [ref[:, (KVH + kv) * HD : (KVH + kv + 1) * HD] for ref in kv_refs], axis=0
        )
        values = jnp.concatenate([values, ones], axis=1)
        old_max = max_ref[kv]
        new_max = jnp.maximum(old_max, jnp.max(scores[kv], axis=2, keepdims=True))
        shift = jnp.concatenate([new_max] * spread, axis=2)[:, :, :keys_count]
        accum, row_sum = weigh(jnp.exp2(scores[kv] - shift), values)
        fix = jnp.exp2(old_max - new_max)
        total = sum_ref[kv] * fix + row_sum
        attended = ((acc_ref[kv] * fix + accum) / total).astype(BF16)
        for group in range(GROUPS):
            head = kv * GROUPS + group
            out_ref[:, head * HD : (head + 1) * HD] = attended[group]
    routed_ref[...] = jnp.dot(place_ref[...], out_ref[...], preferred_element_type=F32)


def send_kernel(blocks, entries, owners, routed_ref, rows_ref, *refs):
    piece_refs, send_refs = refs[:-owners], refs[-owners:]
    me, core = lax.axis_index("ctx"), lax.axis_index("dp")
    share = routed_ref.shape[1] // lax.axis_size("ctx")
    part = project(rows_ref[...], routed_ref, entries, piece_refs, False)
    for step, ref in enumerate(send_refs):
        rows = pl.ds(step * CAP, CAP)
        filled = 0
        for size, flip, offset in blocks:
            lead = pl.multiple_of((me ^ flip(core)) * share + offset(core), size)
            ref[:, filled : filled + size] = routed_ref[rows, pl.ds(lead, size)].astype(BF16)
            filled += size
        ref[:, filled:] = part[step * CAP : (step + 1) * CAP, :].astype(BF16)


def stack(parts):
    return jnp.concatenate([part.astype(F32) for part in parts], axis=0).astype(BF16)


def project(total, att_ref, entries, piece_refs, moved):
    me, core = lax.axis_index("ctx"), lax.axis_index("dp")
    share = att_ref.shape[1] // lax.axis_size("ctx")
    for piece, size, flip, offset, row, column in entries:
        lead = column(core) if moved else (me ^ flip(core)) * share + offset(core)
        columns = pl.ds(pl.multiple_of(lead, size), size)
        rows = pl.ds(pl.multiple_of(row(me, core), size), size)
        total = total + jnp.dot(
            att_ref[:, columns].astype(BF16),
            piece_refs[piece][rows, :],
            preferred_element_type=F32,
        )
    return total


def arrive_kernel(owners, entries, *refs):
    row_refs, piece_refs, (att_ref, hidden_ref) = refs[:owners], refs[owners:-2], refs[-2:]
    row_refs = in_order(row_refs, list(range(1, owners)))
    wide = att_ref.shape[1]
    att_ref[...] = stack([ref[:, :wide] for ref in row_refs])
    hidden = jnp.concatenate([ref[:, wide:].astype(F32) for ref in row_refs], axis=0)
    hidden_ref[...] = project(hidden, att_ref, entries, piece_refs, True)


def more_kernel(entries, att_ref, part_ref, *refs):
    refs[-1][...] = project(part_ref[...], att_ref, entries, refs[:-1], True)


def expert_kernel(entries, count, gain_ref, gate_ref, up_ref, down_ref, att_ref, part_ref, *refs):
    piece_refs, out_refs = refs[:count], refs[count:]
    hidden = project(part_ref[...], att_ref, entries, piece_refs, True)
    mean = jnp.mean(hidden * hidden, axis=1, keepdims=True)
    normed = (hidden * lax.rsqrt(mean + 1e-06) * gain_ref[...]).astype(BF16)
    gate = jnp.dot(normed, gate_ref[...], preferred_element_type=F32)
    up = jnp.dot(normed, up_ref[...], preferred_element_type=F32)
    act = (gate / (1.0 + jnp.exp(-gate)) * up).astype(BF16)
    out = jnp.dot(act, down_ref[...], preferred_element_type=F32)
    for step, ref in enumerate(out_refs):
        ref[...] = out[step * CAP : (step + 1) * CAP, :].astype(BF16)


def project_kernel(entries, att_ref, res_ref, *refs):
    hidden = res_ref[...].astype(F32)
    refs[-1][...] = project(hidden, att_ref, entries, refs[:-1], False)


def combine_kernel(owners, hidden_ref, mix_ref, *refs):
    row_refs, out_ref = in_order(refs[:owners], list(range(owners - 1, 0, -1))), refs[owners]
    rows = stack([ref[...] for ref in row_refs])
    total = hidden_ref[...] + jnp.dot(
        mix_ref[...], jnp.concatenate([rows, rows], axis=0), preferred_element_type=F32
    )
    out_ref[...] = total.astype(BF16)


def call(kernel, outs, args, micros, scratch=(), limit=24, free_in=0, free_out=0):
    vmem, free = pl.BlockSpec(memory_space=pltpu.VMEM), pl.BlockSpec(memory_space=pl.ANY)
    nbytes = sum(math.prod(a.shape) * a.dtype.itemsize for a in list(args) + list(outs))
    return pl.pallas_call(
        kernel,
        out_shape=outs,
        in_specs=[vmem] * (len(args) - free_in) + [free] * free_in,
        out_specs=[vmem] * (len(outs) - free_out) + [free] * free_out,
        scratch_shapes=list(scratch),
        compiler_params=pltpu.CompilerParams(vmem_limit_bytes=limit << 20),
        cost_estimate=pl.CostEstimate(
            flops=int(micros * 1.15e9), bytes_accessed=nbytes, transcendentals=0
        ),
    )(*args)


def in_order(refs, order):
    return [refs[0]] + [refs[1 + order.index(s)] for s in range(1, len(refs))]


def exchange(blocks, sign, order):
    count = len(blocks)
    return [blocks[0]] + [
        lax.ppermute(blocks[s], "exp", [(i, (i + sign * s) % count) for i in range(count)])
        for s in order
    ]


def gather_weight(weight, first, second, attended, pack):
    n_ctx, cores = lax.axis_size("ctx"), lax.axis_size("dp")
    share = weight.shape[0]
    if (n_ctx, cores) != (4, 2):
        whole = lax.all_gather(weight, "ctx", axis=0, tiled=True)
        entries = [
            (
                0,
                share,
                lambda core, f=f: f,
                lambda core: 0,
                lambda me, core, f=f: (me ^ f) * share,
                lambda core, f=f: (f - 1) * share,
            )
            for f in range(n_ctx)
        ]
        home = [(0, share, lambda core: 0, lambda core: 0, lambda me, core: 0, None)]
        blocks = [(share, lambda core, f=f: f, lambda core: 0) for f in range(1, n_ctx)]
        return [whole], entries, entries[1:], pack([weight], home, blocks)
    both = ("ctx", "dp")
    devices = [(me, core) for me in range(n_ctx) for core in range(cores)]
    aside = [(me * 2 + core, (me ^ (1 + core)) * 2 + core) for me, core in devices]
    across = [(me * 2 + core, (me ^ (2 - core)) * 2 + core) for me, core in devices]
    near_first = lax.ppermute(first, both, aside)
    near_second = lax.ppermute(second, both, aside)
    near_first = after(near_first, attended)
    half = share // 2
    top = lambda me, core: 0
    home = [
        (0, share, lambda core: 0, lambda core: 0, top, None),
        (1, half, lambda core: 1 + core, lambda core: core * half, top, None),
    ]
    blocks = [
        (half, lambda core: 1 + core, lambda core: (1 - core) * half),
        (share, lambda core: 2 - core, lambda core: 0),
        (share, lambda core: 3, lambda core: 0),
    ]
    packed = pack([weight, near_first], home, blocks)
    near_first = after(near_first, packed[0])
    far = lax.ppermute(near_first, both, across)
    (near,) = call(
        join_kernel,
        [jax.ShapeDtypeStruct(weight.shape, BF16)],
        [near_first, near_second, attended],
        micros=1,
        free_in=3,
        free_out=1,
        limit=1,
        scratch=[pltpu.SemaphoreType.DMA((2,))],
    )
    swap = [(0, 1), (1, 0)]
    pieces = [weight, near, far, lax.ppermute(near, "dp", swap), lax.ppermute(far, "dp", swap)]
    entries = [
        (0, share, lambda core: 0, lambda core: 0, top, None),
        (1, share, lambda core: 1 + core, lambda core: 0, top, None),
        (2, half, lambda core: 3, lambda core: core * half, top, None),
        (3, share, lambda core: 2 - core, lambda core: 0, top, None),
        (4, half, lambda core: 3, lambda core: (1 - core) * half, top, None),
    ]
    moved = [
        (1, half, None, None, lambda me, core: (1 - core) * half, lambda core: 0),
        (2, half, None, None, top, lambda core: (3 + core) * half),
        (3, half, None, None, top, lambda core: half),
        (3, half, None, None, lambda me, core: half, lambda core: 2 * half),
        (4, half, None, None, top, lambda core: (4 - core) * half),
    ]
    return pieces, entries, moved, packed


def per_device(
    queries,
    keys,
    values,
    segments,
    residual,
    out_weight,
    gain,
    expert_ids,
    route_weights,
    w_gate,
    w_up,
    w_down,
):
    tok_rows = queries.shape[1]
    width = residual.shape[2]
    att_width = queries.shape[2]
    n_ctx, owners = lax.axis_size("ctx"), lax.axis_size("exp")
    slots = owners * CAP
    longest = segments.shape[1] // 2
    back_count = min(n_ctx - 1, -(-(longest - 1) // tok_rows))
    shape = jax.ShapeDtypeStruct

    own_kv = jnp.concatenate([keys[0], values[0]], axis=1)
    kv_blocks = []
    for back in range(1, back_count + 1):
        pairs = [(i, (i + back) % n_ctx) for i in range(n_ctx)]
        kv_blocks.append(lax.ppermute(own_kv, "ctx", pairs))
    (mark,) = call(mark_kernel, [shape((8, 128), F32)], [own_kv], micros=5, free_in=1, limit=1)
    half = shape((out_weight.shape[0] // 2, width), BF16)
    accum, row_max, row_sum, stacked, first, second = call(
        functools.partial(own_kernel, n_ctx),
        [
            shape((KVH, GROUPS, tok_rows, HD), F32),
            shape((KVH, GROUPS, tok_rows, HD), F32),
            shape((KVH, GROUPS, tok_rows, HD), F32),
            shape((KVH, GROUPS * tok_rows, HD), BF16),
            half,
            half,
        ],
        [queries[0], own_kv, segments, mark, out_weight],
        micros=3,
        free_in=1,
        free_out=2,
        scratch=[pltpu.SemaphoreType.DMA((2,))],
    )
    place, mix, res_rows = call(
        route_kernel,
        [
            shape((slots, tok_rows), BF16),
            shape((tok_rows, 2 * slots), BF16),
            shape((slots, width), F32),
        ],
        [expert_ids[0].T, route_weights[0].T, residual[0]],
        micros=1,
    )
    attended, chosen = call(
        functools.partial(rest_kernel, n_ctx, back_count),
        [shape((tok_rows, att_width), BF16), shape((slots, att_width), F32)],
        [segments, accum, row_max, row_sum, stacked, place, *kv_blocks]
        + [gain[None, :], w_gate[0], w_up[0], w_down[0]],
        micros=5,
    )
    def pack(near, home, blocks):
        moved_width = sum(size for size, _, _ in blocks)
        return call(
            functools.partial(send_kernel, blocks, home, owners),
            [shape((CAP, moved_width + width), BF16)] * owners,
            [chosen, res_rows, *near],
            micros=1,
        )

    pieces, entries, moved, routed = gather_weight(out_weight, first, second, attended, pack)
    early, more, late = (pieces[1:2], pieces[2:4], pieces[4:]) if pieces[1:] else ([], [], pieces)

    def listed(part):
        lead = [piece is part[0] for piece in pieces].index(True) if part else 0
        return [(e[0] - lead, *e[1:]) for e in moved if lead <= e[0] < lead + len(part)]

    arrived, part = call(
        functools.partial(arrive_kernel, owners, listed(early)),
        [shape((slots, routed[0].shape[1] - width), BF16), shape((slots, width), F32)],
        [*exchange(routed, 1, range(1, owners)), *early],
        micros=10,
    )
    if more:
        (part,) = call(
            functools.partial(more_kernel, listed(more)),
            [shape((slots, width), F32)],
            [arrived, part, *more],
            micros=1,
        )
    done = call(
        functools.partial(expert_kernel, listed(late), len(late)),
        [shape((CAP, width), BF16)] * owners,
        [gain[None, :], w_gate[0], w_up[0], w_down[0], arrived, part, *late],
        micros=2,
    )
    back = exchange(done, -1, range(owners - 1, 0, -1))
    (hidden,) = call(
        functools.partial(project_kernel, entries),
        [shape((tok_rows, width), F32)],
        [attended, residual[0], *pieces],
        micros=2,
    )
    (out,) = call(
        functools.partial(combine_kernel, owners),
        [shape((tok_rows, width), BF16)],
        [hidden, mix, *back],
        micros=1,
    )
    return out[None]


def solution(mesh):
    return jax.shard_map(
        per_device,
        mesh=mesh,
        in_specs=(
            P(("dp", "exp"), "ctx", None),
            P(("dp", "exp"), "ctx", None),
            P(("dp", "exp"), "ctx", None),
            P(("dp", "exp"), None),
            P(("dp", "exp"), "ctx", None),
            P("ctx", None),
            P(),
            P(("dp", "exp"), "ctx", None),
            P(("dp", "exp"), "ctx", None),
            P("exp", None, None),
            P("exp", None, None),
            P("exp", None, None),
        ),
        out_specs=P(("dp", "exp"), "ctx", None),
        check_vma=False,
    )
```
